32 devices in a mesh: tile: 16 (over z, y, x), mode: 2 (over core).
Axes of the slice: x: 2, y: 2, z: 4, core: 2. Of those that a mesh axis runs over, the one named last changes fastest.
Arguments:
- object_field: float32 [2, 4096, 512], P(None, 'tile'), may hold values from -4.2 to 4.2
- probe: float32 [2, 2, 256, 256], P('mode'), may hold values from -2.1 to 2.1
- positions: int32 [2, 32, 2], P(None, 'tile'), may hold values from 0 to 3840, as said below
- measured: float32 [2, 32, 256, 256], P(None, 'tile'), may hold values from 0.1 to 30
Outputs:
- refined_object: float32 [2, 4096, 512], P(None, 'tile')
- refined_probe: float32 [2, 2, 256, 256], P('mode')
The draws below stay inside these ranges and needn't reach their ends.
Inputs may be any that keep to these rules, and one draw needn't show every extreme that they name: positions[b, j] = (row, column). Position j belongs to tile t = j // 2; its row lies from t * 256 - 256 / 2 to t * 256 - 256 / 2 + 256, both ends reached in some tile, and every pattern lies inside the object of 4096 x 512.
All inputs are finite; a program needn't handle non-finite values.
Results may differ from the reference program's by a relative error of at most 0.0001.
Values sent between devices are 32-bit elements; how exact they have to be, the bound alone decides.
No kernel may reach another device: no remote copies, remote signals or barrier semaphores. Data moves between devices by JAX's collectives and lax.ppermute only.
A program may use at most 64 MiB of HBM per device.

```python
import math
import jax
import jax.numpy as jnp
from jax import lax

PAT = 256
MODES = 2
P_DEV = 2
POS = 32
STRIP = 256
OBJ_W = 512
OBJ_H = 4096
BATCHES = 2


def draw_positions(key, part):
    row_key, col_key = jax.random.split(jax.random.fold_in(key, 11))
    shift_rows = jax.random.randint(row_key, (BATCHES, POS), 0, STRIP + 1)
    tile_of = jnp.arange(POS, dtype=jnp.int32) // P_DEV
    row_values = tile_of[None, :] * STRIP - PAT // 2 + shift_rows
    row_values = jnp.clip(row_values, 0, OBJ_H - PAT)
    col_values = jax.random.randint(col_key, (BATCHES, POS), 0, OBJ_W - PAT + 1)
    row_values = row_values.at[0, 0].set(0)
    col_values = col_values.at[0, 0].set(0)
    row_values = row_values.at[0, POS - 1].set(OBJ_H - PAT)
    col_values = col_values.at[0, POS - 1].set(OBJ_W - PAT)
    row_values = row_values.at[0, P_DEV].set(STRIP - PAT // 2)
    row_values = row_values.at[1, P_DEV].set(2 * STRIP - PAT // 2)
    return jnp.stack([row_values, col_values], axis=2).astype(jnp.int32)


def steps_of(stream_key, extent, pieces, least, top_value):
    def one(dim, blocks):
        heights = jax.random.uniform(jax.random.fold_in(jax.random.fold_in(stream_key, 6), dim), (blocks,), jnp.float32, least / len(pieces), top_value / len(pieces))
        return jnp.repeat(jnp.exp(heights), extent[dim] // blocks).reshape((-1,) + (1,) * (len(extent) - dim - 1))

    loudness = one(*pieces[0])
    for cut in pieces[1:]:
        loudness = loudness * one(*cut)
    return loudness


def noise(key, dims, deviation, bound, cuts=(), held_as=jnp.bfloat16):
    factor_of = steps_of(key, dims, cuts, -0.22, 0.18) if cuts else 1.0
    entries = jax.random.normal(key, dims, jnp.float32) * deviation * factor_of
    return jnp.minimum(jnp.maximum(entries, -bound), bound).astype(held_as)


def setup_inputs(seed: int = 0) -> dict:
    key_of = jax.random.split(jax.random.key(seed), 5)
    return {
        "object_field": noise(key_of[0], (2, OBJ_H, OBJ_W), 0.7, 4.2, ((1, 16),), jnp.float32),
        "probe": noise(key_of[1], (MODES, 2, PAT, PAT), 0.35, 2.1, ((0, 2),), jnp.float32),
        "positions": draw_positions(jax.random.fold_in(key_of[4], 71), 0),
        "measured": jnp.clip(jnp.exp(math.log(30.0) - 5.7037825 * jax.random.uniform(key_of[3], (BATCHES, POS, PAT, PAT), jnp.float32) ** steps_of(key_of[3], (BATCHES, POS, PAT, PAT), ((1, 16),), -0.2, 0.2)), 0.1, 30.0),
    }


def tables(length):
    index_values = jnp.arange(length, dtype=jnp.int32)
    product = index_values[:, None] * index_values[None, :] % length
    angles = product.astype(jnp.float32) * (2.0 * math.pi / length)
    scaling = 1.0 / math.sqrt(length)
    return (jnp.cos(angles) * scaling, jnp.sin(angles) * scaling)

def apply_left(matrix, target):
    return jnp.einsum('ab,pbc->pac', matrix, target, precision=lax.Precision.HIGHEST)

def apply_right(target, matrix):
    return jnp.einsum('pab,bc->pac', target, matrix, precision=lax.Precision.HIGHEST)

def transform(real_part, imag_part, cosine, sine_table, direction):
    left_real = apply_left(cosine, real_part) + direction * apply_left(sine_table, imag_part)
    left_imag = apply_left(cosine, imag_part) - direction * apply_left(sine_table, real_part)
    out_real = apply_right(left_real, cosine) + direction * apply_right(left_imag, sine_table)
    out_imag = apply_right(left_imag, cosine) - direction * apply_right(left_real, sine_table)
    return (out_real, out_imag)

def place_add(target, placed, row_start, col_start):
    zero_index = jnp.int32(0)
    current = lax.dynamic_slice(target, (zero_index, row_start, col_start), placed.shape)
    return lax.dynamic_update_slice(target, current + placed, (zero_index, row_start, col_start))

def reference(object_field, probe, positions, measured):
    cosine, sine_table = tables(PAT)
    tiles = POS // P_DEV
    for minibatch in range(BATCHES):
        current_object = object_field
        current_probe = probe

        def tile_block(carry, block):
            accumulated, probe_total, coverage_total = carry
            offsets, observed = block

            def cut_one(row_start, col_start):
                return lax.dynamic_slice(current_object, (jnp.int32(0), row_start, col_start), (2, PAT, PAT))
            patches = jax.vmap(cut_one)(offsets[:, 0], offsets[:, 1])
            obj_real = patches[:, 0]
            obj_imag = patches[:, 1]
            far_fields = []
            total_power = jnp.zeros(obj_real.shape, jnp.float32)
            for mode_index in range(MODES):
                probe_real = current_probe[mode_index, 0]
                probe_imag = current_probe[mode_index, 1]
                exit_real = probe_real * obj_real - probe_imag * obj_imag
                exit_imag = probe_real * obj_imag + probe_imag * obj_real
                far_real, far_imag = transform(exit_real, exit_imag, cosine, sine_table, 1.0)
                far_fields.append((far_real, far_imag))
                total_power = total_power + far_real * far_real + far_imag * far_imag
            modulus = jnp.sqrt((observed + 1.0) / (total_power + 1.0)) - 1.0
            grad_real = jnp.zeros(obj_real.shape, jnp.float32)
            grad_imag = jnp.zeros(obj_real.shape, jnp.float32)
            probe_power = jnp.zeros((PAT, PAT), jnp.float32)
            probe_steps = []
            for mode_index in range(MODES):
                probe_real = current_probe[mode_index, 0]
                probe_imag = current_probe[mode_index, 1]
                far_real, far_imag = far_fields[mode_index]
                chi_real, chi_imag = transform(modulus * far_real, modulus * far_imag, cosine, sine_table, -1.0)
                grad_real = grad_real + probe_real * chi_real + probe_imag * chi_imag
                grad_imag = grad_imag + probe_real * chi_imag - probe_imag * chi_real
                probe_power = probe_power + probe_real * probe_real + probe_imag * probe_imag
                step_real = lax.optimization_barrier(jnp.sum(obj_real * chi_real + obj_imag * chi_imag, axis=0))
                step_imag = lax.optimization_barrier(jnp.sum(obj_real * chi_imag - obj_imag * chi_real, axis=0))
                probe_steps.append(jnp.stack([step_real, step_imag]))
            coverage = lax.optimization_barrier(jnp.sum(obj_real * obj_real + obj_imag * obj_imag, axis=0))
            for position in range(P_DEV):
                placed = jnp.stack([grad_real[position], grad_imag[position], probe_power])
                accumulated = place_add(accumulated, placed, offsets[position, 0], offsets[position, 1])
            return ((accumulated, probe_total + jnp.stack(probe_steps), coverage_total + coverage), None)
        start = (jnp.zeros((3, OBJ_H, OBJ_W), jnp.float32), jnp.zeros((MODES, 2, PAT, PAT), jnp.float32), jnp.zeros((PAT, PAT), jnp.float32))
        blocks = (positions[minibatch].reshape(tiles, P_DEV, 2), measured[minibatch].reshape(tiles, P_DEV, PAT, PAT))
        (accumulated, probe_total, coverage_total), unused = lax.scan(tile_block, start, blocks)
        divisor = accumulated[2] + 1.0
        object_field = jnp.stack([current_object[0] + accumulated[0] / divisor, current_object[1] + accumulated[1] / divisor])
        probe = current_probe + probe_total / (coverage_total + 1.0)
    return (object_field, probe)
```

```python
import functools
import math

import jax
import jax.numpy as jnp
import numpy as np
from jax import lax
from jax.experimental import pallas as pl
from jax.experimental.pallas import tpu as pltpu
from jax.sharding import PartitionSpec as P

F32 = jnp.float32
BF16 = jnp.bfloat16
VMEM_BYTES = 40 * 1024 * 1024
GROUP = 4


def padded(block, sides, width):
    for axis, dim in sides:
        count = lax.axis_size(axis)
        forward = [(i, i + 1) for i in range(count - 1)]
        backward = [(target, source) for source, target in forward]
        low = lax.ppermute(
            lax.slice_in_dim(block, block.shape[dim] - width, None, axis=dim), axis, forward
        )
        high = lax.ppermute(lax.slice_in_dim(block, 0, width, axis=dim), axis, backward)
        block = jnp.concatenate([low, block, high], axis=dim)
    return block


def tables(length):
    index_values = jnp.arange(length, dtype=jnp.int32)
    product = index_values[:, None] * index_values[None, :] % length
    angles = product.astype(jnp.float32) * (2.0 * math.pi / length)
    scaling = 1.0 / math.sqrt(length)
    return (jnp.cos(angles) * scaling, jnp.sin(angles) * scaling)


def apply_left(matrix, target):
    return jnp.einsum("ab,pbc->pac", matrix, target, precision=lax.Precision.HIGHEST)


def apply_right(target, matrix):
    return jnp.einsum("pab,bc->pac", target, matrix, precision=lax.Precision.HIGHEST)


def transform(real_part, imag_part, cosine, sine_table, direction):
    left_real = apply_left(cosine, real_part) + direction * apply_left(sine_table, imag_part)
    left_imag = apply_left(cosine, imag_part) - direction * apply_left(sine_table, real_part)
    out_real = apply_right(left_real, cosine) + direction * apply_right(left_imag, sine_table)
    out_imag = apply_right(left_imag, cosine) - direction * apply_right(left_real, sine_table)
    return (out_real, out_imag)


def place_add(target, placed, row_start, col_start):
    zero_index = jnp.int32(0)
    current = lax.dynamic_slice(target, (zero_index, row_start, col_start), placed.shape)
    return lax.dynamic_update_slice(target, current + placed, (zero_index, row_start, col_start))


def shards_by_mode(object_field, probe, positions, measured):
    strip_rows = object_field.shape[1]
    object_width = object_field.shape[2]
    pattern = probe.shape[2]
    half_pattern = pattern // 2
    count = positions.shape[1]
    cosine, sine_table = tables(pattern)
    tile_index = lax.axis_index("tile")
    offset = tile_index * strip_rows - half_pattern
    for minibatch in range(measured.shape[0]):
        extended = padded(object_field, (("tile", 1),), half_pattern)
        row_offsets = positions[minibatch, :, 0] - offset
        column_offsets = positions[minibatch, :, 1]

        def cut_one(row_start, col_start):
            return lax.dynamic_slice(
                extended, (jnp.int32(0), row_start, col_start), (2, pattern, pattern)
            )

        patches = jax.vmap(cut_one)(row_offsets, column_offsets)
        obj_real = patches[:, 0]
        obj_imag = patches[:, 1]
        probe_real = probe[0, 0]
        probe_imag = probe[0, 1]
        exit_real = probe_real * obj_real - probe_imag * obj_imag
        exit_imag = probe_real * obj_imag + probe_imag * obj_real
        far_real, far_imag = transform(exit_real, exit_imag, cosine, sine_table, 1.0)
        observed = measured[minibatch]
        intensity = lax.psum(far_real * far_real + far_imag * far_imag, "mode")
        modulus = jnp.sqrt((observed + 1.0) / (intensity + 1.0)) - 1.0
        chi_real, chi_imag = transform(
            modulus * far_real, modulus * far_imag, cosine, sine_table, -1.0
        )
        grad_real = probe_real * chi_real + probe_imag * chi_imag
        grad_imag = probe_real * chi_imag - probe_imag * chi_real
        probe_power = probe_real * probe_real + probe_imag * probe_imag
        step_real = jnp.sum(obj_real * chi_real + obj_imag * chi_imag, axis=0)
        step_imag = jnp.sum(obj_real * chi_imag - obj_imag * chi_real, axis=0)
        coverage = jnp.sum(obj_real * obj_real + obj_imag * obj_imag, axis=0)
        accumulated = jnp.zeros((3, strip_rows + pattern, object_width), jnp.float32)
        for position in range(count):
            placed = jnp.stack([grad_real[position], grad_imag[position], probe_power])
            accumulated = place_add(
                accumulated, placed, row_offsets[position], column_offsets[position]
            )
        rim_rows = jnp.concatenate(
            [accumulated[:, :half_pattern], accumulated[:, strip_rows + half_pattern :]], axis=1
        )
        received = padded(rim_rows, (("tile", 1),), half_pattern)
        own_strip = accumulated[:, half_pattern : half_pattern + strip_rows]
        own_strip = own_strip.at[:, :half_pattern].add(received[:, :half_pattern])
        own_strip = own_strip.at[:, strip_rows - half_pattern :].add(
            received[:, pattern + half_pattern :]
        )
        summed = lax.psum(own_strip, "mode")
        divisor = summed[2] + 1.0
        object_field = jnp.stack(
            [object_field[0] + summed[0] / divisor, object_field[1] + summed[1] / divisor]
        )
        step_stack = jnp.stack([jnp.stack([step_real, step_imag])])
        step_total, coverage_total = lax.psum((step_stack, coverage), "tile")
        probe = probe + step_total / (coverage_total + 1.0)
    return (object_field, probe)


def split_table(length):
    index_values = np.arange(length)
    angles = (index_values[:, None] * index_values[None, :] % length) * (2.0 * np.pi / length)
    scaling = 1.0 / np.sqrt(length)
    parts = []
    for table in (np.cos(angles) * scaling, np.sin(angles) * scaling):
        high = table.astype(jnp.bfloat16)
        parts += [high, (table - high.astype(np.float64)).astype(jnp.bfloat16)]
    return np.stack(parts)


def spot(info, size, minibatch, side, slot):
    tiles, strip, pattern = size
    place = (((side + 1) * 2 + minibatch) * 2 + slot) * 2
    tile = info[24]
    row = info[place] - tile * strip + pattern // 2
    if side < 0:
        row = jnp.where(tile == 0, -pattern, row)
    if side > 0:
        row = jnp.where(tile == tiles - 1, strip + pattern, row)
    return row, info[place + 1]


def take_columns(block, column, width):
    total = block.shape[-1]
    return pltpu.roll(block, lax.rem(total - column, total), 1)[:, :width]


def add_at(tall, block, row, column):
    rows, width = block.shape
    total = tall.shape[1]
    shift = lax.rem(row, 8)
    start = pl.multiple_of(row - shift, 8)
    turned = pltpu.roll(block.reshape(rows // 8, 8, width), shift, 1)
    empty = jnp.zeros((1, 8, width), block.dtype)
    inside = lax.broadcasted_iota(jnp.int32, (rows // 8 + 1, 8, width), 1) >= shift
    moved = jnp.where(
        inside,
        jnp.concatenate([turned, empty], axis=0),
        jnp.concatenate([empty, turned], axis=0),
    ).reshape(rows + 8, width)
    wide = jnp.concatenate([moved, jnp.zeros((rows + 8, total - width), block.dtype)], axis=1)
    tall[pl.ds(start, rows + 8), :] += pltpu.roll(wide, column, 1)


def rows_at(ref, row, rows):
    width = ref.shape[1]
    shift = lax.rem(row, 8)
    start = pl.multiple_of(row - shift, 8)
    block = ref[pl.ds(start, rows + 8), :].reshape(rows // 8 + 1, 8, width)
    turned = pltpu.roll(block, lax.rem(8 - shift, 8), 1)
    inside = lax.broadcasted_iota(jnp.int32, (rows // 8, 8, width), 1) < 8 - shift
    return jnp.where(inside, turned[:-1], turned[1:]).reshape(rows, width)


def halves(value):
    high = value.astype(BF16)
    return high, (value - high.astype(F32)).astype(BF16)


def product(left, right):
    dot = functools.partial(jnp.dot, preferred_element_type=F32)
    return dot(left[0], right[0]) + (dot(left[0], right[1]) + dot(left[1], right[0]))


def edges_kernel(size, info, strip_ref, low1, high1, low2, high2):
    half = low1.shape[1]
    width = low1.shape[2]
    slot = info[25]
    rows = strip_ref.shape[1]
    for minibatch, low, high in ((0, low1, high1), (1, low2, high2)):
        column_below = spot(info, size, minibatch, -1, slot)[1]
        column_above = spot(info, size, minibatch, 1, slot)[1]
        for part in range(2):
            low[part] = take_columns(strip_ref[part, :half], column_below, width)
            high[part] = take_columns(strip_ref[part, rows - half :], column_above, width)


def cut_patch(size, info, minibatch, strip_ref, below, above, window, part):
    half = below.shape[1]
    width = below.shape[2]
    rows = strip_ref.shape[1]
    row, column = spot(info, size, minibatch, 0, info[25])
    window[:half] = below[part]
    window[half : half + rows] = take_columns(strip_ref[part], column, width)
    window[half + rows : rows + width] = above[part]
    return rows_at(window, row, width)


def patch_kernel(size, info, strip_ref, below, above, patch, coverage, window):
    real = cut_patch(size, info, 0, strip_ref, below, above, window, 0)
    patch[0] = real
    power = real * real
    imag = cut_patch(size, info, 0, strip_ref, below, above, window, 1)
    patch[1] = imag
    coverage[...] = power + imag * imag


def illumination_kernel(size, minibatch, info, own, other, out, tall):
    tiles, strip, pattern = size
    tall[pattern : 2 * pattern + strip] = jnp.zeros((pattern + strip, tall.shape[1]), F32)
    power = own[0] * own[0] + own[1] * own[1] + (other[0] * other[0] + other[1] * other[1])
    for side in (-1, 0, 1):
        for slot in range(2):
            row, column = spot(info, size, minibatch, side, slot)
            add_at(tall, power, row + pattern, column)
    out[...] = tall[pattern : 2 * pattern + strip]


def field_kernel(size, minibatch, info, patch, own, other, measured, table, *outs):
    gradient, step_own, step_other = outs
    pattern = patch.shape[1]
    quarter = pattern // GROUP
    slot = info[25]
    cos_high, cos_low, sin_high, sin_low = (table[i] for i in range(4))

    def block(top_left, top_right, low_left, low_right):
        return jnp.concatenate(
            [
                jnp.concatenate([top_left, top_right], axis=1),
                jnp.concatenate([low_left, low_right], axis=1),
            ],
            axis=0,
        )

    first = (
        block(cos_high, sin_high, -sin_high, cos_high),
        block(cos_low, sin_low, -sin_low, cos_low),
    )
    second = (
        block(cos_high, -sin_high, sin_high, cos_high),
        block(cos_low, -sin_low, sin_low, cos_low),
    )
    obj_real, obj_imag = patch[0], patch[1]
    probes = ((own[0], own[1]), (other[0], other[1]))

    def both(fields, left, right):
        (r0, i0), (r1, i1) = fields
        y = product(left, halves(block(r0, r1, i0, i1)))
        y = block(
            y[:pattern, :pattern], y[pattern:, :pattern], y[:pattern, pattern:], y[pattern:, pattern:]
        )
        y = product(halves(y), right)
        return (
            (y[:pattern, :pattern], y[:pattern, pattern:]),
            (y[pattern:, :pattern], y[pattern:, pattern:]),
        )

    exits = [(pr * obj_real - pi * obj_imag, pr * obj_imag + pi * obj_real) for pr, pi in probes]
    far = both(exits, first, second)
    intensity = (far[0][0] * far[0][0] + far[0][1] * far[0][1]) + (
        far[1][0] * far[1][0] + far[1][1] * far[1][1]
    )
    factor = jnp.sqrt((measured[minibatch, slot] + 1.0) / (intensity + 1.0)) - 1.0
    chi = both([(factor * fr, factor * fi) for fr, fi in far], second, first)
    (pr0, pi0), (pr1, pi1) = probes
    (cr0, ci0), (cr1, ci1) = chi
    gradient[0] = (pr0 * cr0 + pi0 * ci0) + (pr1 * cr1 + pi1 * ci1)
    gradient[1] = (pr0 * ci0 - pi0 * cr0) + (pr1 * ci1 - pi1 * cr1)
    mate = lax.rem(info[24], GROUP)
    for step, (cr, ci) in ((step_own, chi[0]), (step_other, chi[1])):
        real = obj_real * cr + obj_imag * ci
        imag = obj_real * ci - obj_imag * cr
        for k in range(GROUP):
            slice_rows = slice(k * quarter, (k + 1) * quarter)
            step[mate ^ k, 0] = real[slice_rows]
            step[mate ^ k, 1] = imag[slice_rows]


def place_all(size, minibatch, info, grads, tall, part):
    tiles, strip, pattern = size
    tall[pattern : 2 * pattern + strip] = jnp.zeros((pattern + strip, tall.shape[1]), F32)
    own = info[25]
    for side, slot, ref, start in grads:
        row, column = spot(info, size, minibatch, side, own if slot == 0 else 1 - own)
        add_at(tall, ref[part], row + pattern + start, column)


def update_kernel(size, info, strip_ref, below, above, illum, own, other, b0, a0, b1, a1, *outs):
    patch, coverage, strip_out, tall, window = outs
    tiles, strip, pattern = size
    half = pattern // 2
    row, column = spot(info, size, 1, 0, info[25])
    grads = ((0, 0, own, 0), (0, 1, other, 0), (-1, 0, b0, 0), (1, 0, a0, 0), (-1, 1, b1, 0), (1, 1, a1, 0))
    for part in range(2):
        place_all(size, 0, info, grads, tall, part)
        change = tall[pattern : 2 * pattern + strip] / (illum[...] + 1.0)
        strip_out[part] = strip_ref[part] + change[half : half + strip]
        old = cut_patch(size, info, 1, strip_ref, below, above, window, part)
        window[: pattern + strip] = take_columns(change, column, pattern)
        new = old + rows_at(window, row, pattern)
        patch[part] = new
        if part == 0:
            coverage[...] = new * new
        else:
            coverage[...] += new * new


def final_kernel(size, info, strip_ref, illum, own, other, b0, a0, b1, a1, strip_out, tall):
    tiles, strip, pattern = size
    half = pattern // 2
    grads = (
        (0, 0, own, 0),
        (0, 1, other, 0),
        (-1, 0, b0, half),
        (1, 0, a0, 0),
        (-1, 1, b1, half),
        (1, 1, a1, 0),
    )
    for part in range(2):
        place_all(size, 1, info, grads, tall, part)
        change = tall[pattern + half : pattern + half + strip] / (illum[half : half + strip] + 1.0)
        strip_out[part] = strip_ref[part] + change


def piece_kernel(info, s0, s1, s2, s3, probe, coverage, out):
    quarter = out.shape[1]
    start = pl.multiple_of(lax.rem(info[24], GROUP) * quarter, quarter)
    rows = pl.ds(start, quarter)
    divisor = coverage[rows, :] + 1.0
    for part in range(2):
        total = (s0[part] + s1[part]) + (s2[part] + s3[part])
        out[part] = probe[part, rows, :] + total / divisor


def gather_kernel(info, p0, p1, p2, p3, out):
    quarter = p0.shape[1]
    mate = lax.rem(info[24], GROUP)
    for k, piece in enumerate((p0, p1, p2, p3)):
        rows = pl.ds(pl.multiple_of((mate ^ k) * quarter, quarter), quarter)
        for part in range(2):
            out[part, rows, :] = piece[part]


def call(kernel, name, outs, inputs, scratch=(), flops=0):
    shapes = [jax.ShapeDtypeStruct(shape, F32) for shape in outs]
    size = 4 * sum(math.prod(shape) for shape in outs) + sum(
        value.size * value.dtype.itemsize for value in inputs
    )
    smem = pl.BlockSpec(memory_space=pltpu.SMEM)
    vmem = pl.BlockSpec(memory_space=pltpu.VMEM)
    return pl.pallas_call(
        kernel,
        out_shape=shapes,
        in_specs=[smem] + [vmem] * (len(inputs) - 1),
        out_specs=[vmem] * len(shapes),
        scratch_shapes=[pltpu.VMEM(shape, F32) for shape in scratch],
        compiler_params=pltpu.CompilerParams(vmem_limit_bytes=VMEM_BYTES),
        cost_estimate=pl.CostEstimate(flops=flops, bytes_accessed=size, transcendentals=0),
        name=name,
    )(*inputs)


def shards_by_position(object_field, probe, positions, measured):
    strip = object_field.shape[1]
    width = object_field.shape[2]
    pattern = probe.shape[2]
    half = pattern // 2
    tiles = lax.axis_size("tile")
    size = (tiles, strip, pattern)
    field = (2, pattern, pattern)
    tall = (3 * pattern + strip + 8, width)
    window = (pattern + strip + 8, pattern)
    up = [(i, i + 1) for i in range(tiles - 1)]
    down = [(i + 1, i) for i in range(tiles - 1)]

    def swap(value):
        return lax.ppermute(value, "mode", [(0, 1), (1, 0)])

    def across(value, k):
        return lax.ppermute(value, "tile", [(i, i ^ k) for i in range(tiles)])

    def from_below(value):
        return lax.ppermute(value, "tile", up)

    def from_above(value):
        return lax.ppermute(value, "tile", down)

    def bind(kernel, *args):
        return functools.partial(kernel, *args)

    table = jnp.asarray(split_table(pattern))
    index = jnp.stack([lax.axis_index("tile"), lax.axis_index("mode")]).astype(jnp.int32)
    below, above = from_below(positions), from_above(positions)
    info = jnp.concatenate([below.ravel(), positions.ravel(), above.ravel(), index])
    own = probe[0]
    other = swap(own)

    low1, high1, low2, high2 = call(
        bind(edges_kernel, size), "edges", [(2, half, pattern)] * 4, (info, object_field)
    )
    below1, above1 = from_below(high1), from_above(low1)
    below2, above2 = from_below(high2), from_above(low2)
    patch, coverage = call(
        bind(patch_kernel, size),
        "patch",
        [field, (pattern, pattern)],
        (info, object_field, below1, above1),
        [window],
    )

    def probe_update(step_own, step_other, total_coverage, own):
        blocks = step_own + swap(step_other)
        piece = blocks[0]
        for k in range(1, GROUP):
            piece = piece + across(blocks[k], k)
        parts = [piece] + [across(piece, GROUP * k) for k in range(1, tiles // GROUP)]
        parts = parts[:3] + [functools.reduce(jnp.add, parts[3:])]
        (fresh,) = call(
            piece_kernel, "piece", [piece.shape], (info, *parts, own, total_coverage)
        )
        fresh_all = [fresh] + [across(fresh, k) for k in range(1, GROUP)]
        (full,) = call(gather_kernel, "gather", [field], (info, *fresh_all))
        return full

    def fields(minibatch, patch, own, other):
        quarter = (GROUP, 2, pattern // GROUP, pattern)
        return call(
            bind(field_kernel, size, minibatch),
            "field",
            [field, quarter, quarter],
            (info, patch, own, other, measured, table),
            flops=2 * 12 * 512**3,
        )

    def illuminate(minibatch, own, other):
        return call(
            bind(illumination_kernel, size, minibatch),
            "illumination",
            [(pattern + strip, width)],
            (info, own, other),
            [tall],
        )[0]

    total_coverage = lax.psum(coverage, ("tile", "mode"))
    gradient, step_own, step_other = fields(0, patch, own, other)
    illum = illuminate(0, own, other)
    grad_below, grad_above = from_below(gradient), from_above(gradient)
    grad_other = swap(gradient)
    below_other, above_other = swap(grad_below), swap(grad_above)
    patch, coverage, object_field = call(
        bind(update_kernel, size),
        "update",
        [field, (pattern, pattern), object_field.shape],
        (info, object_field, below2, above2, illum, gradient, grad_other)
        + (grad_below, grad_above, below_other, above_other),
        [tall, window],
    )
    own = probe_update(step_own, step_other, total_coverage, own)
    other = swap(own)
    coverage, total_coverage = lax.optimization_barrier((coverage, total_coverage))
    total_coverage = lax.psum(coverage, ("tile", "mode"))

    gradient, step_own, step_other = fields(1, patch, own, other)
    illum = illuminate(1, own, other)
    grad_below, grad_above = from_below(gradient[:, half:]), from_above(gradient[:, :half])
    grad_other = swap(gradient)
    below_other, above_other = swap(grad_below), swap(grad_above)
    (object_field,) = call(
        bind(final_kernel, size),
        "final",
        [object_field.shape],
        (info, object_field, illum, gradient, grad_other)
        + (grad_below, grad_above, below_other, above_other),
        [tall],
    )
    own = probe_update(step_own, step_other, total_coverage, own)
    return (object_field, own[None])


def solution(mesh):
    in_specs = (
        P(None, "tile", None),
        P("mode", None, None, None),
        P(None, "tile", None),
        P(None, "tile", None, None),
    )
    out_specs = (P(None, "tile", None), P("mode", None, None, None))

    def whole(object_field, probe, positions, measured):
        tiles, pair = mesh.shape["tile"], mesh.shape["mode"]
        by_position = (
            pair == 2
            and probe.shape[0] == 2
            and positions.shape[:2] == (2, 2 * tiles)
            and tiles >= 2 * GROUP
            and tiles & (tiles - 1) == 0
            and object_field.shape[1] == tiles * probe.shape[2]
        )
        shards = shards_by_position if by_position else shards_by_mode
        return jax.shard_map(
            shards, mesh=mesh, in_specs=in_specs, out_specs=out_specs, check_vma=False
        )(object_field, probe, positions, measured)

    return whole
```

```python
import functools
import math

import jax
import jax.numpy as jnp
import numpy as np
from jax import lax
from jax.experimental import pallas as pl
from jax.experimental.pallas import tpu as pltpu
from jax.sharding import PartitionSpec as P

F32 = jnp.float32
BF16 = jnp.bfloat16
VMEM_BYTES = 40 * 1024 * 1024
GROUP = 4


def padded(block, sides, width):
    for axis, dim in sides:
        count = lax.axis_size(axis)
        forward = [(i, i + 1) for i in range(count - 1)]
        backward = [(target, source) for source, target in forward]
        low = lax.ppermute(
            lax.slice_in_dim(block, block.shape[dim] - width, None, axis=dim), axis, forward
        )
        high = lax.ppermute(lax.slice_in_dim(block, 0, width, axis=dim), axis, backward)
        block = jnp.concatenate([low, block, high], axis=dim)
    return block


def tables(length):
    index_values = jnp.arange(length, dtype=jnp.int32)
    product = index_values[:, None] * index_values[None, :] % length
    angles = product.astype(jnp.float32) * (2.0 * math.pi / length)
    scaling = 1.0 / math.sqrt(length)
    return (jnp.cos(angles) * scaling, jnp.sin(angles) * scaling)


def apply_left(matrix, target):
    return jnp.einsum("ab,pbc->pac", matrix, target, precision=lax.Precision.HIGHEST)


def apply_right(target, matrix):
    return jnp.einsum("pab,bc->pac", target, matrix, precision=lax.Precision.HIGHEST)


def transform(real_part, imag_part, cosine, sine_table, direction):
    left_real = apply_left(cosine, real_part) + direction * apply_left(sine_table, imag_part)
    left_imag = apply_left(cosine, imag_part) - direction * apply_left(sine_table, real_part)
    out_real = apply_right(left_real, cosine) + direction * apply_right(left_imag, sine_table)
    out_imag = apply_right(left_imag, cosine) - direction * apply_right(left_real, sine_table)
    return (out_real, out_imag)


def place_add(target, placed, row_start, col_start):
    zero_index = jnp.int32(0)
    current = lax.dynamic_slice(target, (zero_index, row_start, col_start), placed.shape)
    return lax.dynamic_update_slice(target, current + placed, (zero_index, row_start, col_start))


def shards_by_mode(object_field, probe, positions, measured):
    strip_rows = object_field.shape[1]
    object_width = object_field.shape[2]
    pattern = probe.shape[2]
    half_pattern = pattern // 2
    count = positions.shape[1]
    cosine, sine_table = tables(pattern)
    tile_index = lax.axis_index("tile")
    offset = tile_index * strip_rows - half_pattern
    for minibatch in range(measured.shape[0]):
        extended = padded(object_field, (("tile", 1),), half_pattern)
        row_offsets = positions[minibatch, :, 0] - offset
        column_offsets = positions[minibatch, :, 1]

        def cut_one(row_start, col_start):
            return lax.dynamic_slice(
                extended, (jnp.int32(0), row_start, col_start), (2, pattern, pattern)
            )

        patches = jax.vmap(cut_one)(row_offsets, column_offsets)
        obj_real = patches[:, 0]
        obj_imag = patches[:, 1]
        probe_real = probe[0, 0]
        probe_imag = probe[0, 1]
        exit_real = probe_real * obj_real - probe_imag * obj_imag
        exit_imag = probe_real * obj_imag + probe_imag * obj_real
        far_real, far_imag = transform(exit_real, exit_imag, cosine, sine_table, 1.0)
        observed = measured[minibatch]
        intensity = lax.psum(far_real * far_real + far_imag * far_imag, "mode")
        modulus = jnp.sqrt((observed + 1.0) / (intensity + 1.0)) - 1.0
        chi_real, chi_imag = transform(
            modulus * far_real, modulus * far_imag, cosine, sine_table, -1.0
        )
        grad_real = probe_real * chi_real + probe_imag * chi_imag
        grad_imag = probe_real * chi_imag - probe_imag * chi_real
        probe_power = probe_real * probe_real + probe_imag * probe_imag
        step_real = jnp.sum(obj_real * chi_real + obj_imag * chi_imag, axis=0)
        step_imag = jnp.sum(obj_real * chi_imag - obj_imag * chi_real, axis=0)
        coverage = jnp.sum(obj_real * obj_real + obj_imag * obj_imag, axis=0)
        accumulated = jnp.zeros((3, strip_rows + pattern, object_width), jnp.float32)
        for position in range(count):
            placed = jnp.stack([grad_real[position], grad_imag[position], probe_power])
            accumulated = place_add(
                accumulated, placed, row_offsets[position], column_offsets[position]
            )
        rim_rows = jnp.concatenate(
            [accumulated[:, :half_pattern], accumulated[:, strip_rows + half_pattern :]], axis=1
        )
        received = padded(rim_rows, (("tile", 1),), half_pattern)
        own_strip = accumulated[:, half_pattern : half_pattern + strip_rows]
        own_strip = own_strip.at[:, :half_pattern].add(received[:, :half_pattern])
        own_strip = own_strip.at[:, strip_rows - half_pattern :].add(
            received[:, pattern + half_pattern :]
        )
        summed = lax.psum(own_strip, "mode")
        divisor = summed[2] + 1.0
        object_field = jnp.stack(
            [object_field[0] + summed[0] / divisor, object_field[1] + summed[1] / divisor]
        )
        step_stack = jnp.stack([jnp.stack([step_real, step_imag])])
        step_total, coverage_total = lax.psum((step_stack, coverage), "tile")
        probe = probe + step_total / (coverage_total + 1.0)
    return (object_field, probe)


def split_table(length):
    index_values = np.arange(length)
    angles = (index_values[:, None] * index_values[None, :] % length) * (2.0 * np.pi / length)
    scaling = 1.0 / np.sqrt(length)
    parts = []
    for table in (np.cos(angles) * scaling, np.sin(angles) * scaling):
        high = table.astype(jnp.bfloat16)
        parts += [high, (table - high.astype(np.float64)).astype(jnp.bfloat16)]
    return np.stack(parts)


def spot(info, size, minibatch, side, slot):
    tiles, strip, pattern = size
    place = (((side + 1) * 2 + minibatch) * 2 + slot) * 2
    tile = info[24]
    row = info[place] - tile * strip + pattern // 2
    if side < 0:
        row = jnp.where(tile == 0, -pattern, row)
    if side > 0:
        row = jnp.where(tile == tiles - 1, strip + pattern, row)
    return row, info[place + 1]


def take_columns(block, column, width):
    total = block.shape[-1]
    return pltpu.roll(block, lax.rem(total - column, total), 1)[:, :width]


def add_at(tall, block, row, column):
    rows, width = block.shape
    total = tall.shape[1]
    shift = lax.rem(row, 8)
    start = pl.multiple_of(row - shift, 8)
    turned = pltpu.roll(block.reshape(rows // 8, 8, width), shift, 1)
    empty = jnp.zeros((1, 8, width), block.dtype)
    inside = lax.broadcasted_iota(jnp.int32, (rows // 8 + 1, 8, width), 1) >= shift
    moved = jnp.where(
        inside,
        jnp.concatenate([turned, empty], axis=0),
        jnp.concatenate([empty, turned], axis=0),
    ).reshape(rows + 8, width)
    wide = jnp.concatenate([moved, jnp.zeros((rows + 8, total - width), block.dtype)], axis=1)
    tall[pl.ds(start, rows + 8), :] += pltpu.roll(wide, column, 1)


def rows_at(ref, row, rows):
    width = ref.shape[1]
    shift = lax.rem(row, 8)
    start = pl.multiple_of(row - shift, 8)
    block = ref[pl.ds(start, rows + 8), :].reshape(rows // 8 + 1, 8, width)
    turned = pltpu.roll(block, lax.rem(8 - shift, 8), 1)
    inside = lax.broadcasted_iota(jnp.int32, (rows // 8, 8, width), 1) < 8 - shift
    return jnp.where(inside, turned[:-1], turned[1:]).reshape(rows, width)


def halves(value):
    high = value.astype(BF16)
    return high, (value - high.astype(F32)).astype(BF16)


def product(left, right):
    dot = functools.partial(jnp.dot, preferred_element_type=F32)
    return dot(left[0], right[0]) + (dot(left[0], right[1]) + dot(left[1], right[0]))


def cut_patch(size, info, minibatch, strip_ref, below, above, window, part):
    tiles, rows, width = size
    half = width // 2
    row, column = spot(info, size, minibatch, 0, info[25])

    def columns(block):
        return block if block.shape[1] == width else take_columns(block, column, width)

    window[:half] = columns(below)
    window[half : half + rows] = columns(strip_ref[part])
    window[half + rows : rows + width] = columns(above)
    return rows_at(window, row, width)


def illumination_kernel(size, minibatch, info, own, other, out, tall):
    tiles, strip, pattern = size
    half = pattern // 2
    kept = slice(pattern + half, pattern + half + strip)
    tall[kept] = jnp.zeros((strip, tall.shape[1]), F32)
    power = own[0] * own[0] + own[1] * own[1] + (other[0] * other[0] + other[1] * other[1])
    for side in (-1, 0, 1):
        for slot in range(2):
            row, column = spot(info, size, minibatch, side, slot)
            add_at(tall, power, row + pattern, column)
    out[...] = tall[kept]


def field_kernel(size, minibatch, info, strip_ref, *refs):
    edges, (own, other, measured, table), (gradient, step_own, step_other, window) = (
        refs[:-8],
        refs[-8:-4],
        refs[-4:],
    )
    pattern = size[2]
    quarter = pattern // GROUP
    slot = info[25]
    cos_high, cos_low, sin_high, sin_low = (table[i] for i in range(4))

    def block(top_left, top_right, low_left, low_right):
        return jnp.concatenate(
            [
                jnp.concatenate([top_left, top_right], axis=1),
                jnp.concatenate([low_left, low_right], axis=1),
            ],
            axis=0,
        )

    first = (
        block(cos_high, sin_high, -sin_high, cos_high),
        block(cos_low, sin_low, -sin_low, cos_low),
    )
    second = (
        block(cos_high, -sin_high, sin_high, cos_high),
        block(cos_low, -sin_low, sin_low, cos_low),
    )
    def edge(side, part):
        if len(edges) == 2:
            return edges[side][part]
        return jnp.where(slot == part, edges[2 * side][...], edges[2 * side + 1][...])

    obj_real, obj_imag = (
        cut_patch(size, info, minibatch, strip_ref, edge(0, part), edge(1, part), window, part)
        for part in range(2)
    )
    probes = ((own[0], own[1]), (other[0], other[1]))

    def both(fields, left, right):
        (r0, i0), (r1, i1) = fields
        y = product(left, halves(block(r0, r1, i0, i1)))
        y = block(
            y[:pattern, :pattern], y[pattern:, :pattern], y[:pattern, pattern:], y[pattern:, pattern:]
        )
        y = product(halves(y), right)
        return (
            (y[:pattern, :pattern], y[:pattern, pattern:]),
            (y[pattern:, :pattern], y[pattern:, pattern:]),
        )

    exits = [(pr * obj_real - pi * obj_imag, pr * obj_imag + pi * obj_real) for pr, pi in probes]
    far = both(exits, first, second)
    intensity = (far[0][0] * far[0][0] + far[0][1] * far[0][1]) + (
        far[1][0] * far[1][0] + far[1][1] * far[1][1]
    )
    factor = jnp.sqrt((measured[minibatch, slot] + 1.0) / (intensity + 1.0)) - 1.0
    chi = both([(factor * fr, factor * fi) for fr, fi in far], second, first)
    (pr0, pi0), (pr1, pi1) = probes
    (cr0, ci0), (cr1, ci1) = chi
    gradient[0] = (pr0 * cr0 + pi0 * ci0) + (pr1 * cr1 + pi1 * ci1)
    gradient[1] = (pr0 * ci0 - pi0 * cr0) + (pr1 * ci1 - pi1 * cr1)
    mate = lax.rem(info[24], GROUP)
    coverage = obj_real * obj_real + obj_imag * obj_imag
    for step, (cr, ci) in ((step_own, chi[0]), (step_other, chi[1])):
        real = obj_real * cr + obj_imag * ci
        imag = obj_real * ci - obj_imag * cr
        for k in range(GROUP):
            slice_rows = slice(k * quarter, (k + 1) * quarter)
            step[mate ^ k, 0] = real[slice_rows]
            step[mate ^ k, 1] = imag[slice_rows]
            step[mate ^ k, 2] = coverage[slice_rows]


def update_kernel(size, minibatch, info, strip_ref, illum, own, other, b0, a0, b1, a1, *outs):
    strip_out, *edges, tall = outs
    tiles, strip, pattern = size
    half = pattern // 2
    slot = info[25]
    kept = slice(pattern + half, pattern + half + strip)
    grads = (
        (0, slot, own, 0),
        (0, 1 - slot, other, 0),
        (-1, slot, b0, half),
        (1, slot, a0, 0),
        (-1, 1 - slot, b1, half),
        (1, 1 - slot, a1, 0),
    )
    for part in range(2):
        tall[kept] = jnp.zeros((strip, tall.shape[1]), F32)
        for side, place, ref, start in grads:
            row, column = spot(info, size, minibatch, side, place)
            add_at(tall, ref[part], row + pattern + start, column)
        fresh = strip_ref[part] + tall[kept] / (illum[...] + 1.0)
        strip_out[part] = fresh
        if edges:
            column_below = spot(info, size, minibatch + 1, -1, slot)[1]
            column_above = spot(info, size, minibatch + 1, 1, slot)[1]
            edges[0][part] = take_columns(fresh[:half], column_below, pattern)
            edges[1][part] = take_columns(fresh[strip - half :], column_above, pattern)


def piece_kernel(info, s0, s1, s2, s3, probe, out):
    quarter = out.shape[1]
    start = pl.multiple_of(lax.rem(info[24], GROUP) * quarter, quarter)
    rows = pl.ds(start, quarter)

    def total(part):
        return (s0[part] + s1[part]) + (s2[part] + s3[part])

    divisor = total(2) + 1.0
    for part in range(2):
        out[part] = probe[part, rows, :] + total(part) / divisor


def gather_kernel(info, p0, p1, p2, p3, out):
    quarter = p0.shape[1]
    mate = lax.rem(info[24], GROUP)
    for k, piece in enumerate((p0, p1, p2, p3)):
        rows = pl.ds(pl.multiple_of((mate ^ k) * quarter, quarter), quarter)
        for part in range(2):
            out[part, rows, :] = piece[part]


def call(kernel, name, outs, inputs, scratch=(), flops=0):
    shapes = [jax.ShapeDtypeStruct(shape, F32) for shape in outs]
    size = 4 * sum(math.prod(shape) for shape in outs) + sum(
        value.size * value.dtype.itemsize for value in inputs
    )
    smem = pl.BlockSpec(memory_space=pltpu.SMEM)
    vmem = pl.BlockSpec(memory_space=pltpu.VMEM)
    return pl.pallas_call(
        kernel,
        out_shape=shapes,
        in_specs=[smem] + [vmem] * (len(inputs) - 1),
        out_specs=[vmem] * len(shapes),
        scratch_shapes=[pltpu.VMEM(shape, F32) for shape in scratch],
        compiler_params=pltpu.CompilerParams(vmem_limit_bytes=VMEM_BYTES),
        cost_estimate=pl.CostEstimate(flops=flops, bytes_accessed=size, transcendentals=0),
        name=name,
    )(*inputs)


def shards_by_position(object_field, probe, positions, measured):
    strip = object_field.shape[1]
    width = object_field.shape[2]
    pattern = probe.shape[2]
    half = pattern // 2
    tiles = lax.axis_size("tile")
    size = (tiles, strip, pattern)
    field = (2, pattern, pattern)
    tall = (3 * pattern + strip + 8, width)
    window = (pattern + strip + 8, pattern)
    up = [(i, i + 1) for i in range(tiles - 1)]
    down = [(i + 1, i) for i in range(tiles - 1)]

    def swap(value):
        return lax.ppermute(value, "mode", [(0, 1), (1, 0)])

    def across(value, k):
        return lax.ppermute(value, "tile", [(i, i ^ k) for i in range(tiles)])

    def from_below(value):
        return lax.ppermute(value, "tile", up)

    def from_above(value):
        return lax.ppermute(value, "tile", down)

    def bind(kernel, *args):
        return functools.partial(kernel, *args)

    table = jnp.asarray(split_table(pattern))
    tile, slot = lax.axis_index("tile"), lax.axis_index("mode")
    one_part = lax.dynamic_index_in_dim(object_field, slot, 0, keepdims=False)
    edges = [from_below(one_part[strip - half :]), from_above(one_part[:half])]
    edges = [edges[0], swap(edges[0]), edges[1], swap(edges[1])]
    index = jnp.stack([tile, slot]).astype(jnp.int32)
    below, above = from_below(positions), from_above(positions)
    info = jnp.concatenate([below.ravel(), positions.ravel(), above.ravel(), index])
    own = probe[0]
    other = swap(own)

    for minibatch in range(2):
        quarter = (GROUP, 3, pattern // GROUP, pattern)
        gradient, step_own, step_other = call(
            bind(field_kernel, size, minibatch),
            "field",
            [field, quarter, quarter],
            (info, object_field, *edges, own, other, measured, table),
            [window],
            flops=2 * 12 * 512**3,
        )
        (illum,) = call(
            bind(illumination_kernel, size, minibatch),
            "illumination",
            [(strip, width)],
            (info, own, other),
            [tall],
        )
        rim_below, rim_above = from_below(gradient[:, half:]), from_above(gradient[:, :half])
        rims = (gradient, swap(gradient), rim_below, rim_above, swap(rim_below), swap(rim_above))
        last = minibatch == 1
        object_field, *edges = call(
            bind(update_kernel, size, minibatch),
            "update",
            [object_field.shape] + ([] if last else [(2, half, pattern)] * 2),
            (info, object_field, illum, *rims),
            [tall],
        )
        if not last:
            edges = [from_below(edges[1]), from_above(edges[0])]

        blocks = step_own + swap(step_other)
        piece = blocks[0]
        for k in range(1, GROUP):
            piece = piece + across(blocks[k], k)
        parts = [piece] + [across(piece, GROUP * k) for k in range(1, tiles // GROUP)]
        parts = parts[:3] + [functools.reduce(jnp.add, parts[3:])]
        (fresh,) = call(
            piece_kernel, "piece", [(2, pattern // GROUP, pattern)], (info, *parts, own)
        )
        fresh_all = [fresh] + [across(fresh, k) for k in range(1, GROUP)]
        (own,) = call(gather_kernel, "gather", [field], (info, *fresh_all))
        if not last:
            other = swap(own)
    return (object_field, own[None])


def solution(mesh):
    in_specs = (
        P(None, "tile", None),
        P("mode", None, None, None),
        P(None, "tile", None),
        P(None, "tile", None, None),
    )
    out_specs = (P(None, "tile", None), P("mode", None, None, None))

    def whole(object_field, probe, positions, measured):
        tiles, pair = mesh.shape["tile"], mesh.shape["mode"]
        by_position = (
            pair == 2
            and probe.shape[0] == 2
            and positions.shape[:2] == (2, 2 * tiles)
            and tiles >= 2 * GROUP
            and tiles & (tiles - 1) == 0
            and object_field.shape[1] == tiles * probe.shape[2]
        )
        shards = shards_by_position if by_position else shards_by_mode
        return jax.shard_map(
            shards, mesh=mesh, in_specs=in_specs, out_specs=out_specs, check_vma=False
        )(object_field, probe, positions, measured)

    return whole
```

```python
import functools
import math

import jax
import jax.numpy as jnp
import numpy as np
from jax import lax
from jax.experimental import pallas as pl
from jax.experimental.pallas import tpu as pltpu
from jax.sharding import PartitionSpec as P

F32 = jnp.float32
BF16 = jnp.bfloat16
VMEM_BYTES = 40 * 1024 * 1024


def padded(block, sides, width):
    for axis, dim in sides:
        count = lax.axis_size(axis)
        forward = [(i, i + 1) for i in range(count - 1)]
        backward = [(target, source) for source, target in forward]
        low = lax.ppermute(
            lax.slice_in_dim(block, block.shape[dim] - width, None, axis=dim), axis, forward
        )
        high = lax.ppermute(lax.slice_in_dim(block, 0, width, axis=dim), axis, backward)
        block = jnp.concatenate([low, block, high], axis=dim)
    return block


def tables(length):
    index_values = jnp.arange(length, dtype=jnp.int32)
    product = index_values[:, None] * index_values[None, :] % length
    angles = product.astype(jnp.float32) * (2.0 * math.pi / length)
    scaling = 1.0 / math.sqrt(length)
    return (jnp.cos(angles) * scaling, jnp.sin(angles) * scaling)


def apply_left(matrix, target):
    return jnp.einsum("ab,pbc->pac", matrix, target, precision=lax.Precision.HIGHEST)


def apply_right(target, matrix):
    return jnp.einsum("pab,bc->pac", target, matrix, precision=lax.Precision.HIGHEST)


def transform(real_part, imag_part, cosine, sine_table, direction):
    left_real = apply_left(cosine, real_part) + direction * apply_left(sine_table, imag_part)
    left_imag = apply_left(cosine, imag_part) - direction * apply_left(sine_table, real_part)
    out_real = apply_right(left_real, cosine) + direction * apply_right(left_imag, sine_table)
    out_imag = apply_right(left_imag, cosine) - direction * apply_right(left_real, sine_table)
    return (out_real, out_imag)


def place_add(target, placed, row_start, col_start):
    zero_index = jnp.int32(0)
    current = lax.dynamic_slice(target, (zero_index, row_start, col_start), placed.shape)
    return lax.dynamic_update_slice(target, current + placed, (zero_index, row_start, col_start))


def shards_by_mode(object_field, probe, positions, measured):
    strip_rows = object_field.shape[1]
    object_width = object_field.shape[2]
    pattern = probe.shape[2]
    half_pattern = pattern // 2
    count = positions.shape[1]
    cosine, sine_table = tables(pattern)
    tile_index = lax.axis_index("tile")
    offset = tile_index * strip_rows - half_pattern
    for minibatch in range(measured.shape[0]):
        extended = padded(object_field, (("tile", 1),), half_pattern)
        row_offsets = positions[minibatch, :, 0] - offset
        column_offsets = positions[minibatch, :, 1]

        def cut_one(row_start, col_start):
            return lax.dynamic_slice(
                extended, (jnp.int32(0), row_start, col_start), (2, pattern, pattern)
            )

        patches = jax.vmap(cut_one)(row_offsets, column_offsets)
        obj_real = patches[:, 0]
        obj_imag = patches[:, 1]
        probe_real = probe[0, 0]
        probe_imag = probe[0, 1]
        exit_real = probe_real * obj_real - probe_imag * obj_imag
        exit_imag = probe_real * obj_imag + probe_imag * obj_real
        far_real, far_imag = transform(exit_real, exit_imag, cosine, sine_table, 1.0)
        observed = measured[minibatch]
        intensity = lax.psum(far_real * far_real + far_imag * far_imag, "mode")
        modulus = jnp.sqrt((observed + 1.0) / (intensity + 1.0)) - 1.0
        chi_real, chi_imag = transform(
            modulus * far_real, modulus * far_imag, cosine, sine_table, -1.0
        )
        grad_real = probe_real * chi_real + probe_imag * chi_imag
        grad_imag = probe_real * chi_imag - probe_imag * chi_real
        probe_power = probe_real * probe_real + probe_imag * probe_imag
        step_real = jnp.sum(obj_real * chi_real + obj_imag * chi_imag, axis=0)
        step_imag = jnp.sum(obj_real * chi_imag - obj_imag * chi_real, axis=0)
        coverage = jnp.sum(obj_real * obj_real + obj_imag * obj_imag, axis=0)
        accumulated = jnp.zeros((3, strip_rows + pattern, object_width), jnp.float32)
        for position in range(count):
            placed = jnp.stack([grad_real[position], grad_imag[position], probe_power])
            accumulated = place_add(
                accumulated, placed, row_offsets[position], column_offsets[position]
            )
        rim_rows = jnp.concatenate(
            [accumulated[:, :half_pattern], accumulated[:, strip_rows + half_pattern :]], axis=1
        )
        received = padded(rim_rows, (("tile", 1),), half_pattern)
        own_strip = accumulated[:, half_pattern : half_pattern + strip_rows]
        own_strip = own_strip.at[:, :half_pattern].add(received[:, :half_pattern])
        own_strip = own_strip.at[:, strip_rows - half_pattern :].add(
            received[:, pattern + half_pattern :]
        )
        summed = lax.psum(own_strip, "mode")
        divisor = summed[2] + 1.0
        object_field = jnp.stack(
            [object_field[0] + summed[0] / divisor, object_field[1] + summed[1] / divisor]
        )
        step_stack = jnp.stack([jnp.stack([step_real, step_imag])])
        step_total, coverage_total = lax.psum((step_stack, coverage), "tile")
        probe = probe + step_total / (coverage_total + 1.0)
    return (object_field, probe)


def table_of(length):
    index_values = np.arange(length)
    angles = (index_values[:, None] * index_values[None, :] % length) * (2.0 * np.pi / length)
    scaling = 1.0 / np.sqrt(length)
    return np.stack([np.cos(angles) * scaling, np.sin(angles) * scaling]).astype(np.float32)


def spot(info, size, minibatch, side, slot):
    tiles, strip, pattern = size
    place = (((side + 1) * 2 + minibatch) * 2 + slot) * 2
    tile = info[24]
    row = info[place] - tile * strip + pattern // 2
    if side < 0:
        row = jnp.where(tile == 0, -pattern, row)
    if side > 0:
        row = jnp.where(tile == tiles - 1, strip + pattern, row)
    return row, info[place + 1]


def part_of(ref, part):
    if len(ref.shape) == 3:
        return ref[part]
    return ref[:, part].reshape(ref.shape[0] * ref.shape[2], ref.shape[3])


def take_columns(block, column, width):
    total = block.shape[-1]
    return pltpu.roll(block, lax.rem(total - column, total), 1)[:, :width]


def add_at(tall, block, row, column):
    rows, width = block.shape
    total = tall.shape[1]
    shift = lax.rem(row, 8)
    start = pl.multiple_of(row - shift, 8)
    turned = pltpu.roll(block.reshape(rows // 8, 8, width), shift, 1)
    empty = jnp.zeros((1, 8, width), block.dtype)
    inside = lax.broadcasted_iota(jnp.int32, (rows // 8 + 1, 8, width), 1) >= shift
    moved = jnp.where(
        inside,
        jnp.concatenate([turned, empty], axis=0),
        jnp.concatenate([empty, turned], axis=0),
    ).reshape(rows + 8, width)
    wide = jnp.concatenate([moved, jnp.zeros((rows + 8, total - width), block.dtype)], axis=1)
    tall[pl.ds(start, rows + 8), :] += pltpu.roll(wide, column, 1)


def rows_at(ref, row, rows):
    width = ref.shape[1]
    shift = lax.rem(row, 8)
    start = pl.multiple_of(row - shift, 8)
    block = ref[pl.ds(start, rows + 8), :].reshape(rows // 8 + 1, 8, width)
    turned = pltpu.roll(block, lax.rem(8 - shift, 8), 1)
    inside = lax.broadcasted_iota(jnp.int32, (rows // 8, 8, width), 1) < 8 - shift
    return jnp.where(inside, turned[:-1], turned[1:]).reshape(rows, width)


def halves(value):
    high = value.astype(BF16)
    return high, (value - high.astype(F32)).astype(BF16)


def product(left, right):
    dot = functools.partial(jnp.dot, preferred_element_type=F32)
    return dot(left[0], right[0]) + (dot(left[0], right[1]) + dot(left[1], right[0]))


def cut_patch(size, info, minibatch, strip_ref, below, above, window, part):
    tiles, rows, width = size
    half = width // 2
    row, column = spot(info, size, minibatch, 0, info[25])

    def columns(block):
        return block if block.shape[1] == width else take_columns(block, column, width)

    window[:half] = columns(below)
    window[half : half + rows] = columns(strip_ref[part])
    window[half + rows : rows + width] = columns(above)
    return rows_at(window, row, width)


def illumination_kernel(size, minibatch, info, own, other, out, tall):
    tiles, strip, pattern = size
    half = pattern // 2
    kept = slice(pattern + half, pattern + half + strip)
    tall[kept] = jnp.zeros((strip, tall.shape[1]), F32)
    (pr0, pi0), (pr1, pi1) = ((part_of(ref, 0), part_of(ref, 1)) for ref in (own, other))
    power = pr0 * pr0 + pi0 * pi0 + (pr1 * pr1 + pi1 * pi1)
    for side in (-1, 0, 1):
        for slot in range(2):
            row, column = spot(info, size, minibatch, side, slot)
            add_at(tall, power, row + pattern, column)
    out[...] = tall[kept]


def field_kernel(size, minibatch, info, strip_ref, *refs):
    edges, (own, other, measured, table) = refs[:-10], refs[-10:-6]
    gradient, step_own, step_other, window, observed, arrived = refs[-6:]
    tiles, strip, pattern = size
    slot = info[25]
    fetch = pltpu.make_async_copy(measured.at[minibatch, slot], observed, arrived)
    fetch.start()
    (cos_high, cos_low), (sin_high, sin_low) = halves(table[0]), halves(table[1])

    def block(top_left, top_right, low_left, low_right):
        return jnp.concatenate(
            [
                jnp.concatenate([top_left, top_right], axis=1),
                jnp.concatenate([low_left, low_right], axis=1),
            ],
            axis=0,
        )

    first = (
        block(cos_high, sin_high, -sin_high, cos_high),
        block(cos_low, sin_low, -sin_low, cos_low),
    )
    second = (
        block(cos_high, -sin_high, sin_high, cos_high),
        block(cos_low, -sin_low, sin_low, cos_low),
    )
    def edge(side, part):
        if len(edges) == 2:
            return edges[side][part]
        return jnp.where(slot == part, edges[2 * side][...], edges[2 * side + 1][...])

    obj_real, obj_imag = (
        cut_patch(size, info, minibatch, strip_ref, edge(0, part), edge(1, part), window, part)
        for part in range(2)
    )
    probes = [(part_of(ref, 0), part_of(ref, 1)) for ref in (own, other)]

    def both(fields, left, right):
        (r0, i0), (r1, i1) = fields
        y = product(left, halves(block(r0, r1, i0, i1)))
        y = block(
            y[:pattern, :pattern], y[pattern:, :pattern], y[:pattern, pattern:], y[pattern:, pattern:]
        )
        y = product(halves(y), right)
        return (
            (y[:pattern, :pattern], y[:pattern, pattern:]),
            (y[pattern:, :pattern], y[pattern:, pattern:]),
        )

    exits = [(pr * obj_real - pi * obj_imag, pr * obj_imag + pi * obj_real) for pr, pi in probes]
    far = both(exits, first, second)
    intensity = (far[0][0] * far[0][0] + far[0][1] * far[0][1]) + (
        far[1][0] * far[1][0] + far[1][1] * far[1][1]
    )
    fetch.wait()
    factor = jnp.sqrt((observed[...] + 1.0) / (intensity + 1.0)) - 1.0
    chi = both([(factor * fr, factor * fi) for fr, fi in far], second, first)
    (pr0, pi0), (pr1, pi1) = probes
    (cr0, ci0), (cr1, ci1) = chi
    gradient[0] = (pr0 * cr0 + pi0 * ci0) + (pr1 * cr1 + pi1 * ci1)
    gradient[1] = (pr0 * ci0 - pi0 * cr0) + (pr1 * ci1 - pi1 * cr1)
    coverage = obj_real * obj_real + obj_imag * obj_imag
    rows = pattern // tiles
    for step, (cr, ci) in ((step_own, chi[0]), (step_other, chi[1])):
        for part, value in (
            (0, obj_real * cr + obj_imag * ci),
            (1, obj_real * ci - obj_imag * cr),
            (2, coverage),
        ):
            step[:, part] = value.reshape(tiles, rows, pattern)


def update_kernel(size, minibatch, info, strip_ref, illum, own, other, b0, a0, b1, a1, *outs):
    strip_out, *edges, tall = outs
    tiles, strip, pattern = size
    half = pattern // 2
    slot = info[25]
    kept = slice(pattern + half, pattern + half + strip)
    grads = (
        (0, slot, own, 0),
        (0, 1 - slot, other, 0),
        (-1, slot, b0, half),
        (1, slot, a0, 0),
        (-1, 1 - slot, b1, half),
        (1, 1 - slot, a1, 0),
    )
    for part in range(2):
        tall[kept] = jnp.zeros((strip, tall.shape[1]), F32)
        for side, place, ref, start in grads:
            row, column = spot(info, size, minibatch, side, place)
            add_at(tall, ref[part], row + pattern + start, column)
        fresh = strip_ref[part] + tall[kept] / (illum[...] + 1.0)
        strip_out[part] = fresh
        if edges:
            column_below = spot(info, size, minibatch + 1, -1, slot)[1]
            column_above = spot(info, size, minibatch + 1, 1, slot)[1]
            edges[0][part] = take_columns(fresh[:half], column_below, pattern)
            edges[1][part] = take_columns(fresh[strip - half :], column_above, pattern)


def piece_kernel(info, sums, probe, out):
    tiles, parts, rows, width = sums.shape
    tile = info[24]
    total = sums[0]
    for k in range(1, tiles):
        total += sums[k]
    divisor = total[2] + 1.0
    for part in range(2):
        if len(probe.shape) == 3:
            held = probe[part, pl.ds(pl.multiple_of(tile * rows, rows), rows), :]
        else:
            held = probe[tile, part]
        fresh = held + total[part] / divisor
        for k in range(tiles):
            out[k, part] = fresh


def gather_kernel(info, blocks, out):
    for part in range(2):
        out[part] = part_of(blocks, part)


def call(kernel, name, outs, inputs, scratch=(), flops=0, far=None):
    shapes = [jax.ShapeDtypeStruct(shape, F32) for shape in outs]
    size = 4 * sum(math.prod(shape) for shape in outs) + sum(
        value.size * value.dtype.itemsize for value in inputs
    )
    smem = pl.BlockSpec(memory_space=pltpu.SMEM)
    vmem = pl.BlockSpec(memory_space=pltpu.VMEM)
    return pl.pallas_call(
        kernel,
        out_shape=shapes,
        in_specs=[smem]
        + [pl.BlockSpec(memory_space=pl.ANY) if value is far else vmem for value in inputs[1:]],
        out_specs=[vmem] * len(shapes),
        scratch_shapes=[pltpu.VMEM(shape, F32) for shape in scratch]
        + ([] if far is None else [pltpu.SemaphoreType.DMA]),
        compiler_params=pltpu.CompilerParams(vmem_limit_bytes=VMEM_BYTES),
        cost_estimate=pl.CostEstimate(flops=flops, bytes_accessed=size, transcendentals=0),
        name=name,
    )(*inputs)


def shards_by_position(object_field, probe, positions, measured):
    strip = object_field.shape[1]
    width = object_field.shape[2]
    pattern = probe.shape[2]
    half = pattern // 2
    tiles = lax.axis_size("tile")
    size = (tiles, strip, pattern)
    field = (2, pattern, pattern)
    tall = (3 * pattern + strip + 8, width)
    window = (pattern + strip + 8, pattern)
    up = [(i, i + 1) for i in range(tiles - 1)]
    down = [(i + 1, i) for i in range(tiles - 1)]

    def swap(value):
        return lax.ppermute(value, "mode", [(0, 1), (1, 0)])

    def to_all(blocks):
        return lax.all_to_all(blocks, "tile", 0, 0, tiled=True)

    def from_below(value):
        return lax.ppermute(value, "tile", up)

    def from_above(value):
        return lax.ppermute(value, "tile", down)

    def bind(kernel, *args):
        return functools.partial(kernel, *args)

    table = jnp.asarray(table_of(pattern))
    tile, slot = lax.axis_index("tile"), lax.axis_index("mode")
    one_part = lax.dynamic_index_in_dim(object_field, slot, 0, keepdims=False)
    edges = [from_below(one_part[strip - half :]), from_above(one_part[:half])]
    edges = [edges[0], swap(edges[0]), edges[1], swap(edges[1])]
    index = jnp.stack([tile, slot]).astype(jnp.int32)
    below, above = from_below(positions), from_above(positions)
    here = jnp.concatenate([positions.ravel()] * 3 + [index])
    info = jnp.concatenate([below.ravel(), positions.ravel(), above.ravel(), index])
    own = probe[0]
    other = swap(own)

    for minibatch in range(2):
        blocks = (tiles, 3, pattern // tiles, pattern)
        gradient, step_own, step_other = call(
            bind(field_kernel, size, minibatch),
            "field",
            [field, blocks, blocks],
            (here, object_field, *edges, own, other, measured, table),
            [window, (pattern, pattern)],
            flops=2 * 12 * 512**3,
            far=measured,
        )
        (illum,) = call(
            bind(illumination_kernel, size, minibatch),
            "illumination",
            [(strip, width)],
            (info, own, other),
            [tall],
        )
        rim_below, rim_above = from_below(gradient[:, half:]), from_above(gradient[:, :half])
        rims = (gradient, swap(gradient), rim_below, rim_above, swap(rim_below), swap(rim_above))
        last = minibatch == 1
        object_field, *edges = call(
            bind(update_kernel, size, minibatch),
            "update",
            [object_field.shape] + ([] if last else [(2, half, pattern)] * 2),
            (info, object_field, illum, *rims),
            [tall],
        )
        if not last:
            edges = [from_below(edges[1]), from_above(edges[0])]

        sums = to_all(step_own + swap(step_other))
        (fresh,) = call(
            piece_kernel, "piece", [(tiles, 2, pattern // tiles, pattern)], (here, sums, own)
        )
        own = to_all(fresh)
        if not last:
            other = swap(own)
    (own,) = call(gather_kernel, "gather", [field], (here, own))
    return (object_field, own[None])


def solution(mesh):
    in_specs = (
        P(None, "tile", None),
        P("mode", None, None, None),
        P(None, "tile", None),
        P(None, "tile", None, None),
    )
    out_specs = (P(None, "tile", None), P("mode", None, None, None))

    def whole(object_field, probe, positions, measured):
        tiles, pair = mesh.shape["tile"], mesh.shape["mode"]
        by_position = (
            pair == 2
            and probe.shape[0] == 2
            and positions.shape[:2] == (2, 2 * tiles)
            and probe.shape[2] % (8 * tiles) == 0
            and object_field.shape[1] == tiles * probe.shape[2]
        )
        shards = shards_by_position if by_position else shards_by_mode
        return jax.shard_map(
            shards, mesh=mesh, in_specs=in_specs, out_specs=out_specs, check_vma=False
        )(object_field, probe, positions, measured)

    return whole
```

```python
import functools
import math

import jax
import jax.numpy as jnp
import numpy as np
from jax import lax
from jax.experimental import pallas as pl
from jax.experimental.pallas import tpu as pltpu
from jax.sharding import PartitionSpec as P

F32 = jnp.float32
BF16 = jnp.bfloat16
VMEM_BYTES = 40 * 1024 * 1024


def padded(block, sides, width):
    for axis, dim in sides:
        count = lax.axis_size(axis)
        forward = [(i, i + 1) for i in range(count - 1)]
        backward = [(target, source) for source, target in forward]
        low = lax.ppermute(
            lax.slice_in_dim(block, block.shape[dim] - width, None, axis=dim), axis, forward
        )
        high = lax.ppermute(lax.slice_in_dim(block, 0, width, axis=dim), axis, backward)
        block = jnp.concatenate([low, block, high], axis=dim)
    return block


def tables(length):
    index_values = jnp.arange(length, dtype=jnp.int32)
    product = index_values[:, None] * index_values[None, :] % length
    angles = product.astype(jnp.float32) * (2.0 * math.pi / length)
    scaling = 1.0 / math.sqrt(length)
    return (jnp.cos(angles) * scaling, jnp.sin(angles) * scaling)


def apply_left(matrix, target):
    return jnp.einsum("ab,pbc->pac", matrix, target, precision=lax.Precision.HIGHEST)


def apply_right(target, matrix):
    return jnp.einsum("pab,bc->pac", target, matrix, precision=lax.Precision.HIGHEST)


def transform(real_part, imag_part, cosine, sine_table, direction):
    left_real = apply_left(cosine, real_part) + direction * apply_left(sine_table, imag_part)
    left_imag = apply_left(cosine, imag_part) - direction * apply_left(sine_table, real_part)
    out_real = apply_right(left_real, cosine) + direction * apply_right(left_imag, sine_table)
    out_imag = apply_right(left_imag, cosine) - direction * apply_right(left_real, sine_table)
    return (out_real, out_imag)


def place_add(target, placed, row_start, col_start):
    zero_index = jnp.int32(0)
    current = lax.dynamic_slice(target, (zero_index, row_start, col_start), placed.shape)
    return lax.dynamic_update_slice(target, current + placed, (zero_index, row_start, col_start))


def shards_by_mode(object_field, probe, positions, measured):
    strip_rows = object_field.shape[1]
    object_width = object_field.shape[2]
    pattern = probe.shape[2]
    half_pattern = pattern // 2
    count = positions.shape[1]
    cosine, sine_table = tables(pattern)
    tile_index = lax.axis_index("tile")
    offset = tile_index * strip_rows - half_pattern
    for minibatch in range(measured.shape[0]):
        extended = padded(object_field, (("tile", 1),), half_pattern)
        row_offsets = positions[minibatch, :, 0] - offset
        column_offsets = positions[minibatch, :, 1]

        def cut_one(row_start, col_start):
            return lax.dynamic_slice(
                extended, (jnp.int32(0), row_start, col_start), (2, pattern, pattern)
            )

        patches = jax.vmap(cut_one)(row_offsets, column_offsets)
        obj_real = patches[:, 0]
        obj_imag = patches[:, 1]
        probe_real = probe[0, 0]
        probe_imag = probe[0, 1]
        exit_real = probe_real * obj_real - probe_imag * obj_imag
        exit_imag = probe_real * obj_imag + probe_imag * obj_real
        far_real, far_imag = transform(exit_real, exit_imag, cosine, sine_table, 1.0)
        observed = measured[minibatch]
        intensity = lax.psum(far_real * far_real + far_imag * far_imag, "mode")
        modulus = jnp.sqrt((observed + 1.0) / (intensity + 1.0)) - 1.0
        chi_real, chi_imag = transform(
            modulus * far_real, modulus * far_imag, cosine, sine_table, -1.0
        )
        grad_real = probe_real * chi_real + probe_imag * chi_imag
        grad_imag = probe_real * chi_imag - probe_imag * chi_real
        probe_power = probe_real * probe_real + probe_imag * probe_imag
        step_real = jnp.sum(obj_real * chi_real + obj_imag * chi_imag, axis=0)
        step_imag = jnp.sum(obj_real * chi_imag - obj_imag * chi_real, axis=0)
        coverage = jnp.sum(obj_real * obj_real + obj_imag * obj_imag, axis=0)
        accumulated = jnp.zeros((3, strip_rows + pattern, object_width), jnp.float32)
        for position in range(count):
            placed = jnp.stack([grad_real[position], grad_imag[position], probe_power])
            accumulated = place_add(
                accumulated, placed, row_offsets[position], column_offsets[position]
            )
        rim_rows = jnp.concatenate(
            [accumulated[:, :half_pattern], accumulated[:, strip_rows + half_pattern :]], axis=1
        )
        received = padded(rim_rows, (("tile", 1),), half_pattern)
        own_strip = accumulated[:, half_pattern : half_pattern + strip_rows]
        own_strip = own_strip.at[:, :half_pattern].add(received[:, :half_pattern])
        own_strip = own_strip.at[:, strip_rows - half_pattern :].add(
            received[:, pattern + half_pattern :]
        )
        summed = lax.psum(own_strip, "mode")
        divisor = summed[2] + 1.0
        object_field = jnp.stack(
            [object_field[0] + summed[0] / divisor, object_field[1] + summed[1] / divisor]
        )
        step_stack = jnp.stack([jnp.stack([step_real, step_imag])])
        step_total, coverage_total = lax.psum((step_stack, coverage), "tile")
        probe = probe + step_total / (coverage_total + 1.0)
    return (object_field, probe)


def table_of(length):
    index_values = np.arange(length)
    angles = (index_values[:, None] * index_values[None, :] % length) * (2.0 * np.pi / length)
    scaling = 1.0 / np.sqrt(length)
    return np.stack([np.cos(angles) * scaling, np.sin(angles) * scaling]).astype(np.float32)


def spot(info, size, minibatch, side, slot):
    tiles, strip, pattern = size
    place = (((side + 1) * 2 + minibatch) * 2 + slot) * 2
    tile = info[24]
    row = info[place] - tile * strip + pattern // 2
    if side < 0:
        row = jnp.where(tile == 0, -pattern, row)
    if side > 0:
        row = jnp.where(tile == tiles - 1, strip + pattern, row)
    return row, info[place + 1]


def part_of(ref, part):
    if len(ref.shape) == 3:
        return ref[part]
    return ref[:, part].reshape(ref.shape[0] * ref.shape[2], ref.shape[3])


def take_columns(block, column, width):
    total = block.shape[-1]
    return pltpu.roll(block, lax.rem(total - column, total), 1)[:, :width]


def add_at(tall, block, row, column):
    rows, width = block.shape
    total = tall.shape[1]
    shift = lax.rem(row, 8)
    start = pl.multiple_of(row - shift, 8)
    turned = pltpu.roll(block.reshape(rows // 8, 8, width), shift, 1)
    empty = jnp.zeros((1, 8, width), block.dtype)
    inside = lax.broadcasted_iota(jnp.int32, (rows // 8 + 1, 8, width), 1) >= shift
    moved = jnp.where(
        inside,
        jnp.concatenate([turned, empty], axis=0),
        jnp.concatenate([empty, turned], axis=0),
    ).reshape(rows + 8, width)
    wide = jnp.concatenate([moved, jnp.zeros((rows + 8, total - width), block.dtype)], axis=1)
    tall[pl.ds(start, rows + 8), :] += pltpu.roll(wide, column, 1)


def rows_at(ref, row, rows):
    width = ref.shape[1]
    shift = lax.rem(row, 8)
    start = pl.multiple_of(row - shift, 8)
    block = ref[pl.ds(start, rows + 8), :].reshape(rows // 8 + 1, 8, width)
    turned = pltpu.roll(block, lax.rem(8 - shift, 8), 1)
    inside = lax.broadcasted_iota(jnp.int32, (rows // 8, 8, width), 1) < 8 - shift
    return jnp.where(inside, turned[:-1], turned[1:]).reshape(rows, width)


def halves(value):
    high = value.astype(BF16)
    return high, (value - high.astype(F32)).astype(BF16)


def product(left, right):
    dot = functools.partial(jnp.dot, preferred_element_type=F32)
    return dot(left[0], right[0]) + (dot(left[0], right[1]) + dot(left[1], right[0]))


def cut_patch(size, info, minibatch, strip_ref, below, above, window, part):
    tiles, rows, width = size
    half = width // 2
    row, column = spot(info, size, minibatch, 0, info[25])

    def columns(block):
        return block if block.shape[1] == width else take_columns(block, column, width)

    window[:half] = columns(below)
    window[half : half + rows] = columns(strip_ref[part])
    window[half + rows : rows + width] = columns(above)
    return rows_at(window, row, width)


def illumination_kernel(size, minibatch, info, own, other, out, tall):
    tiles, strip, pattern = size
    half = pattern // 2
    kept = slice(pattern + half, pattern + half + strip)
    tall[kept] = jnp.zeros((strip, tall.shape[1]), F32)
    (pr0, pi0), (pr1, pi1) = ((part_of(ref, 0), part_of(ref, 1)) for ref in (own, other))
    power = pr0 * pr0 + pi0 * pi0 + (pr1 * pr1 + pi1 * pi1)
    for side in (-1, 0, 1):
        for slot in range(2):
            row, column = spot(info, size, minibatch, side, slot)
            add_at(tall, power, row + pattern, column)
    out[...] = tall[kept]


def patch_kernel(size, minibatch, info, strip_ref, *refs):
    edges, (patch, coverage, window) = refs[:-3], refs[-3:]
    tiles, strip, pattern = size

    def edge(side, part):
        if len(edges) == 2:
            return edges[side][part]
        return jnp.where(info[25] == part, edges[2 * side][...], edges[2 * side + 1][...])

    for part in range(2):
        value = cut_patch(
            size, info, minibatch, strip_ref, edge(0, part), edge(1, part), window, part
        )
        patch[part] = value
    power = patch[0] * patch[0] + patch[1] * patch[1]
    coverage[...] = power.reshape(coverage.shape)


def field_kernel(size, minibatch, info, patch, own, other, measured, table, *refs):
    gradient, step_own, step_other, observed, arrived = refs
    tiles, strip, pattern = size
    slot = info[25]
    fetch = pltpu.make_async_copy(measured.at[minibatch, slot], observed, arrived)
    fetch.start()
    (cos_high, cos_low), (sin_high, sin_low) = halves(table[0]), halves(table[1])

    def block(top_left, top_right, low_left, low_right):
        return jnp.concatenate(
            [
                jnp.concatenate([top_left, top_right], axis=1),
                jnp.concatenate([low_left, low_right], axis=1),
            ],
            axis=0,
        )

    first = (
        block(cos_high, sin_high, -sin_high, cos_high),
        block(cos_low, sin_low, -sin_low, cos_low),
    )
    second = (
        block(cos_high, -sin_high, sin_high, cos_high),
        block(cos_low, -sin_low, sin_low, cos_low),
    )
    obj_real, obj_imag = patch[0], patch[1]
    probes = [(part_of(ref, 0), part_of(ref, 1)) for ref in (own, other)]

    def both(fields, left, right):
        (r0, i0), (r1, i1) = fields
        y = product(left, halves(block(r0, r1, i0, i1)))
        y = block(
            y[:pattern, :pattern], y[pattern:, :pattern], y[:pattern, pattern:], y[pattern:, pattern:]
        )
        y = product(halves(y), right)
        return (
            (y[:pattern, :pattern], y[:pattern, pattern:]),
            (y[pattern:, :pattern], y[pattern:, pattern:]),
        )

    exits = [(pr * obj_real - pi * obj_imag, pr * obj_imag + pi * obj_real) for pr, pi in probes]
    far = both(exits, first, second)
    intensity = (far[0][0] * far[0][0] + far[0][1] * far[0][1]) + (
        far[1][0] * far[1][0] + far[1][1] * far[1][1]
    )
    fetch.wait()
    factor = jnp.sqrt((observed[...] + 1.0) / (intensity + 1.0)) - 1.0
    chi = both([(factor * fr, factor * fi) for fr, fi in far], second, first)
    (pr0, pi0), (pr1, pi1) = probes
    (cr0, ci0), (cr1, ci1) = chi
    gradient[0] = (pr0 * cr0 + pi0 * ci0) + (pr1 * cr1 + pi1 * ci1)
    gradient[1] = (pr0 * ci0 - pi0 * cr0) + (pr1 * ci1 - pi1 * cr1)
    rows = pattern // tiles
    for step, (cr, ci) in ((step_own, chi[0]), (step_other, chi[1])):
        for part, value in (
            (0, obj_real * cr + obj_imag * ci),
            (1, obj_real * ci - obj_imag * cr),
        ):
            step[:, part] = value.reshape(tiles, rows, pattern)


def update_kernel(size, minibatch, info, strip_ref, illum, own, other, b0, a0, b1, a1, *outs):
    strip_out, *edges, tall = outs
    tiles, strip, pattern = size
    half = pattern // 2
    slot = info[25]
    kept = slice(pattern + half, pattern + half + strip)
    grads = (
        (0, slot, own, 0),
        (0, 1 - slot, other, 0),
        (-1, slot, b0, half),
        (1, slot, a0, 0),
        (-1, 1 - slot, b1, half),
        (1, 1 - slot, a1, 0),
    )
    for part in range(2):
        tall[kept] = jnp.zeros((strip, tall.shape[1]), F32)
        for side, place, ref, start in grads:
            row, column = spot(info, size, minibatch, side, place)
            add_at(tall, ref[part], row + pattern + start, column)
        fresh = strip_ref[part] + tall[kept] / (illum[...] + 1.0)
        strip_out[part] = fresh
        if edges:
            column_below = spot(info, size, minibatch + 1, -1, slot)[1]
            column_above = spot(info, size, minibatch + 1, 1, slot)[1]
            edges[0][part] = take_columns(fresh[:half], column_below, pattern)
            edges[1][part] = take_columns(fresh[strip - half :], column_above, pattern)


def total_of(sums):
    total = sums[0]
    for k in range(1, sums.shape[0]):
        total += sums[k]
    return total


def sum_kernel(info, sums, out):
    out[...] = total_of(sums)


def piece_kernel(info, sums, coverage, coverage_other, probe, out):
    tiles, parts, rows, width = sums.shape
    tile = info[24]
    total = total_of(sums)
    divisor = coverage[...] + coverage_other[...] + 1.0
    for part in range(2):
        if len(probe.shape) == 3:
            held = probe[part, pl.ds(pl.multiple_of(tile * rows, rows), rows), :]
        else:
            held = probe[tile, part]
        fresh = held + total[part] / divisor
        for k in range(tiles):
            out[k, part] = fresh


def gather_kernel(info, blocks, out):
    for part in range(2):
        out[part] = part_of(blocks, part)


def call(kernel, name, outs, inputs, scratch=(), flops=0, far=None):
    shapes = [jax.ShapeDtypeStruct(shape, F32) for shape in outs]
    size = 4 * sum(math.prod(shape) for shape in outs) + sum(
        value.size * value.dtype.itemsize for value in inputs
    )
    smem = pl.BlockSpec(memory_space=pltpu.SMEM)
    vmem = pl.BlockSpec(memory_space=pltpu.VMEM)
    return pl.pallas_call(
        kernel,
        out_shape=shapes,
        in_specs=[smem]
        + [pl.BlockSpec(memory_space=pl.ANY) if value is far else vmem for value in inputs[1:]],
        out_specs=[vmem] * len(shapes),
        scratch_shapes=[pltpu.VMEM(shape, F32) for shape in scratch]
        + ([] if far is None else [pltpu.SemaphoreType.DMA]),
        compiler_params=pltpu.CompilerParams(vmem_limit_bytes=VMEM_BYTES),
        cost_estimate=pl.CostEstimate(flops=flops, bytes_accessed=size, transcendentals=0),
        name=name,
    )(*inputs)


def shards_by_position(object_field, probe, positions, measured):
    strip = object_field.shape[1]
    width = object_field.shape[2]
    pattern = probe.shape[2]
    half = pattern // 2
    tiles = lax.axis_size("tile")
    size = (tiles, strip, pattern)
    field = (2, pattern, pattern)
    tall = (3 * pattern + strip + 8, width)
    window = (pattern + strip + 8, pattern)
    up = [(i, i + 1) for i in range(tiles - 1)]
    down = [(i + 1, i) for i in range(tiles - 1)]

    def swap(value):
        return lax.ppermute(value, "mode", [(0, 1), (1, 0)])

    def to_all(blocks):
        return lax.all_to_all(blocks, "tile", 0, 0, tiled=True)

    def from_below(value):
        return lax.ppermute(value, "tile", up)

    def from_above(value):
        return lax.ppermute(value, "tile", down)

    def bind(kernel, *args):
        return functools.partial(kernel, *args)

    table = jnp.asarray(table_of(pattern))
    tile, slot = lax.axis_index("tile"), lax.axis_index("mode")
    one_part = lax.dynamic_index_in_dim(object_field, slot, 0, keepdims=False)
    edges = [from_below(one_part[strip - half :]), from_above(one_part[:half])]
    below, above = from_below(positions), from_above(positions)
    *edges, below, above = lax.optimization_barrier((*edges, below, above))
    edges = [edges[0], swap(edges[0]), edges[1], swap(edges[1])]
    index = jnp.stack([tile, slot]).astype(jnp.int32)
    here = jnp.concatenate([positions.ravel()] * 3 + [index])
    info = jnp.concatenate([below.ravel(), positions.ravel(), above.ravel(), index])
    own = probe[0]
    other = swap(own)

    for minibatch in range(2):
        rows = pattern // tiles
        patch, coverage = call(
            bind(patch_kernel, size, minibatch),
            "patch",
            [field, (tiles, rows, pattern)],
            (here, object_field, *edges),
            [window],
        )
        (coverage,) = call(sum_kernel, "coverage", [(rows, pattern)], (here, to_all(coverage)))
        coverage_other = swap(coverage)
        blocks = (tiles, 2, rows, pattern)
        gradient, step_own, step_other = call(
            bind(field_kernel, size, minibatch),
            "field",
            [field, blocks, blocks],
            (here, patch, own, other, measured, table),
            [(pattern, pattern)],
            flops=2 * 12 * 512**3,
            far=measured,
        )
        (illum,) = call(
            bind(illumination_kernel, size, minibatch),
            "illumination",
            [(strip, width)],
            (info, own, other),
            [tall],
        )
        rim_below, rim_above = from_below(gradient[:, half:]), from_above(gradient[:, :half])
        sums = to_all(step_own + swap(step_other))
        sums, rim_below, rim_above = lax.optimization_barrier((sums, rim_below, rim_above))
        rims = (gradient, swap(gradient), rim_below, rim_above, swap(rim_below), swap(rim_above))
        last = minibatch == 1
        object_field, *edges = call(
            bind(update_kernel, size, minibatch),
            "update",
            [object_field.shape] + ([] if last else [(2, half, pattern)] * 2),
            (info, object_field, illum, *rims),
            [tall],
        )
        if not last:
            edges = [from_below(edges[1]), from_above(edges[0])]

        (fresh,) = call(
            piece_kernel, "piece", [blocks], (here, sums, coverage, coverage_other, own)
        )
        own = to_all(fresh)
        if not last:
            other = swap(own)
    (own,) = call(gather_kernel, "gather", [field], (here, own))
    return (object_field, own[None])


def solution(mesh):
    in_specs = (
        P(None, "tile", None),
        P("mode", None, None, None),
        P(None, "tile", None),
        P(None, "tile", None, None),
    )
    out_specs = (P(None, "tile", None), P("mode", None, None, None))

    def whole(object_field, probe, positions, measured):
        tiles, pair = mesh.shape["tile"], mesh.shape["mode"]
        by_position = (
            pair == 2
            and probe.shape[0] == 2
            and positions.shape[:2] == (2, 2 * tiles)
            and probe.shape[2] % (8 * tiles) == 0
            and object_field.shape[1] == tiles * probe.shape[2]
        )
        shards = shards_by_position if by_position else shards_by_mode
        return jax.shard_map(
            shards, mesh=mesh, in_specs=in_specs, out_specs=out_specs, check_vma=False
        )(object_field, probe, positions, measured)

    return whole
```

```python
import functools
import math

import jax
import jax.numpy as jnp
import numpy as np
from jax import lax
from jax.experimental import pallas as pl
from jax.experimental.pallas import tpu as pltpu
from jax.sharding import PartitionSpec as P

F32 = jnp.float32
BF16 = jnp.bfloat16
VMEM_BYTES = 40 * 1024 * 1024
GROUP = 4


def padded(block, sides, width):
    for axis, dim in sides:
        count = lax.axis_size(axis)
        forward = [(i, i + 1) for i in range(count - 1)]
        backward = [(target, source) for source, target in forward]
        low = lax.ppermute(
            lax.slice_in_dim(block, block.shape[dim] - width, None, axis=dim), axis, forward
        )
        high = lax.ppermute(lax.slice_in_dim(block, 0, width, axis=dim), axis, backward)
        block = jnp.concatenate([low, block, high], axis=dim)
    return block


def tables(length):
    index_values = jnp.arange(length, dtype=jnp.int32)
    product = index_values[:, None] * index_values[None, :] % length
    angles = product.astype(jnp.float32) * (2.0 * math.pi / length)
    scaling = 1.0 / math.sqrt(length)
    return (jnp.cos(angles) * scaling, jnp.sin(angles) * scaling)


def apply_left(matrix, target):
    return jnp.einsum("ab,pbc->pac", matrix, target, precision=lax.Precision.HIGHEST)


def apply_right(target, matrix):
    return jnp.einsum("pab,bc->pac", target, matrix, precision=lax.Precision.HIGHEST)


def transform(real_part, imag_part, cosine, sine_table, direction):
    left_real = apply_left(cosine, real_part) + direction * apply_left(sine_table, imag_part)
    left_imag = apply_left(cosine, imag_part) - direction * apply_left(sine_table, real_part)
    out_real = apply_right(left_real, cosine) + direction * apply_right(left_imag, sine_table)
    out_imag = apply_right(left_imag, cosine) - direction * apply_right(left_real, sine_table)
    return (out_real, out_imag)


def place_add(target, placed, row_start, col_start):
    zero_index = jnp.int32(0)
    current = lax.dynamic_slice(target, (zero_index, row_start, col_start), placed.shape)
    return lax.dynamic_update_slice(target, current + placed, (zero_index, row_start, col_start))


def shards_by_mode(object_field, probe, positions, measured):
    strip_rows = object_field.shape[1]
    object_width = object_field.shape[2]
    pattern = probe.shape[2]
    half_pattern = pattern // 2
    count = positions.shape[1]
    cosine, sine_table = tables(pattern)
    tile_index = lax.axis_index("tile")
    offset = tile_index * strip_rows - half_pattern
    for minibatch in range(measured.shape[0]):
        extended = padded(object_field, (("tile", 1),), half_pattern)
        row_offsets = positions[minibatch, :, 0] - offset
        column_offsets = positions[minibatch, :, 1]

        def cut_one(row_start, col_start):
            return lax.dynamic_slice(
                extended, (jnp.int32(0), row_start, col_start), (2, pattern, pattern)
            )

        patches = jax.vmap(cut_one)(row_offsets, column_offsets)
        obj_real = patches[:, 0]
        obj_imag = patches[:, 1]
        probe_real = probe[0, 0]
        probe_imag = probe[0, 1]
        exit_real = probe_real * obj_real - probe_imag * obj_imag
        exit_imag = probe_real * obj_imag + probe_imag * obj_real
        far_real, far_imag = transform(exit_real, exit_imag, cosine, sine_table, 1.0)
        observed = measured[minibatch]
        intensity = lax.psum(far_real * far_real + far_imag * far_imag, "mode")
        modulus = jnp.sqrt((observed + 1.0) / (intensity + 1.0)) - 1.0
        chi_real, chi_imag = transform(
            modulus * far_real, modulus * far_imag, cosine, sine_table, -1.0
        )
        grad_real = probe_real * chi_real + probe_imag * chi_imag
        grad_imag = probe_real * chi_imag - probe_imag * chi_real
        probe_power = probe_real * probe_real + probe_imag * probe_imag
        step_real = jnp.sum(obj_real * chi_real + obj_imag * chi_imag, axis=0)
        step_imag = jnp.sum(obj_real * chi_imag - obj_imag * chi_real, axis=0)
        coverage = jnp.sum(obj_real * obj_real + obj_imag * obj_imag, axis=0)
        accumulated = jnp.zeros((3, strip_rows + pattern, object_width), jnp.float32)
        for position in range(count):
            placed = jnp.stack([grad_real[position], grad_imag[position], probe_power])
            accumulated = place_add(
                accumulated, placed, row_offsets[position], column_offsets[position]
            )
        rim_rows = jnp.concatenate(
            [accumulated[:, :half_pattern], accumulated[:, strip_rows + half_pattern :]], axis=1
        )
        received = padded(rim_rows, (("tile", 1),), half_pattern)
        own_strip = accumulated[:, half_pattern : half_pattern + strip_rows]
        own_strip = own_strip.at[:, :half_pattern].add(received[:, :half_pattern])
        own_strip = own_strip.at[:, strip_rows - half_pattern :].add(
            received[:, pattern + half_pattern :]
        )
        summed = lax.psum(own_strip, "mode")
        divisor = summed[2] + 1.0
        object_field = jnp.stack(
            [object_field[0] + summed[0] / divisor, object_field[1] + summed[1] / divisor]
        )
        step_stack = jnp.stack([jnp.stack([step_real, step_imag])])
        step_total, coverage_total = lax.psum((step_stack, coverage), "tile")
        probe = probe + step_total / (coverage_total + 1.0)
    return (object_field, probe)


def table_of(length):
    index_values = np.arange(length)
    angles = (index_values[:, None] * index_values[None, :] % length) * (2.0 * np.pi / length)
    scaling = 1.0 / np.sqrt(length)
    return np.stack([np.cos(angles) * scaling, np.sin(angles) * scaling]).astype(np.float32)


def spot(info, size, minibatch, side, slot):
    tiles, strip, pattern = size
    place = (((side + 1) * 2 + minibatch) * 2 + slot) * 2
    tile = info[24]
    row = info[place] - tile * strip + pattern // 2
    if side < 0:
        row = jnp.where(tile == 0, -pattern, row)
    if side > 0:
        row = jnp.where(tile == tiles - 1, strip + pattern, row)
    return row, info[place + 1]


def take_columns(block, column, width):
    total = block.shape[-1]
    return pltpu.roll(block, lax.rem(total - column, total), 1)[:, :width]


def add_at(tall, block, row, column):
    rows, width = block.shape
    total = tall.shape[1]
    shift = lax.rem(row, 8)
    start = pl.multiple_of(row - shift, 8)
    turned = pltpu.roll(block.reshape(rows // 8, 8, width), shift, 1)
    empty = jnp.zeros((1, 8, width), block.dtype)
    inside = lax.broadcasted_iota(jnp.int32, (rows // 8 + 1, 8, width), 1) >= shift
    moved = jnp.where(
        inside,
        jnp.concatenate([turned, empty], axis=0),
        jnp.concatenate([empty, turned], axis=0),
    ).reshape(rows + 8, width)
    wide = jnp.concatenate([moved, jnp.zeros((rows + 8, total - width), block.dtype)], axis=1)
    tall[pl.ds(start, rows + 8), :] += pltpu.roll(wide, column, 1)


def rows_at(ref, row, rows):
    width = ref.shape[1]
    shift = lax.rem(row, 8)
    start = pl.multiple_of(row - shift, 8)
    block = ref[pl.ds(start, rows + 8), :].reshape(rows // 8 + 1, 8, width)
    turned = pltpu.roll(block, lax.rem(8 - shift, 8), 1)
    inside = lax.broadcasted_iota(jnp.int32, (rows // 8, 8, width), 1) < 8 - shift
    return jnp.where(inside, turned[:-1], turned[1:]).reshape(rows, width)


def halves(value):
    high = value.astype(BF16)
    return high, (value - high.astype(F32)).astype(BF16)


def product(left, right):
    dot = functools.partial(jnp.dot, preferred_element_type=F32)
    return dot(left[0], right[0]) + (dot(left[0], right[1]) + dot(left[1], right[0]))


def cut_patch(size, info, minibatch, strip_ref, below, above, window, part):
    tiles, rows, width = size
    half = width // 2
    row, column = spot(info, size, minibatch, 0, info[25])

    def columns(block):
        return block if block.shape[1] == width else take_columns(block, column, width)

    window[:half] = columns(below)
    window[half : half + rows] = columns(strip_ref[part])
    window[half + rows : rows + width] = columns(above)
    return rows_at(window, row, width)


def illumination_kernel(size, minibatch, info, own, other, out, tall):
    tiles, strip, pattern = size
    half = pattern // 2
    kept = slice(pattern + half, pattern + half + strip)
    tall[kept] = jnp.zeros((strip, tall.shape[1]), F32)
    (pr0, pi0), (pr1, pi1) = ((ref[0], ref[1]) for ref in (own, other))
    power = pr0 * pr0 + pi0 * pi0 + (pr1 * pr1 + pi1 * pi1)
    for side in (-1, 0, 1):
        for slot in range(2):
            row, column = spot(info, size, minibatch, side, slot)
            add_at(tall, power, row + pattern, column)
    out[...] = tall[kept]


def field_kernel(size, minibatch, info, strip_ref, *refs):
    edges, (own, other, measured, table) = refs[:-10], refs[-10:-6]
    gradient, step_own, step_other, window, observed, arrived = refs[-6:]
    tiles, strip, pattern = size
    slot = info[25]
    fetch = pltpu.make_async_copy(measured.at[minibatch, slot], observed, arrived)
    fetch.start()
    (cos_high, cos_low), (sin_high, sin_low) = halves(table[0]), halves(table[1])

    def block(top_left, top_right, low_left, low_right):
        return jnp.concatenate(
            [
                jnp.concatenate([top_left, top_right], axis=1),
                jnp.concatenate([low_left, low_right], axis=1),
            ],
            axis=0,
        )

    first = (
        block(cos_high, sin_high, -sin_high, cos_high),
        block(cos_low, sin_low, -sin_low, cos_low),
    )
    second = (
        block(cos_high, -sin_high, sin_high, cos_high),
        block(cos_low, -sin_low, sin_low, cos_low),
    )
    def edge(side, part):
        if len(edges) == 2:
            return edges[side][part]
        return jnp.where(slot == part, edges[2 * side][...], edges[2 * side + 1][...])

    obj_real, obj_imag = (
        cut_patch(size, info, minibatch, strip_ref, edge(0, part), edge(1, part), window, part)
        for part in range(2)
    )
    probes = [(ref[0], ref[1]) for ref in (own, other)]

    def both(fields, left, right):
        (r0, i0), (r1, i1) = fields
        y = product(left, halves(block(r0, r1, i0, i1)))
        y = block(
            y[:pattern, :pattern], y[pattern:, :pattern], y[:pattern, pattern:], y[pattern:, pattern:]
        )
        y = product(halves(y), right)
        return (
            (y[:pattern, :pattern], y[:pattern, pattern:]),
            (y[pattern:, :pattern], y[pattern:, pattern:]),
        )

    exits = [(pr * obj_real - pi * obj_imag, pr * obj_imag + pi * obj_real) for pr, pi in probes]
    far = both(exits, first, second)
    intensity = (far[0][0] * far[0][0] + far[0][1] * far[0][1]) + (
        far[1][0] * far[1][0] + far[1][1] * far[1][1]
    )
    fetch.wait()
    factor = jnp.sqrt((observed[...] + 1.0) / (intensity + 1.0)) - 1.0
    chi = both([(factor * fr, factor * fi) for fr, fi in far], second, first)
    (pr0, pi0), (pr1, pi1) = probes
    (cr0, ci0), (cr1, ci1) = chi
    gradient[0] = (pr0 * cr0 + pi0 * ci0) + (pr1 * cr1 + pi1 * ci1)
    gradient[1] = (pr0 * ci0 - pi0 * cr0) + (pr1 * ci1 - pi1 * cr1)
    coverage = obj_real * obj_real + obj_imag * obj_imag
    rows = pattern // (2 * GROUP)
    for step, keeper, (cr, ci) in ((step_own, slot, chi[0]), (step_other, 1 - slot, chi[1])):
        real = obj_real * cr + obj_imag * ci
        imag = obj_real * ci - obj_imag * cr
        for half, mate in enumerate((lax.rem(info[24], GROUP), lax.div(info[24], GROUP))):
            for k in range(GROUP):
                start = (half * GROUP + k) * rows
                block = step.at[half, mate ^ k]
                block[:rows] = real[start : start + rows]
                block[rows : 2 * rows] = imag[start : start + rows]
                middle = start + rows // 2
                block[2 * rows :] = jnp.where(
                    keeper == 0, coverage[start:middle], coverage[middle : start + rows]
                )


def update_kernel(size, minibatch, info, strip_ref, illum, own, other, b0, a0, b1, a1, *outs):
    strip_out, *edges, tall = outs
    tiles, strip, pattern = size
    half = pattern // 2
    slot = info[25]
    kept = slice(pattern + half, pattern + half + strip)
    grads = (
        (0, slot, own, 0),
        (0, 1 - slot, other, 0),
        (-1, slot, b0, half),
        (1, slot, a0, 0),
        (-1, 1 - slot, b1, half),
        (1, 1 - slot, a1, 0),
    )
    for part in range(2):
        tall[kept] = jnp.zeros((strip, tall.shape[1]), F32)
        for side, place, ref, start in grads:
            row, column = spot(info, size, minibatch, side, place)
            add_at(tall, ref[part], row + pattern + start, column)
        fresh = strip_ref[part] + tall[kept] / (illum[...] + 1.0)
        strip_out[part] = fresh
        if edges:
            column_below = spot(info, size, minibatch + 1, -1, slot)[1]
            column_above = spot(info, size, minibatch + 1, 1, slot)[1]
            edges[0][part] = take_columns(fresh[:half], column_below, pattern)
            edges[1][part] = take_columns(fresh[strip - half :], column_above, pattern)


def probe_kernel(info, own_totals, other_totals, *refs):
    probes, outs = refs[: len(refs) // 2], refs[len(refs) // 2 :]
    slot = info[25]
    rows = outs[0].shape[1] // (2 * GROUP)
    for half, mate in enumerate((lax.rem(info[24], GROUP), lax.div(info[24], GROUP))):
        for k in range(GROUP):
            start = half * GROUP * rows + pl.multiple_of((mate ^ k) * rows, rows)
            where = pl.ds(start, rows)
            mine, theirs = own_totals[half, k], other_totals[half, k]
            own_half, other_half = mine[2 * rows :], theirs[theirs.shape[0] - rows // 2 :]
            coverage = jnp.concatenate(
                [
                    jnp.where(slot == 0, own_half, other_half),
                    jnp.where(slot == 0, other_half, own_half),
                ],
                axis=0,
            )
            divisor = coverage + 1.0
            for totals, probe, out in zip((mine, theirs), probes, outs):
                for part in range(2):
                    change = totals[part * rows : (part + 1) * rows] / divisor
                    out[part, where, :] = probe[part, where, :] + change


def call(kernel, name, outs, inputs, scratch=(), flops=0, far=None):
    shapes = [jax.ShapeDtypeStruct(shape, F32) for shape in outs]
    size = 4 * sum(math.prod(shape) for shape in outs) + sum(
        value.size * value.dtype.itemsize for value in inputs
    )
    smem = pl.BlockSpec(memory_space=pltpu.SMEM)
    vmem = pl.BlockSpec(memory_space=pltpu.VMEM)
    return pl.pallas_call(
        kernel,
        out_shape=shapes,
        in_specs=[smem]
        + [pl.BlockSpec(memory_space=pl.ANY) if value is far else vmem for value in inputs[1:]],
        out_specs=[vmem] * len(shapes),
        scratch_shapes=[pltpu.VMEM(shape, F32) for shape in scratch]
        + ([] if far is None else [pltpu.SemaphoreType.DMA]),
        compiler_params=pltpu.CompilerParams(vmem_limit_bytes=VMEM_BYTES),
        cost_estimate=pl.CostEstimate(flops=flops, bytes_accessed=size, transcendentals=0),
        name=name,
    )(*inputs)


def shards_by_position(object_field, probe, positions, measured):
    strip = object_field.shape[1]
    width = object_field.shape[2]
    pattern = probe.shape[2]
    half = pattern // 2
    tiles = lax.axis_size("tile")
    size = (tiles, strip, pattern)
    field = (2, pattern, pattern)
    tall = (3 * pattern + strip + 8, width)
    window = (pattern + strip + 8, pattern)
    up = [(i, i + 1) for i in range(tiles - 1)]
    down = [(i + 1, i) for i in range(tiles - 1)]

    def swap(value):
        return lax.ppermute(value, "mode", [(0, 1), (1, 0)])

    def across(value, k):
        return lax.ppermute(value, "tile", [(i, i ^ k) for i in range(tiles)])

    def scatter(blocks, unit):
        mates = [across(blocks[k], unit * k) for k in range(1, GROUP)]
        return functools.reduce(jnp.add, mates, blocks[0])

    def exchange(piece, unit):
        mates = [across(piece, unit * k) for k in range(1, GROUP)]
        return functools.reduce(jnp.add, mates, piece)

    def gather(piece, unit):
        return jnp.stack([piece] + [across(piece, unit * k) for k in range(1, GROUP)])

    def from_below(value):
        return lax.ppermute(value, "tile", up)

    def from_above(value):
        return lax.ppermute(value, "tile", down)

    def bind(kernel, *args):
        return functools.partial(kernel, *args)

    table = jnp.asarray(table_of(pattern))
    tile, slot = lax.axis_index("tile"), lax.axis_index("mode")
    one_part = lax.dynamic_index_in_dim(object_field, slot, 0, keepdims=False)
    edges = [from_below(one_part[strip - half :]), from_above(one_part[:half])]
    below, above = from_below(positions), from_above(positions)
    *edges, below, above = lax.optimization_barrier((*edges, below, above))
    edges = [edges[0], swap(edges[0]), edges[1], swap(edges[1])]
    index = jnp.stack([tile, slot]).astype(jnp.int32)
    here = jnp.concatenate([positions.ravel()] * 3 + [index])
    info = jnp.concatenate([below.ravel(), positions.ravel(), above.ravel(), index])
    own = probe[0]
    other = swap(own)

    for minibatch in range(2):
        last = minibatch == 1
        rows = pattern // (2 * GROUP)
        blocks = (2, GROUP, 2 * rows + rows // 2, pattern)
        gradient, step_own, step_other = call(
            bind(field_kernel, size, minibatch),
            "field",
            [field, blocks, blocks],
            (here, object_field, *edges, own, other, measured, table),
            [window, (pattern, pattern)],
            flops=2 * 12 * 512**3,
            far=measured,
        )
        (illum,) = call(
            bind(illumination_kernel, size, minibatch),
            "illumination",
            [(strip, width)],
            (info, own, other),
            [tall],
        )
        steps = step_own + swap(step_other)
        plane_piece, line_piece = scatter(steps[0], 1), scatter(steps[1], GROUP)
        source = gradient
        if last:
            source, plane_piece, line_piece = lax.optimization_barrier(
                (source, plane_piece, line_piece)
            )
        rim_below, rim_above = from_below(source[:, half:]), from_above(source[:, :half])
        if not last:
            rim_below, rim_above, plane_piece, line_piece = lax.optimization_barrier(
                (rim_below, rim_above, plane_piece, line_piece)
            )
        rims = (gradient, swap(gradient), rim_below, rim_above, swap(rim_below), swap(rim_above))
        object_field, *edges = call(
            bind(update_kernel, size, minibatch),
            "update",
            [object_field.shape] + ([] if last else [(2, half, pattern)] * 2),
            (info, object_field, illum, *rims),
            [tall],
        )
        plane_piece, line_piece = exchange(plane_piece, GROUP), exchange(line_piece, 1)
        if not last:
            object_field, *edges, plane_piece, line_piece = lax.optimization_barrier(
                (object_field, *edges, plane_piece, line_piece)
            )
            edges = [from_below(edges[1]), from_above(edges[0])]
        totals = jnp.stack([gather(plane_piece, 1), gather(line_piece, GROUP)])
        if last:
            others = swap(totals[:, :, 2 * rows :])
            (own,) = call(probe_kernel, "probe", [field], (here, totals, others, own))
        else:
            totals, *edges = lax.optimization_barrier((totals, *edges))
            own, other = call(
                probe_kernel, "probe", [field] * 2, (here, totals, swap(totals), own, other)
            )
    return (object_field, own[None])


def solution(mesh):
    in_specs = (
        P(None, "tile", None),
        P("mode", None, None, None),
        P(None, "tile", None),
        P(None, "tile", None, None),
    )
    out_specs = (P(None, "tile", None), P("mode", None, None, None))

    def whole(object_field, probe, positions, measured):
        tiles, pair = mesh.shape["tile"], mesh.shape["mode"]
        by_position = (
            pair == 2
            and probe.shape[0] == 2
            and positions.shape[:2] == (2, 2 * tiles)
            and tiles == GROUP * GROUP
            and probe.shape[2] % (16 * 2 * GROUP) == 0
            and object_field.shape[1] == tiles * probe.shape[2]
        )
        shards = shards_by_position if by_position else shards_by_mode
        return jax.shard_map(
            shards, mesh=mesh, in_specs=in_specs, out_specs=out_specs, check_vma=False
        )(object_field, probe, positions, measured)

    return whole
```

```python
import functools
import math

import jax
import jax.numpy as jnp
import numpy as np
from jax import lax
from jax.experimental import pallas as pl
from jax.experimental.pallas import tpu as pltpu
from jax.sharding import PartitionSpec as P

F32 = jnp.float32
BF16 = jnp.bfloat16
VMEM_BYTES = 16 * 1024 * 1024
GROUP = 4


def padded(block, sides, width):
    for axis, dim in sides:
        count = lax.axis_size(axis)
        forward = [(i, i + 1) for i in range(count - 1)]
        backward = [(target, source) for source, target in forward]
        low = lax.ppermute(
            lax.slice_in_dim(block, block.shape[dim] - width, None, axis=dim), axis, forward
        )
        high = lax.ppermute(lax.slice_in_dim(block, 0, width, axis=dim), axis, backward)
        block = jnp.concatenate([low, block, high], axis=dim)
    return block


def tables(length):
    index_values = jnp.arange(length, dtype=jnp.int32)
    product = index_values[:, None] * index_values[None, :] % length
    angles = product.astype(jnp.float32) * (2.0 * math.pi / length)
    scaling = 1.0 / math.sqrt(length)
    return (jnp.cos(angles) * scaling, jnp.sin(angles) * scaling)


def apply_left(matrix, target):
    return jnp.einsum("ab,pbc->pac", matrix, target, precision=lax.Precision.HIGHEST)


def apply_right(target, matrix):
    return jnp.einsum("pab,bc->pac", target, matrix, precision=lax.Precision.HIGHEST)


def transform(real_part, imag_part, cosine, sine_table, direction):
    left_real = apply_left(cosine, real_part) + direction * apply_left(sine_table, imag_part)
    left_imag = apply_left(cosine, imag_part) - direction * apply_left(sine_table, real_part)
    out_real = apply_right(left_real, cosine) + direction * apply_right(left_imag, sine_table)
    out_imag = apply_right(left_imag, cosine) - direction * apply_right(left_real, sine_table)
    return (out_real, out_imag)


def place_add(target, placed, row_start, col_start):
    zero_index = jnp.int32(0)
    current = lax.dynamic_slice(target, (zero_index, row_start, col_start), placed.shape)
    return lax.dynamic_update_slice(target, current + placed, (zero_index, row_start, col_start))


def shards_by_mode(object_field, probe, positions, measured):
    strip_rows = object_field.shape[1]
    object_width = object_field.shape[2]
    pattern = probe.shape[2]
    half_pattern = pattern // 2
    count = positions.shape[1]
    cosine, sine_table = tables(pattern)
    tile_index = lax.axis_index("tile")
    offset = tile_index * strip_rows - half_pattern
    for minibatch in range(measured.shape[0]):
        extended = padded(object_field, (("tile", 1),), half_pattern)
        row_offsets = positions[minibatch, :, 0] - offset
        column_offsets = positions[minibatch, :, 1]

        def cut_one(row_start, col_start):
            return lax.dynamic_slice(
                extended, (jnp.int32(0), row_start, col_start), (2, pattern, pattern)
            )

        patches = jax.vmap(cut_one)(row_offsets, column_offsets)
        obj_real = patches[:, 0]
        obj_imag = patches[:, 1]
        probe_real = probe[0, 0]
        probe_imag = probe[0, 1]
        exit_real = probe_real * obj_real - probe_imag * obj_imag
        exit_imag = probe_real * obj_imag + probe_imag * obj_real
        far_real, far_imag = transform(exit_real, exit_imag, cosine, sine_table, 1.0)
        observed = measured[minibatch]
        intensity = lax.psum(far_real * far_real + far_imag * far_imag, "mode")
        modulus = jnp.sqrt((observed + 1.0) / (intensity + 1.0)) - 1.0
        chi_real, chi_imag = transform(
            modulus * far_real, modulus * far_imag, cosine, sine_table, -1.0
        )
        grad_real = probe_real * chi_real + probe_imag * chi_imag
        grad_imag = probe_real * chi_imag - probe_imag * chi_real
        probe_power = probe_real * probe_real + probe_imag * probe_imag
        step_real = jnp.sum(obj_real * chi_real + obj_imag * chi_imag, axis=0)
        step_imag = jnp.sum(obj_real * chi_imag - obj_imag * chi_real, axis=0)
        coverage = jnp.sum(obj_real * obj_real + obj_imag * obj_imag, axis=0)
        accumulated = jnp.zeros((3, strip_rows + pattern, object_width), jnp.float32)
        for position in range(count):
            placed = jnp.stack([grad_real[position], grad_imag[position], probe_power])
            accumulated = place_add(
                accumulated, placed, row_offsets[position], column_offsets[position]
            )
        rim_rows = jnp.concatenate(
            [accumulated[:, :half_pattern], accumulated[:, strip_rows + half_pattern :]], axis=1
        )
        received = padded(rim_rows, (("tile", 1),), half_pattern)
        own_strip = accumulated[:, half_pattern : half_pattern + strip_rows]
        own_strip = own_strip.at[:, :half_pattern].add(received[:, :half_pattern])
        own_strip = own_strip.at[:, strip_rows - half_pattern :].add(
            received[:, pattern + half_pattern :]
        )
        summed = lax.psum(own_strip, "mode")
        divisor = summed[2] + 1.0
        object_field = jnp.stack(
            [object_field[0] + summed[0] / divisor, object_field[1] + summed[1] / divisor]
        )
        step_stack = jnp.stack([jnp.stack([step_real, step_imag])])
        step_total, coverage_total = lax.psum((step_stack, coverage), "tile")
        probe = probe + step_total / (coverage_total + 1.0)
    return (object_field, probe)


def table_of(length):
    index_values = np.arange(length)
    angles = (index_values[:, None] * index_values[None, :] % length) * (2.0 * np.pi / length)
    scaling = 1.0 / np.sqrt(length)
    return np.stack([np.cos(angles) * scaling, np.sin(angles) * scaling]).astype(np.float32)


def spot(info, size, minibatch, side, slot):
    tiles, strip, pattern = size
    place = (((side + 1) * 2 + minibatch) * 2 + slot) * 2
    tile = info[24]
    row = info[place] - tile * strip + pattern // 2
    if side < 0:
        row = jnp.where(tile == 0, -pattern, row)
    if side > 0:
        row = jnp.where(tile == tiles - 1, strip + pattern, row)
    return row, info[place + 1]


def take_columns(block, column, width):
    total = block.shape[-1]
    return pltpu.roll(block, lax.rem(total - column, total), 1)[:, :width]


def add_at(tall, block, row, column):
    rows, width = block.shape
    total = tall.shape[1]
    shift = lax.rem(row, 8)
    start = pl.multiple_of(row - shift, 8)
    turned = pltpu.roll(block.reshape(rows // 8, 8, width), shift, 1)
    empty = jnp.zeros((1, 8, width), block.dtype)
    inside = lax.broadcasted_iota(jnp.int32, (rows // 8 + 1, 8, width), 1) >= shift
    moved = jnp.where(
        inside,
        jnp.concatenate([turned, empty], axis=0),
        jnp.concatenate([empty, turned], axis=0),
    ).reshape(rows + 8, width)
    wide = jnp.concatenate([moved, jnp.zeros((rows + 8, total - width), block.dtype)], axis=1)
    tall[pl.ds(start, rows + 8), :] += pltpu.roll(wide, column, 1)


def rows_at(ref, row, rows):
    width = ref.shape[1]
    shift = lax.rem(row, 8)
    start = pl.multiple_of(row - shift, 8)
    block = ref[pl.ds(start, rows + 8), :].reshape(rows // 8 + 1, 8, width)
    turned = pltpu.roll(block, lax.rem(8 - shift, 8), 1)
    inside = lax.broadcasted_iota(jnp.int32, (rows // 8, 8, width), 1) < 8 - shift
    return jnp.where(inside, turned[:-1], turned[1:]).reshape(rows, width)


def halves(value):
    high = value.astype(BF16)
    return high, (value - high.astype(F32)).astype(BF16)


def product(left, right):
    dot = functools.partial(jnp.dot, preferred_element_type=F32)
    return dot(left[0], right[0]) + (dot(left[0], right[1]) + dot(left[1], right[0]))


def cut_patch(size, info, minibatch, strip_ref, below, above, window, part):
    tiles, rows, width = size
    half = width // 2
    row, column = spot(info, size, minibatch, 0, info[25])

    def columns(block):
        return block if block.shape[1] == width else take_columns(block, column, width)

    window[:half] = columns(below)
    window[half : half + rows] = columns(strip_ref[part])
    window[half + rows : rows + width] = columns(above)
    return rows_at(window, row, width)


def illumination_kernel(size, minibatch, info, own, other, out, tall):
    tiles, strip, pattern = size
    half = pattern // 2
    kept = slice(pattern + half, pattern + half + strip)
    tall[kept] = jnp.zeros((strip, tall.shape[1]), F32)
    (pr0, pi0), (pr1, pi1) = ((ref[0], ref[1]) for ref in (own, other))
    power = pr0 * pr0 + pi0 * pi0 + (pr1 * pr1 + pi1 * pi1)
    for side in (-1, 0, 1):
        for slot in range(2):
            row, column = spot(info, size, minibatch, side, slot)
            add_at(tall, power, row + pattern, column)
    out[...] = tall[kept]


def ready_kernel(info, probe, measured, table, own, observed, split):
    own[...] = probe[...]
    for minibatch in range(2):
        observed[minibatch] = measured[minibatch, info[25]]
    for i in range(2):
        split[2 * i], split[2 * i + 1] = halves(table[i])


def field_kernel(size, minibatch, info, strip_ref, *refs):
    tiles, strip, pattern = size
    slot = info[25]
    count = 2 if minibatch else 4
    edges, (own, other, measured, table) = refs[:count], refs[count : count + 4]
    gradient, step_own, step_other, window = refs[count + 4 :]

    def edge(side, part):
        if len(edges) == 2:
            return edges[side][part]
        return jnp.where(slot == part, edges[2 * side][...], edges[2 * side + 1][...])

    obj_real, obj_imag = (
        cut_patch(size, info, minibatch, strip_ref, edge(0, part), edge(1, part), window, part)
        for part in range(2)
    )
    cos_high, cos_low, sin_high, sin_low = (table[i] for i in range(4))

    def block(top_left, top_right, low_left, low_right):
        return jnp.concatenate(
            [
                jnp.concatenate([top_left, top_right], axis=1),
                jnp.concatenate([low_left, low_right], axis=1),
            ],
            axis=0,
        )

    first = (
        block(cos_high, sin_high, -sin_high, cos_high),
        block(cos_low, sin_low, -sin_low, cos_low),
    )
    second = (
        block(cos_high, -sin_high, sin_high, cos_high),
        block(cos_low, -sin_low, sin_low, cos_low),
    )
    probes = [(ref[0], ref[1]) for ref in (own, other)]

    def both(fields, left, right):
        (r0, i0), (r1, i1) = fields
        y = product(left, halves(block(r0, r1, i0, i1)))
        y = block(
            y[:pattern, :pattern], y[pattern:, :pattern], y[:pattern, pattern:], y[pattern:, pattern:]
        )
        y = product(halves(y), right)
        return (
            (y[:pattern, :pattern], y[:pattern, pattern:]),
            (y[pattern:, :pattern], y[pattern:, pattern:]),
        )

    exits = [(pr * obj_real - pi * obj_imag, pr * obj_imag + pi * obj_real) for pr, pi in probes]
    far = both(exits, first, second)
    intensity = (far[0][0] * far[0][0] + far[0][1] * far[0][1]) + (
        far[1][0] * far[1][0] + far[1][1] * far[1][1]
    )
    factor = jnp.sqrt((measured[minibatch] + 1.0) / (intensity + 1.0)) - 1.0
    chi = both([(factor * fr, factor * fi) for fr, fi in far], second, first)
    (pr0, pi0), (pr1, pi1) = probes
    (cr0, ci0), (cr1, ci1) = chi
    gradient[0] = (pr0 * cr0 + pi0 * ci0) + (pr1 * cr1 + pi1 * ci1)
    gradient[1] = (pr0 * ci0 - pi0 * cr0) + (pr1 * ci1 - pi1 * cr1)
    coverage = obj_real * obj_real + obj_imag * obj_imag
    rows = pattern // GROUP
    mate = lax.rem(info[24], GROUP)
    for step, keeper, (cr, ci) in ((step_own, slot, chi[0]), (step_other, 1 - slot, chi[1])):
        real = obj_real * cr + obj_imag * ci
        imag = obj_real * ci - obj_imag * cr
        for k in range(GROUP):
            start = k * rows
            block = step.at[mate ^ k]
            block[:rows] = real[start : start + rows]
            block[rows : 2 * rows] = imag[start : start + rows]
            middle = start + rows // 2
            block[2 * rows :] = jnp.where(
                keeper == 0, coverage[start:middle], coverage[middle : start + rows]
            )


def update_kernel(size, minibatch, info, strip_ref, illum, own, other, b0, a0, b1, a1, *outs):
    strip_out, *edges, tall = outs
    tiles, strip, pattern = size
    half = pattern // 2
    slot = info[25]
    kept = slice(pattern + half, pattern + half + strip)
    grads = (
        (0, slot, own, 0),
        (0, 1 - slot, other, 0),
        (-1, slot, b0, half),
        (1, slot, a0, 0),
        (-1, 1 - slot, b1, half),
        (1, 1 - slot, a1, 0),
    )
    for part in range(2):
        tall[kept] = jnp.zeros((strip, tall.shape[1]), F32)
        for side, place, ref, start in grads:
            row, column = spot(info, size, minibatch, side, place)
            add_at(tall, ref[part], row + pattern + start, column)
        fresh = strip_ref[part] + tall[kept] / (illum[...] + 1.0)
        strip_out[part] = fresh
        if edges:
            column_below = spot(info, size, minibatch + 1, -1, slot)[1]
            column_above = spot(info, size, minibatch + 1, 1, slot)[1]
            edges[0][part] = take_columns(fresh[:half], column_below, pattern)
            edges[1][part] = take_columns(fresh[strip - half :], column_above, pattern)


def probe_kernel(info, own_totals, other_totals, *refs):
    probes, outs = refs[: len(refs) // 2], refs[len(refs) // 2 :]
    slot = info[25]
    rows = outs[0].shape[1] // GROUP
    mate = lax.rem(info[24], GROUP)
    for k in range(GROUP):
        where = pl.ds(pl.multiple_of((mate ^ k) * rows, rows), rows)
        mine, theirs = own_totals[k], other_totals[k]
        own_half, other_half = mine[2 * rows :], theirs[theirs.shape[0] - rows // 2 :]
        coverage = jnp.concatenate(
            [
                jnp.where(slot == 0, own_half, other_half),
                jnp.where(slot == 0, other_half, own_half),
            ],
            axis=0,
        )
        divisor = coverage + 1.0
        for totals, probe, out in zip((mine, theirs), probes, outs):
            for part in range(2):
                change = totals[part * rows : (part + 1) * rows] / divisor
                out[part, where, :] = probe[part, where, :] + change


def call(kernel, name, outs, inputs, scratch=(), flops=0):
    shapes = [
        shape if isinstance(shape, jax.ShapeDtypeStruct) else jax.ShapeDtypeStruct(shape, F32)
        for shape in outs
    ]
    size = sum(value.size * value.dtype.itemsize for value in (*shapes, *inputs))
    smem = pl.BlockSpec(memory_space=pltpu.SMEM)
    vmem = pl.BlockSpec(memory_space=pltpu.VMEM)
    return pl.pallas_call(
        kernel,
        out_shape=shapes,
        in_specs=[smem] + [vmem] * (len(inputs) - 1),
        out_specs=[vmem] * len(shapes),
        scratch_shapes=[pltpu.VMEM(shape, F32) for shape in scratch],
        compiler_params=pltpu.CompilerParams(vmem_limit_bytes=VMEM_BYTES),
        cost_estimate=pl.CostEstimate(flops=flops, bytes_accessed=size, transcendentals=0),
        name=name,
    )(*inputs)


def shards_by_position(object_field, probe, positions, measured):
    strip = object_field.shape[1]
    width = object_field.shape[2]
    pattern = probe.shape[2]
    half = pattern // 2
    tiles = lax.axis_size("tile")
    size = (tiles, strip, pattern)
    field = (2, pattern, pattern)
    tall = (3 * pattern + strip + 8, width)
    window = (pattern + strip + 8, pattern)
    up = [(i, i + 1) for i in range(tiles - 1)]
    down = [(i + 1, i) for i in range(tiles - 1)]

    def swap(value):
        return lax.ppermute(value, "mode", [(0, 1), (1, 0)])

    def across(value, k):
        return lax.ppermute(value, "tile", [(i, i ^ k) for i in range(tiles)])

    def scatter(blocks, unit):
        mates = [across(blocks[k], unit * k) for k in range(1, GROUP)]
        return functools.reduce(jnp.add, mates, blocks[0])

    def exchange(piece, unit):
        mates = [across(piece, unit * k) for k in range(1, GROUP)]
        return functools.reduce(jnp.add, mates, piece)

    def gather(piece, unit):
        return jnp.stack([piece] + [across(piece, unit * k) for k in range(1, GROUP)])

    def from_below(value):
        return lax.ppermute(value, "tile", up)

    def from_above(value):
        return lax.ppermute(value, "tile", down)

    def bind(kernel, *args):
        return functools.partial(kernel, *args)

    tile, slot = lax.axis_index("tile"), lax.axis_index("mode")
    index = jnp.stack([tile, slot]).astype(jnp.int32)
    here = jnp.concatenate([positions.ravel()] * 3 + [index])
    one_part = lax.dynamic_index_in_dim(object_field, slot, 0, keepdims=False)
    edges = [from_below(one_part[strip - half :]), from_above(one_part[:half])]
    below, above = from_below(positions), from_above(positions)
    other = swap(probe[0])
    own, observed, table = call(
        ready_kernel,
        "ready",
        [field, field, jax.ShapeDtypeStruct((4, pattern, pattern), BF16)],
        (here, probe[0], measured, jnp.asarray(table_of(pattern))),
    )
    *edges, below, above, own, observed, table = lax.optimization_barrier(
        (*edges, below, above, own, observed, table)
    )
    edges = [edges[0], swap(edges[0]), edges[1], swap(edges[1])]
    info = jnp.concatenate([below.ravel(), positions.ravel(), above.ravel(), index])

    for minibatch in range(2):
        last = minibatch == 1
        rows = pattern // GROUP
        blocks = (GROUP, 2 * rows + rows // 2, pattern)
        gradient, step_own, step_other = call(
            bind(field_kernel, size, minibatch),
            "field",
            [field, blocks, blocks],
            (here, object_field, *edges, own, other, observed, table),
            [window],
            flops=2 * 12 * 512**3,
        )
        (illum,) = call(
            bind(illumination_kernel, size, minibatch),
            "illumination",
            [(strip, width)],
            (info, own, other),
            [tall],
        )
        steps = step_own + swap(step_other)
        piece = scatter(steps, 1)
        source = gradient
        if last:
            source, piece = lax.optimization_barrier((source, piece))
        rim_below, rim_above = from_below(source[:, half:]), from_above(source[:, :half])
        if not last:
            rim_below, rim_above, piece = lax.optimization_barrier((rim_below, rim_above, piece))
        rims = (gradient, swap(gradient), rim_below, rim_above, swap(rim_below), swap(rim_above))
        object_field, *edges = call(
            bind(update_kernel, size, minibatch),
            "update",
            [object_field.shape] + ([] if last else [(2, half, pattern)] * 2),
            (info, object_field, illum, *rims),
            [tall],
        )
        piece = exchange(piece, GROUP)
        if not last:
            edges = [from_below(edges[1]), from_above(edges[0])]
            piece, *edges = lax.optimization_barrier((piece, *edges))
        totals = gather(piece, 1)
        if last:
            others = swap(totals[:, 2 * rows :])
            (own,) = call(probe_kernel, "probe", [field], (here, totals, others, own))
        else:
            own, other = call(
                probe_kernel, "probe", [field] * 2, (here, totals, swap(totals), own, other)
            )
    return (object_field, own[None])


def solution(mesh):
    in_specs = (
        P(None, "tile", None),
        P("mode", None, None, None),
        P(None, "tile", None),
        P(None, "tile", None, None),
    )
    out_specs = (P(None, "tile", None), P("mode", None, None, None))

    def whole(object_field, probe, positions, measured):
        tiles, pair = mesh.shape["tile"], mesh.shape["mode"]
        by_position = (
            pair == 2
            and probe.shape[0] == 2
            and positions.shape[:2] == (2, 2 * tiles)
            and tiles == GROUP * GROUP
            and probe.shape[2] % (16 * 2 * GROUP) == 0
            and object_field.shape[1] == tiles * probe.shape[2]
        )
        shards = shards_by_position if by_position else shards_by_mode
        return jax.shard_map(
            shards, mesh=mesh, in_specs=in_specs, out_specs=out_specs, check_vma=False
        )(object_field, probe, positions, measured)

    return whole
```

```python
import functools
import math

import jax
import jax.numpy as jnp
import numpy as np
from jax import lax
from jax.experimental import pallas as pl
from jax.experimental.pallas import tpu as pltpu
from jax.sharding import PartitionSpec as P

F32 = jnp.float32
BF16 = jnp.bfloat16
VMEM_BYTES = 16 * 1024 * 1024
GROUP = 4


def padded(block, sides, width):
    for axis, dim in sides:
        count = lax.axis_size(axis)
        forward = [(i, i + 1) for i in range(count - 1)]
        backward = [(target, source) for source, target in forward]
        low = lax.ppermute(
            lax.slice_in_dim(block, block.shape[dim] - width, None, axis=dim), axis, forward
        )
        high = lax.ppermute(lax.slice_in_dim(block, 0, width, axis=dim), axis, backward)
        block = jnp.concatenate([low, block, high], axis=dim)
    return block


def tables(length):
    index_values = jnp.arange(length, dtype=jnp.int32)
    product = index_values[:, None] * index_values[None, :] % length
    angles = product.astype(jnp.float32) * (2.0 * math.pi / length)
    scaling = 1.0 / math.sqrt(length)
    return (jnp.cos(angles) * scaling, jnp.sin(angles) * scaling)


def apply_left(matrix, target):
    return jnp.einsum("ab,pbc->pac", matrix, target, precision=lax.Precision.HIGHEST)


def apply_right(target, matrix):
    return jnp.einsum("pab,bc->pac", target, matrix, precision=lax.Precision.HIGHEST)


def transform(real_part, imag_part, cosine, sine_table, direction):
    left_real = apply_left(cosine, real_part) + direction * apply_left(sine_table, imag_part)
    left_imag = apply_left(cosine, imag_part) - direction * apply_left(sine_table, real_part)
    out_real = apply_right(left_real, cosine) + direction * apply_right(left_imag, sine_table)
    out_imag = apply_right(left_imag, cosine) - direction * apply_right(left_real, sine_table)
    return (out_real, out_imag)


def place_add(target, placed, row_start, col_start):
    zero_index = jnp.int32(0)
    current = lax.dynamic_slice(target, (zero_index, row_start, col_start), placed.shape)
    return lax.dynamic_update_slice(target, current + placed, (zero_index, row_start, col_start))


def shards_by_mode(object_field, probe, positions, measured):
    strip_rows = object_field.shape[1]
    object_width = object_field.shape[2]
    pattern = probe.shape[2]
    half_pattern = pattern // 2
    count = positions.shape[1]
    cosine, sine_table = tables(pattern)
    tile_index = lax.axis_index("tile")
    offset = tile_index * strip_rows - half_pattern
    for minibatch in range(measured.shape[0]):
        extended = padded(object_field, (("tile", 1),), half_pattern)
        row_offsets = positions[minibatch, :, 0] - offset
        column_offsets = positions[minibatch, :, 1]

        def cut_one(row_start, col_start):
            return lax.dynamic_slice(
                extended, (jnp.int32(0), row_start, col_start), (2, pattern, pattern)
            )

        patches = jax.vmap(cut_one)(row_offsets, column_offsets)
        obj_real = patches[:, 0]
        obj_imag = patches[:, 1]
        probe_real = probe[0, 0]
        probe_imag = probe[0, 1]
        exit_real = probe_real * obj_real - probe_imag * obj_imag
        exit_imag = probe_real * obj_imag + probe_imag * obj_real
        far_real, far_imag = transform(exit_real, exit_imag, cosine, sine_table, 1.0)
        observed = measured[minibatch]
        intensity = lax.psum(far_real * far_real + far_imag * far_imag, "mode")
        modulus = jnp.sqrt((observed + 1.0) / (intensity + 1.0)) - 1.0
        chi_real, chi_imag = transform(
            modulus * far_real, modulus * far_imag, cosine, sine_table, -1.0
        )
        grad_real = probe_real * chi_real + probe_imag * chi_imag
        grad_imag = probe_real * chi_imag - probe_imag * chi_real
        probe_power = probe_real * probe_real + probe_imag * probe_imag
        step_real = jnp.sum(obj_real * chi_real + obj_imag * chi_imag, axis=0)
        step_imag = jnp.sum(obj_real * chi_imag - obj_imag * chi_real, axis=0)
        coverage = jnp.sum(obj_real * obj_real + obj_imag * obj_imag, axis=0)
        accumulated = jnp.zeros((3, strip_rows + pattern, object_width), jnp.float32)
        for position in range(count):
            placed = jnp.stack([grad_real[position], grad_imag[position], probe_power])
            accumulated = place_add(
                accumulated, placed, row_offsets[position], column_offsets[position]
            )
        rim_rows = jnp.concatenate(
            [accumulated[:, :half_pattern], accumulated[:, strip_rows + half_pattern :]], axis=1
        )
        received = padded(rim_rows, (("tile", 1),), half_pattern)
        own_strip = accumulated[:, half_pattern : half_pattern + strip_rows]
        own_strip = own_strip.at[:, :half_pattern].add(received[:, :half_pattern])
        own_strip = own_strip.at[:, strip_rows - half_pattern :].add(
            received[:, pattern + half_pattern :]
        )
        summed = lax.psum(own_strip, "mode")
        divisor = summed[2] + 1.0
        object_field = jnp.stack(
            [object_field[0] + summed[0] / divisor, object_field[1] + summed[1] / divisor]
        )
        step_stack = jnp.stack([jnp.stack([step_real, step_imag])])
        step_total, coverage_total = lax.psum((step_stack, coverage), "tile")
        probe = probe + step_total / (coverage_total + 1.0)
    return (object_field, probe)


def table_of(length):
    index_values = np.arange(length)
    angles = (index_values[:, None] * index_values[None, :] % length) * (2.0 * np.pi / length)
    scaling = 1.0 / np.sqrt(length)
    return np.stack([np.cos(angles) * scaling, np.sin(angles) * scaling]).astype(np.float32)


def spot(info, size, minibatch, side, slot):
    tiles, strip, pattern = size
    place = (((side + 1) * 2 + minibatch) * 2 + slot) * 2
    tile = info[24]
    row = info[place] - tile * strip + pattern // 2
    if side < 0:
        row = jnp.where(tile == 0, -pattern, row)
    if side > 0:
        row = jnp.where(tile == tiles - 1, strip + pattern, row)
    return row, info[place + 1]


def take_columns(block, column, width):
    total = block.shape[-1]
    return pltpu.roll(block, lax.rem(total - column, total), 1)[:, :width]


def add_at(tall, block, row, column):
    rows, width = block.shape
    total = tall.shape[1]
    shift = lax.rem(row, 8)
    start = pl.multiple_of(row - shift, 8)
    turned = pltpu.roll(block.reshape(rows // 8, 8, width), shift, 1)
    empty = jnp.zeros((1, 8, width), block.dtype)
    inside = lax.broadcasted_iota(jnp.int32, (rows // 8 + 1, 8, width), 1) >= shift
    moved = jnp.where(
        inside,
        jnp.concatenate([turned, empty], axis=0),
        jnp.concatenate([empty, turned], axis=0),
    ).reshape(rows + 8, width)
    wide = jnp.concatenate([moved, jnp.zeros((rows + 8, total - width), block.dtype)], axis=1)
    tall[pl.ds(start, rows + 8), :] += pltpu.roll(wide, column, 1)


def rows_at(ref, row, rows):
    width = ref.shape[1]
    shift = lax.rem(row, 8)
    start = pl.multiple_of(row - shift, 8)
    block = ref[pl.ds(start, rows + 8), :].reshape(rows // 8 + 1, 8, width)
    turned = pltpu.roll(block, lax.rem(8 - shift, 8), 1)
    inside = lax.broadcasted_iota(jnp.int32, (rows // 8, 8, width), 1) < 8 - shift
    return jnp.where(inside, turned[:-1], turned[1:]).reshape(rows, width)


def halves(value):
    high = value.astype(BF16)
    return high, (value - high.astype(F32)).astype(BF16)


def product(left, right):
    dot = functools.partial(jnp.dot, preferred_element_type=F32)
    return dot(left[0], right[0]) + (dot(left[0], right[1]) + dot(left[1], right[0]))


def cut_patch(size, info, minibatch, strip_ref, below, above, window, part):
    tiles, rows, width = size
    half = width // 2
    row, column = spot(info, size, minibatch, 0, info[25])

    def columns(block):
        return block if block.shape[1] == width else take_columns(block, column, width)

    window[:half] = columns(below)
    window[half : half + rows] = columns(strip_ref[part])
    window[half + rows : rows + width] = columns(above)
    return rows_at(window, row, width)


def illumination_kernel(size, minibatch, info, own, other, out, tall):
    tiles, strip, pattern = size
    half = pattern // 2
    kept = slice(pattern + half, pattern + half + strip)
    tall[kept] = jnp.zeros((strip, tall.shape[1]), F32)
    (pr0, pi0), (pr1, pi1) = ((ref[0], ref[1]) for ref in (own, other))
    power = pr0 * pr0 + pi0 * pi0 + (pr1 * pr1 + pi1 * pi1)
    for side in (-1, 0, 1):
        for slot in range(2):
            row, column = spot(info, size, minibatch, side, slot)
            add_at(tall, power, row + pattern, column)
    out[...] = tall[kept]


def ready_kernel(info, probe, measured, table, own, observed, split):
    own[...] = probe[...]
    for minibatch in range(2):
        observed[minibatch] = measured[minibatch, info[25]]
    for i in range(2):
        split[2 * i], split[2 * i + 1] = halves(table[i])


def field_kernel(size, minibatch, info, strip_ref, *refs):
    tiles, strip, pattern = size
    slot = info[25]
    count = 2 if minibatch else 4
    edges, (own, other, measured, table) = refs[:count], refs[count : count + 4]
    gradient, step_own, step_other, window = refs[count + 4 :]

    def edge(side, part):
        if len(edges) == 2:
            return edges[side][part]
        return jnp.where(slot == part, edges[2 * side][...], edges[2 * side + 1][...])

    obj_real, obj_imag = (
        cut_patch(size, info, minibatch, strip_ref, edge(0, part), edge(1, part), window, part)
        for part in range(2)
    )
    cos_high, cos_low, sin_high, sin_low = (table[i] for i in range(4))

    def block(top_left, top_right, low_left, low_right):
        return jnp.concatenate(
            [
                jnp.concatenate([top_left, top_right], axis=1),
                jnp.concatenate([low_left, low_right], axis=1),
            ],
            axis=0,
        )

    first = (
        block(cos_high, sin_high, -sin_high, cos_high),
        block(cos_low, sin_low, -sin_low, cos_low),
    )
    second = (
        block(cos_high, -sin_high, sin_high, cos_high),
        block(cos_low, -sin_low, sin_low, cos_low),
    )
    probes = [(ref[0], ref[1]) for ref in (own, other)]

    def both(fields, left, right):
        (r0, i0), (r1, i1) = fields
        y = product(left, halves(block(r0, r1, i0, i1)))
        y = block(
            y[:pattern, :pattern], y[pattern:, :pattern], y[:pattern, pattern:], y[pattern:, pattern:]
        )
        y = product(halves(y), right)
        return (
            (y[:pattern, :pattern], y[:pattern, pattern:]),
            (y[pattern:, :pattern], y[pattern:, pattern:]),
        )

    exits = [(pr * obj_real - pi * obj_imag, pr * obj_imag + pi * obj_real) for pr, pi in probes]
    far = both(exits, first, second)
    intensity = (far[0][0] * far[0][0] + far[0][1] * far[0][1]) + (
        far[1][0] * far[1][0] + far[1][1] * far[1][1]
    )
    factor = jnp.sqrt((measured[minibatch] + 1.0) / (intensity + 1.0)) - 1.0
    chi = both([(factor * fr, factor * fi) for fr, fi in far], second, first)
    (pr0, pi0), (pr1, pi1) = probes
    (cr0, ci0), (cr1, ci1) = chi
    gradient[0] = (pr0 * cr0 + pi0 * ci0) + (pr1 * cr1 + pi1 * ci1)
    gradient[1] = (pr0 * ci0 - pi0 * cr0) + (pr1 * ci1 - pi1 * cr1)
    coverage = obj_real * obj_real + obj_imag * obj_imag
    rows = pattern // GROUP
    mate = lax.rem(info[24], GROUP)
    for step, keeper, (cr, ci) in ((step_own, slot, chi[0]), (step_other, 1 - slot, chi[1])):
        real = obj_real * cr + obj_imag * ci
        imag = obj_real * ci - obj_imag * cr
        for k in range(GROUP):
            start = k * rows
            block = step.at[mate ^ k]
            block[:rows] = real[start : start + rows]
            block[rows : 2 * rows] = imag[start : start + rows]
            middle = start + rows // 2
            block[2 * rows :] = jnp.where(
                keeper == 0, coverage[start:middle], coverage[middle : start + rows]
            )


def update_kernel(size, minibatch, info, strip_ref, illum, own, other, b0, a0, b1, a1, *outs):
    strip_out, *edges, tall = outs
    tiles, strip, pattern = size
    half = pattern // 2
    slot = info[25]
    kept = slice(pattern + half, pattern + half + strip)
    grads = (
        (0, slot, own, 0),
        (0, 1 - slot, other, 0),
        (-1, slot, b0, half),
        (1, slot, a0, 0),
        (-1, 1 - slot, b1, half),
        (1, 1 - slot, a1, 0),
    )
    for part in range(2):
        tall[kept] = jnp.zeros((strip, tall.shape[1]), F32)
        for side, place, ref, start in grads:
            row, column = spot(info, size, minibatch, side, place)
            add_at(tall, ref[part], row + pattern + start, column)
        fresh = strip_ref[part] + tall[kept] / (illum[...] + 1.0)
        strip_out[part] = fresh
        if edges:
            column_below = spot(info, size, minibatch + 1, -1, slot)[1]
            column_above = spot(info, size, minibatch + 1, 1, slot)[1]
            edges[0][part] = take_columns(fresh[:half], column_below, pattern)
            edges[1][part] = take_columns(fresh[strip - half :], column_above, pattern)


def probe_kernel(info, own_totals, other_totals, *refs):
    probes, outs = refs[: len(refs) // 2], refs[len(refs) // 2 :]
    slot = info[25]
    rows = outs[0].shape[1] // GROUP
    mate = lax.rem(info[24], GROUP)
    for k in range(GROUP):
        where = pl.ds(pl.multiple_of((mate ^ k) * rows, rows), rows)
        mine, theirs = own_totals[k], other_totals[k]
        own_half, other_half = mine[2 * rows :], theirs[theirs.shape[0] - rows // 2 :]
        coverage = jnp.concatenate(
            [
                jnp.where(slot == 0, own_half, other_half),
                jnp.where(slot == 0, other_half, own_half),
            ],
            axis=0,
        )
        divisor = coverage + 1.0
        for totals, probe, out in zip((mine, theirs), probes, outs):
            for part in range(2):
                change = totals[part * rows : (part + 1) * rows] / divisor
                out[part, where, :] = probe[part, where, :] + change


def call(kernel, name, outs, inputs, scratch=(), flops=0):
    shapes = [
        shape if isinstance(shape, jax.ShapeDtypeStruct) else jax.ShapeDtypeStruct(shape, F32)
        for shape in outs
    ]
    size = sum(value.size * value.dtype.itemsize for value in (*shapes, *inputs))
    smem = pl.BlockSpec(memory_space=pltpu.SMEM)
    vmem = pl.BlockSpec(memory_space=pltpu.VMEM)
    return pl.pallas_call(
        kernel,
        out_shape=shapes,
        in_specs=[smem] + [vmem] * (len(inputs) - 1),
        out_specs=[vmem] * len(shapes),
        scratch_shapes=[pltpu.VMEM(shape, F32) for shape in scratch],
        compiler_params=pltpu.CompilerParams(vmem_limit_bytes=VMEM_BYTES),
        cost_estimate=pl.CostEstimate(flops=flops, bytes_accessed=size, transcendentals=0),
        name=name,
    )(*inputs)


def shards_by_position(object_field, probe, positions, measured):
    strip = object_field.shape[1]
    width = object_field.shape[2]
    pattern = probe.shape[2]
    half = pattern // 2
    tiles = lax.axis_size("tile")
    size = (tiles, strip, pattern)
    field = (2, pattern, pattern)
    tall = (3 * pattern + strip + 8, width)
    window = (pattern + strip + 8, pattern)
    up = [(i, i + 1) for i in range(tiles - 1)]
    down = [(i + 1, i) for i in range(tiles - 1)]

    def swap(value):
        return lax.ppermute(value, "mode", [(0, 1), (1, 0)])

    def across(value, k):
        return lax.ppermute(value, "tile", [(i, i ^ k) for i in range(tiles)])

    def scatter(blocks, unit):
        mates = [across(blocks[k], unit * k) for k in range(1, GROUP)]
        return functools.reduce(jnp.add, mates, blocks[0])

    def exchange(piece, unit):
        piece = piece + across(piece, unit)
        return piece + across(piece, 2 * unit)

    def gather(piece, unit):
        return jnp.stack([piece] + [across(piece, unit * k) for k in range(1, GROUP)])

    def from_below(value):
        return lax.ppermute(value, "tile", up)

    def from_above(value):
        return lax.ppermute(value, "tile", down)

    def bind(kernel, *args):
        return functools.partial(kernel, *args)

    tile, slot = lax.axis_index("tile"), lax.axis_index("mode")
    index = jnp.stack([tile, slot]).astype(jnp.int32)
    here = jnp.concatenate([positions.ravel()] * 3 + [index])
    one_part = lax.dynamic_index_in_dim(object_field, slot, 0, keepdims=False)
    edges = [from_below(one_part[strip - half :]), from_above(one_part[:half])]
    below, above = from_below(positions), from_above(positions)
    other = swap(probe[0])
    own, observed, table = call(
        ready_kernel,
        "ready",
        [field, field, jax.ShapeDtypeStruct((4, pattern, pattern), BF16)],
        (here, probe[0], measured, jnp.asarray(table_of(pattern))),
    )
    *edges, below, above, own, observed, table = lax.optimization_barrier(
        (*edges, below, above, own, observed, table)
    )
    edges = [edges[0], swap(edges[0]), edges[1], swap(edges[1])]
    info = jnp.concatenate([below.ravel(), positions.ravel(), above.ravel(), index])

    for minibatch in range(2):
        last = minibatch == 1
        rows = pattern // GROUP
        blocks = (GROUP, 2 * rows + rows // 2, pattern)
        gradient, step_own, step_other = call(
            bind(field_kernel, size, minibatch),
            "field",
            [field, blocks, blocks],
            (here, object_field, *edges, own, other, observed, table),
            [window],
            flops=2 * 12 * 512**3,
        )
        (illum,) = call(
            bind(illumination_kernel, size, minibatch),
            "illumination",
            [(strip, width)],
            (info, own, other),
            [tall],
        )
        steps = step_own + swap(step_other)
        piece = scatter(steps, 1)
        if last:
            gradient, piece, illum = lax.optimization_barrier((gradient, piece, illum))
        rim_below, rim_above = from_below(gradient[:, half:]), from_above(gradient[:, :half])
        if not last:
            gradient, rim_below, rim_above, piece, illum = lax.optimization_barrier(
                (gradient, rim_below, rim_above, piece, illum)
            )
        rims = (gradient, swap(gradient), rim_below, rim_above, swap(rim_below), swap(rim_above))
        object_field, *edges = call(
            bind(update_kernel, size, minibatch),
            "update",
            [object_field.shape] + ([] if last else [(2, half, pattern)] * 2),
            (info, object_field, illum, *rims),
            [tall],
        )
        piece = exchange(piece, GROUP)
        if not last:
            edges = [from_below(edges[1]), from_above(edges[0])]
            piece, *edges = lax.optimization_barrier((piece, *edges))
        totals = gather(piece, 1)
        if last:
            totals, object_field = lax.optimization_barrier((totals, object_field))
            others = swap(totals[:, 2 * rows :])
            (own,) = call(probe_kernel, "probe", [field], (here, totals, others, own))
        else:
            own, other = call(
                probe_kernel, "probe", [field] * 2, (here, totals, swap(totals), own, other)
            )
    return (object_field, own[None])


def solution(mesh):
    in_specs = (
        P(None, "tile", None),
        P("mode", None, None, None),
        P(None, "tile", None),
        P(None, "tile", None, None),
    )
    out_specs = (P(None, "tile", None), P("mode", None, None, None))

    def whole(object_field, probe, positions, measured):
        tiles, pair = mesh.shape["tile"], mesh.shape["mode"]
        by_position = (
            pair == 2
            and probe.shape[0] == 2
            and positions.shape[:2] == (2, 2 * tiles)
            and tiles == GROUP * GROUP
            and probe.shape[2] % (16 * 2 * GROUP) == 0
            and object_field.shape[1] == tiles * probe.shape[2]
        )
        shards = shards_by_position if by_position else shards_by_mode
        return jax.shard_map(
            shards, mesh=mesh, in_specs=in_specs, out_specs=out_specs, check_vma=False
        )(object_field, probe, positions, measured)

    return whole
```

```python
import functools
import math

import jax
import jax.numpy as jnp
import numpy as np
from jax import lax
from jax.experimental import pallas as pl
from jax.experimental.pallas import tpu as pltpu
from jax.sharding import PartitionSpec as P

F32 = jnp.float32
BF16 = jnp.bfloat16
VMEM_BYTES = 16 * 1024 * 1024
GROUP = 4


def padded(block, sides, width):
    for axis, dim in sides:
        count = lax.axis_size(axis)
        forward = [(i, i + 1) for i in range(count - 1)]
        backward = [(target, source) for source, target in forward]
        low = lax.ppermute(
            lax.slice_in_dim(block, block.shape[dim] - width, None, axis=dim), axis, forward
        )
        high = lax.ppermute(lax.slice_in_dim(block, 0, width, axis=dim), axis, backward)
        block = jnp.concatenate([low, block, high], axis=dim)
    return block


def tables(length):
    index_values = jnp.arange(length, dtype=jnp.int32)
    product = index_values[:, None] * index_values[None, :] % length
    angles = product.astype(jnp.float32) * (2.0 * math.pi / length)
    scaling = 1.0 / math.sqrt(length)
    return (jnp.cos(angles) * scaling, jnp.sin(angles) * scaling)


def apply_left(matrix, target):
    return jnp.einsum("ab,pbc->pac", matrix, target, precision=lax.Precision.HIGHEST)


def apply_right(target, matrix):
    return jnp.einsum("pab,bc->pac", target, matrix, precision=lax.Precision.HIGHEST)


def transform(real_part, imag_part, cosine, sine_table, direction):
    left_real = apply_left(cosine, real_part) + direction * apply_left(sine_table, imag_part)
    left_imag = apply_left(cosine, imag_part) - direction * apply_left(sine_table, real_part)
    out_real = apply_right(left_real, cosine) + direction * apply_right(left_imag, sine_table)
    out_imag = apply_right(left_imag, cosine) - direction * apply_right(left_real, sine_table)
    return (out_real, out_imag)


def place_add(target, placed, row_start, col_start):
    zero_index = jnp.int32(0)
    current = lax.dynamic_slice(target, (zero_index, row_start, col_start), placed.shape)
    return lax.dynamic_update_slice(target, current + placed, (zero_index, row_start, col_start))


def shards_by_mode(object_field, probe, positions, measured):
    strip_rows = object_field.shape[1]
    object_width = object_field.shape[2]
    pattern = probe.shape[2]
    half_pattern = pattern // 2
    count = positions.shape[1]
    cosine, sine_table = tables(pattern)
    tile_index = lax.axis_index("tile")
    offset = tile_index * strip_rows - half_pattern
    for minibatch in range(measured.shape[0]):
        extended = padded(object_field, (("tile", 1),), half_pattern)
        row_offsets = positions[minibatch, :, 0] - offset
        column_offsets = positions[minibatch, :, 1]

        def cut_one(row_start, col_start):
            return lax.dynamic_slice(
                extended, (jnp.int32(0), row_start, col_start), (2, pattern, pattern)
            )

        patches = jax.vmap(cut_one)(row_offsets, column_offsets)
        obj_real = patches[:, 0]
        obj_imag = patches[:, 1]
        probe_real = probe[0, 0]
        probe_imag = probe[0, 1]
        exit_real = probe_real * obj_real - probe_imag * obj_imag
        exit_imag = probe_real * obj_imag + probe_imag * obj_real
        far_real, far_imag = transform(exit_real, exit_imag, cosine, sine_table, 1.0)
        observed = measured[minibatch]
        intensity = lax.psum(far_real * far_real + far_imag * far_imag, "mode")
        modulus = jnp.sqrt((observed + 1.0) / (intensity + 1.0)) - 1.0
        chi_real, chi_imag = transform(
            modulus * far_real, modulus * far_imag, cosine, sine_table, -1.0
        )
        grad_real = probe_real * chi_real + probe_imag * chi_imag
        grad_imag = probe_real * chi_imag - probe_imag * chi_real
        probe_power = probe_real * probe_real + probe_imag * probe_imag
        step_real = jnp.sum(obj_real * chi_real + obj_imag * chi_imag, axis=0)
        step_imag = jnp.sum(obj_real * chi_imag - obj_imag * chi_real, axis=0)
        coverage = jnp.sum(obj_real * obj_real + obj_imag * obj_imag, axis=0)
        accumulated = jnp.zeros((3, strip_rows + pattern, object_width), jnp.float32)
        for position in range(count):
            placed = jnp.stack([grad_real[position], grad_imag[position], probe_power])
            accumulated = place_add(
                accumulated, placed, row_offsets[position], column_offsets[position]
            )
        rim_rows = jnp.concatenate(
            [accumulated[:, :half_pattern], accumulated[:, strip_rows + half_pattern :]], axis=1
        )
        received = padded(rim_rows, (("tile", 1),), half_pattern)
        own_strip = accumulated[:, half_pattern : half_pattern + strip_rows]
        own_strip = own_strip.at[:, :half_pattern].add(received[:, :half_pattern])
        own_strip = own_strip.at[:, strip_rows - half_pattern :].add(
            received[:, pattern + half_pattern :]
        )
        summed = lax.psum(own_strip, "mode")
        divisor = summed[2] + 1.0
        object_field = jnp.stack(
            [object_field[0] + summed[0] / divisor, object_field[1] + summed[1] / divisor]
        )
        step_stack = jnp.stack([jnp.stack([step_real, step_imag])])
        step_total, coverage_total = lax.psum((step_stack, coverage), "tile")
        probe = probe + step_total / (coverage_total + 1.0)
    return (object_field, probe)


def table_of(length):
    index_values = np.arange(length)
    angles = (index_values[:, None] * index_values[None, :] % length) * (2.0 * np.pi / length)
    scaling = 1.0 / np.sqrt(length)
    return np.stack([np.cos(angles) * scaling, np.sin(angles) * scaling]).astype(np.float32)


def spot(info, size, minibatch, side, slot):
    tiles, strip, pattern = size
    place = (((side + 1) * 2 + minibatch) * 2 + slot) * 2
    tile = info[24]
    row = info[place] - tile * strip + pattern // 2
    if side < 0:
        row = jnp.where(tile == 0, -pattern, row)
    if side > 0:
        row = jnp.where(tile == tiles - 1, strip + pattern, row)
    return row, info[place + 1]


def take_columns(block, column, width):
    total = block.shape[-1]
    return pltpu.roll(block, lax.rem(total - column, total), 1)[:, :width]


def add_at(tall, block, row, column):
    rows, width = block.shape
    total = tall.shape[1]
    shift = lax.rem(row, 8)
    start = pl.multiple_of(row - shift, 8)
    turned = pltpu.roll(block.reshape(rows // 8, 8, width), shift, 1)
    empty = jnp.zeros((1, 8, width), block.dtype)
    inside = lax.broadcasted_iota(jnp.int32, (rows // 8 + 1, 8, width), 1) >= shift
    moved = jnp.where(
        inside,
        jnp.concatenate([turned, empty], axis=0),
        jnp.concatenate([empty, turned], axis=0),
    ).reshape(rows + 8, width)
    wide = jnp.concatenate([moved, jnp.zeros((rows + 8, total - width), block.dtype)], axis=1)
    tall[pl.ds(start, rows + 8), :] += pltpu.roll(wide, column, 1)


def rows_at(ref, row, rows):
    width = ref.shape[1]
    shift = lax.rem(row, 8)
    start = pl.multiple_of(row - shift, 8)
    block = ref[pl.ds(start, rows + 8), :].reshape(rows // 8 + 1, 8, width)
    turned = pltpu.roll(block, lax.rem(8 - shift, 8), 1)
    inside = lax.broadcasted_iota(jnp.int32, (rows // 8, 8, width), 1) < 8 - shift
    return jnp.where(inside, turned[:-1], turned[1:]).reshape(rows, width)


def halves(value):
    high = value.astype(BF16)
    return high, (value - high.astype(F32)).astype(BF16)


def product(left, right):
    dot = functools.partial(jnp.dot, preferred_element_type=F32)
    return dot(left[0], right[0]) + (dot(left[0], right[1]) + dot(left[1], right[0]))


def cut_patch(size, info, minibatch, strip_ref, below, above, window, part):
    tiles, rows, width = size
    half = width // 2
    row, column = spot(info, size, minibatch, 0, info[25])

    def columns(block):
        return block if block.shape[1] == width else take_columns(block, column, width)

    window[:half] = columns(below)
    window[half : half + rows] = columns(strip_ref[part])
    window[half + rows : rows + width] = columns(above)
    return rows_at(window, row, width)


def illumination_kernel(size, minibatch, info, own, other, out, tall):
    tiles, strip, pattern = size
    half = pattern // 2
    kept = slice(pattern + half, pattern + half + strip)
    tall[kept] = jnp.zeros((strip, tall.shape[1]), F32)
    (pr0, pi0), (pr1, pi1) = ((ref[0], ref[1]) for ref in (own, other))
    power = pr0 * pr0 + pi0 * pi0 + (pr1 * pr1 + pi1 * pi1)
    for side in (-1, 0, 1):
        for slot in range(2):
            row, column = spot(info, size, minibatch, side, slot)
            add_at(tall, power, row + pattern, column)
    out[...] = tall[kept]


def patch_kernel(size, minibatch, info, strip_ref, below, above, patch, window):
    for part in range(2):
        patch[part] = cut_patch(
            size, info, minibatch, strip_ref, below[part], above[part], window, part
        )


def ready_kernel(info, probe, measured, table, own, observed, split):
    own[...] = probe[...]
    for minibatch in range(2):
        observed[minibatch] = measured[minibatch, info[25]]
    for i in range(2):
        split[2 * i], split[2 * i + 1] = halves(table[i])


def field_kernel(size, minibatch, info, strip_ref, *refs):
    tiles, strip, pattern = size
    slot = info[25]
    if minibatch:
        own, other, measured, table, gradient, top, bottom, step_own, step_other = refs
        obj_real, obj_imag = strip_ref[0], strip_ref[1]
    else:
        *edges, own, other, measured, table = refs[:-6]
        gradient, top, bottom, step_own, step_other, window = refs[-6:]
        sides = (jnp.where(slot == 0, edges[i][...], edges[i + 1][...]) for i in (0, 2))
        others = (jnp.where(slot == 0, edges[i + 1][...], edges[i][...]) for i in (0, 2))
        obj_real, obj_imag = (
            cut_patch(size, info, minibatch, strip_ref, *ends, window, part)
            for part, ends in enumerate((sides, others))
        )
    cos_high, cos_low, sin_high, sin_low = (table[i] for i in range(4))

    def block(top_left, top_right, low_left, low_right):
        return jnp.concatenate(
            [
                jnp.concatenate([top_left, top_right], axis=1),
                jnp.concatenate([low_left, low_right], axis=1),
            ],
            axis=0,
        )

    first = (
        block(cos_high, sin_high, -sin_high, cos_high),
        block(cos_low, sin_low, -sin_low, cos_low),
    )
    second = (
        block(cos_high, -sin_high, sin_high, cos_high),
        block(cos_low, -sin_low, sin_low, cos_low),
    )
    probes = [(ref[0], ref[1]) for ref in (own, other)]

    def both(fields, left, right):
        (r0, i0), (r1, i1) = fields
        y = product(left, halves(block(r0, r1, i0, i1)))
        y = block(
            y[:pattern, :pattern], y[pattern:, :pattern], y[:pattern, pattern:], y[pattern:, pattern:]
        )
        y = product(halves(y), right)
        return (
            (y[:pattern, :pattern], y[:pattern, pattern:]),
            (y[pattern:, :pattern], y[pattern:, pattern:]),
        )

    exits = [(pr * obj_real - pi * obj_imag, pr * obj_imag + pi * obj_real) for pr, pi in probes]
    far = both(exits, first, second)
    intensity = (far[0][0] * far[0][0] + far[0][1] * far[0][1]) + (
        far[1][0] * far[1][0] + far[1][1] * far[1][1]
    )
    factor = jnp.sqrt((measured[minibatch] + 1.0) / (intensity + 1.0)) - 1.0
    chi = both([(factor * fr, factor * fi) for fr, fi in far], second, first)
    (pr0, pi0), (pr1, pi1) = probes
    (cr0, ci0), (cr1, ci1) = chi
    half = top.shape[1]
    for part, value in (
        (0, (pr0 * cr0 + pi0 * ci0) + (pr1 * cr1 + pi1 * ci1)),
        (1, (pr0 * ci0 - pi0 * cr0) + (pr1 * ci1 - pi1 * cr1)),
    ):
        gradient[part], top[part], bottom[part] = value, value[:half], value[half:]
    coverage = obj_real * obj_real + obj_imag * obj_imag
    rows = pattern // GROUP
    mate = lax.rem(info[24], GROUP)
    for step, keeper, (cr, ci) in ((step_own, slot, chi[0]), (step_other, 1 - slot, chi[1])):
        real = obj_real * cr + obj_imag * ci
        imag = obj_real * ci - obj_imag * cr
        for k in range(GROUP):
            start = k * rows
            block = step.at[mate ^ k]
            block[:rows] = real[start : start + rows]
            block[rows : 2 * rows] = imag[start : start + rows]
            middle = start + rows // 2
            block[2 * rows :] = jnp.where(
                keeper == 0, coverage[start:middle], coverage[middle : start + rows]
            )


def update_kernel(size, minibatch, info, strip_ref, illum, own, other, b0, a0, b1, a1, *outs):
    strip_out, *edges, tall = outs
    tiles, strip, pattern = size
    half = pattern // 2
    slot = info[25]
    kept = slice(pattern + half, pattern + half + strip)
    grads = (
        (0, slot, own, 0),
        (0, 1 - slot, other, 0),
        (-1, slot, b0, half),
        (1, slot, a0, 0),
        (-1, 1 - slot, b1, half),
        (1, 1 - slot, a1, 0),
    )
    for part in range(2):
        tall[kept] = jnp.zeros((strip, tall.shape[1]), F32)
        for side, place, ref, start in grads:
            row, column = spot(info, size, minibatch, side, place)
            add_at(tall, ref[part], row + pattern + start, column)
        fresh = strip_ref[part] + tall[kept] / (illum[...] + 1.0)
        strip_out[part] = fresh
        if edges:
            column_below = spot(info, size, minibatch + 1, -1, slot)[1]
            column_above = spot(info, size, minibatch + 1, 1, slot)[1]
            edges[0][part] = take_columns(fresh[:half], column_below, pattern)
            edges[1][part] = take_columns(fresh[strip - half :], column_above, pattern)


def probe_kernel(info, own_totals, other_totals, *refs):
    probes, outs = refs[: len(refs) // 2], refs[len(refs) // 2 :]
    slot = info[25]
    rows = outs[0].shape[1] // GROUP
    mate = lax.rem(info[24], GROUP)
    for k in range(GROUP):
        where = pl.ds(pl.multiple_of((mate ^ k) * rows, rows), rows)
        mine, theirs = own_totals[k], other_totals[k]
        own_half, other_half = mine[2 * rows :], theirs[theirs.shape[0] - rows // 2 :]
        coverage = jnp.concatenate(
            [
                jnp.where(slot == 0, own_half, other_half),
                jnp.where(slot == 0, other_half, own_half),
            ],
            axis=0,
        )
        divisor = coverage + 1.0
        for totals, probe, out in zip((mine, theirs), probes, outs):
            for part in range(2):
                change = totals[part * rows : (part + 1) * rows] / divisor
                out[part, where, :] = probe[part, where, :] + change


def call(kernel, name, outs, inputs, scratch=(), flops=0):
    shapes = [
        shape if isinstance(shape, jax.ShapeDtypeStruct) else jax.ShapeDtypeStruct(shape, F32)
        for shape in outs
    ]
    size = sum(value.size * value.dtype.itemsize for value in (*shapes, *inputs))
    smem = pl.BlockSpec(memory_space=pltpu.SMEM)
    vmem = pl.BlockSpec(memory_space=pltpu.VMEM)
    return pl.pallas_call(
        kernel,
        out_shape=shapes,
        in_specs=[smem] + [vmem] * (len(inputs) - 1),
        out_specs=[vmem] * len(shapes),
        scratch_shapes=[pltpu.VMEM(shape, F32) for shape in scratch],
        compiler_params=pltpu.CompilerParams(vmem_limit_bytes=VMEM_BYTES),
        cost_estimate=pl.CostEstimate(flops=flops, bytes_accessed=size, transcendentals=0),
        name=name,
    )(*inputs)


def shards_by_position(object_field, probe, positions, measured):
    strip = object_field.shape[1]
    width = object_field.shape[2]
    pattern = probe.shape[2]
    half = pattern // 2
    tiles = lax.axis_size("tile")
    size = (tiles, strip, pattern)
    field = (2, pattern, pattern)
    tall = (3 * pattern + strip + 8, width)
    window = (pattern + strip + 8, pattern)
    up = [(i, i + 1) for i in range(tiles - 1)]
    down = [(i + 1, i) for i in range(tiles - 1)]

    def swap(value):
        return lax.ppermute(value, "mode", [(0, 1), (1, 0)])

    def across(value, k):
        return lax.ppermute(value, "tile", [(i, i ^ k) for i in range(tiles)])

    def scatter(blocks, unit):
        mates = [across(blocks[k], unit * k) for k in range(1, GROUP)]
        return functools.reduce(jnp.add, mates, blocks[0])

    def exchange(piece, unit, pairwise):
        if pairwise:
            piece = piece + across(piece, unit)
            return piece + across(piece, 2 * unit)
        return scatter([piece] * GROUP, unit)

    def gather(piece, unit):
        return jnp.stack([piece] + [across(piece, unit * k) for k in range(1, GROUP)])

    def from_below(value):
        return lax.ppermute(value, "tile", up)

    def from_above(value):
        return lax.ppermute(value, "tile", down)

    def bind(kernel, *args):
        return functools.partial(kernel, *args)

    tile, slot = lax.axis_index("tile"), lax.axis_index("mode")
    index = jnp.stack([tile, slot]).astype(jnp.int32)
    here = jnp.concatenate([positions.ravel()] * 3 + [index])
    one_part = lax.dynamic_index_in_dim(object_field, slot, 0, keepdims=False)
    edges = [from_below(one_part[strip - half :]), from_above(one_part[:half])]
    below, above = from_below(positions), from_above(positions)
    other = swap(probe[0])
    own, observed, table = call(
        ready_kernel,
        "ready",
        [field, field, jax.ShapeDtypeStruct((4, pattern, pattern), BF16)],
        (here, probe[0], measured, jnp.asarray(table_of(pattern))),
    )
    *edges, below, above, own, observed, table = lax.optimization_barrier(
        (*edges, below, above, own, observed, table)
    )
    edges = [edges[0], swap(edges[0]), edges[1], swap(edges[1])]
    info = jnp.concatenate([below.ravel(), positions.ravel(), above.ravel(), index])

    for minibatch in range(2):
        last = minibatch == 1
        rows = pattern // GROUP
        blocks = (GROUP, 2 * rows + rows // 2, pattern)
        cut = (object_field, *edges)
        if last:
            cut = call(
                bind(patch_kernel, size, minibatch), "patch", [field], (here, *cut), [window], 10**10
            )
        rim = (2, half, pattern)
        gradient, top, bottom, step_own, step_other = call(
            bind(field_kernel, size, minibatch),
            "field",
            [field, rim, rim, blocks, blocks],
            (here, *cut, own, other, observed, table),
            [] if last else [window],
            flops=2 * 12 * 512**3,
        )
        (illum,) = call(
            bind(illumination_kernel, size, minibatch),
            "illumination",
            [(strip, width)],
            (info, own, other),
            [tall],
        )
        brought = swap(step_other)
        steps = [step_own[k] + brought[k] for k in range(GROUP)]
        piece = scatter(steps, 1)
        if last:
            gradient, top, bottom, piece, illum = lax.optimization_barrier(
                (gradient, top, bottom, piece, illum)
            )
        rim_below, rim_above = from_below(bottom), from_above(top)
        if not last:
            gradient, rim_below, rim_above, illum = lax.optimization_barrier(
                (gradient, rim_below, rim_above, illum)
            )
        rims = (gradient, swap(gradient), rim_below, rim_above, swap(rim_below), swap(rim_above))
        object_field, *edges = call(
            bind(update_kernel, size, minibatch),
            "update",
            [object_field.shape] + ([] if last else [rim] * 2),
            (info, object_field, illum, *rims),
            [tall],
            flops=0,
        )
        piece = exchange(piece, GROUP, last)
        if not last:
            edges = [from_below(edges[1]), from_above(edges[0])]
            piece, *edges = lax.optimization_barrier((piece, *edges))
        totals = gather(piece, 1)
        if last:
            totals, object_field = lax.optimization_barrier((totals, object_field))
            others = swap(totals[:, 2 * rows :])
            (own,) = call(probe_kernel, "probe", [field], (here, totals, others, own))
        else:
            own, other = call(
                probe_kernel, "probe", [field] * 2, (here, totals, swap(totals), own, other)
            )
    return (object_field, own[None])


def solution(mesh):
    in_specs = (
        P(None, "tile", None),
        P("mode", None, None, None),
        P(None, "tile", None),
        P(None, "tile", None, None),
    )
    out_specs = (P(None, "tile", None), P("mode", None, None, None))

    def whole(object_field, probe, positions, measured):
        tiles, pair = mesh.shape["tile"], mesh.shape["mode"]
        by_position = (
            pair == 2
            and probe.shape[0] == 2
            and positions.shape[:2] == (2, 2 * tiles)
            and tiles == GROUP * GROUP
            and probe.shape[2] % (16 * 2 * GROUP) == 0
            and object_field.shape[1] == tiles * probe.shape[2]
        )
        shards = shards_by_position if by_position else shards_by_mode
        return jax.shard_map(
            shards, mesh=mesh, in_specs=in_specs, out_specs=out_specs, check_vma=False
        )(object_field, probe, positions, measured)

    return whole
```

```python
import functools
import math

import jax
import jax.numpy as jnp
import numpy as np
from jax import lax
from jax.experimental import pallas as pl
from jax.experimental.pallas import tpu as pltpu
from jax.sharding import PartitionSpec as P

F32 = jnp.float32
BF16 = jnp.bfloat16
VMEM_BYTES = 16 * 1024 * 1024
GROUP = 4
UNITS = ((2, 1), (4, 8))


def padded(block, sides, width):
    for axis, dim in sides:
        count = lax.axis_size(axis)
        forward = [(i, i + 1) for i in range(count - 1)]
        backward = [(target, source) for source, target in forward]
        low = lax.ppermute(
            lax.slice_in_dim(block, block.shape[dim] - width, None, axis=dim), axis, forward
        )
        high = lax.ppermute(lax.slice_in_dim(block, 0, width, axis=dim), axis, backward)
        block = jnp.concatenate([low, block, high], axis=dim)
    return block


def tables(length):
    index_values = jnp.arange(length, dtype=jnp.int32)
    product = index_values[:, None] * index_values[None, :] % length
    angles = product.astype(jnp.float32) * (2.0 * math.pi / length)
    scaling = 1.0 / math.sqrt(length)
    return (jnp.cos(angles) * scaling, jnp.sin(angles) * scaling)


def apply_left(matrix, target):
    return jnp.einsum("ab,pbc->pac", matrix, target, precision=lax.Precision.HIGHEST)


def apply_right(target, matrix):
    return jnp.einsum("pab,bc->pac", target, matrix, precision=lax.Precision.HIGHEST)


def transform(real_part, imag_part, cosine, sine_table, direction):
    left_real = apply_left(cosine, real_part) + direction * apply_left(sine_table, imag_part)
    left_imag = apply_left(cosine, imag_part) - direction * apply_left(sine_table, real_part)
    out_real = apply_right(left_real, cosine) + direction * apply_right(left_imag, sine_table)
    out_imag = apply_right(left_imag, cosine) - direction * apply_right(left_real, sine_table)
    return (out_real, out_imag)


def place_add(target, placed, row_start, col_start):
    zero_index = jnp.int32(0)
    current = lax.dynamic_slice(target, (zero_index, row_start, col_start), placed.shape)
    return lax.dynamic_update_slice(target, current + placed, (zero_index, row_start, col_start))


def shards_by_mode(object_field, probe, positions, measured):
    strip_rows = object_field.shape[1]
    object_width = object_field.shape[2]
    pattern = probe.shape[2]
    half_pattern = pattern // 2
    count = positions.shape[1]
    cosine, sine_table = tables(pattern)
    tile_index = lax.axis_index("tile")
    offset = tile_index * strip_rows - half_pattern
    for minibatch in range(measured.shape[0]):
        extended = padded(object_field, (("tile", 1),), half_pattern)
        row_offsets = positions[minibatch, :, 0] - offset
        column_offsets = positions[minibatch, :, 1]

        def cut_one(row_start, col_start):
            return lax.dynamic_slice(
                extended, (jnp.int32(0), row_start, col_start), (2, pattern, pattern)
            )

        patches = jax.vmap(cut_one)(row_offsets, column_offsets)
        obj_real = patches[:, 0]
        obj_imag = patches[:, 1]
        probe_real = probe[0, 0]
        probe_imag = probe[0, 1]
        exit_real = probe_real * obj_real - probe_imag * obj_imag
        exit_imag = probe_real * obj_imag + probe_imag * obj_real
        far_real, far_imag = transform(exit_real, exit_imag, cosine, sine_table, 1.0)
        observed = measured[minibatch]
        intensity = lax.psum(far_real * far_real + far_imag * far_imag, "mode")
        modulus = jnp.sqrt((observed + 1.0) / (intensity + 1.0)) - 1.0
        chi_real, chi_imag = transform(
            modulus * far_real, modulus * far_imag, cosine, sine_table, -1.0
        )
        grad_real = probe_real * chi_real + probe_imag * chi_imag
        grad_imag = probe_real * chi_imag - probe_imag * chi_real
        probe_power = probe_real * probe_real + probe_imag * probe_imag
        step_real = jnp.sum(obj_real * chi_real + obj_imag * chi_imag, axis=0)
        step_imag = jnp.sum(obj_real * chi_imag - obj_imag * chi_real, axis=0)
        coverage = jnp.sum(obj_real * obj_real + obj_imag * obj_imag, axis=0)
        accumulated = jnp.zeros((3, strip_rows + pattern, object_width), jnp.float32)
        for position in range(count):
            placed = jnp.stack([grad_real[position], grad_imag[position], probe_power])
            accumulated = place_add(
                accumulated, placed, row_offsets[position], column_offsets[position]
            )
        rim_rows = jnp.concatenate(
            [accumulated[:, :half_pattern], accumulated[:, strip_rows + half_pattern :]], axis=1
        )
        received = padded(rim_rows, (("tile", 1),), half_pattern)
        own_strip = accumulated[:, half_pattern : half_pattern + strip_rows]
        own_strip = own_strip.at[:, :half_pattern].add(received[:, :half_pattern])
        own_strip = own_strip.at[:, strip_rows - half_pattern :].add(
            received[:, pattern + half_pattern :]
        )
        summed = lax.psum(own_strip, "mode")
        divisor = summed[2] + 1.0
        object_field = jnp.stack(
            [object_field[0] + summed[0] / divisor, object_field[1] + summed[1] / divisor]
        )
        step_stack = jnp.stack([jnp.stack([step_real, step_imag])])
        step_total, coverage_total = lax.psum((step_stack, coverage), "tile")
        probe = probe + step_total / (coverage_total + 1.0)
    return (object_field, probe)


def table_of(length):
    index_values = np.arange(length)
    angles = (index_values[:, None] * index_values[None, :] % length) * (2.0 * np.pi / length)
    scaling = 1.0 / np.sqrt(length)
    return np.stack([np.cos(angles) * scaling, np.sin(angles) * scaling]).astype(np.float32)


def spot(info, size, minibatch, side, slot):
    tiles, strip, pattern = size
    place = (((side + 1) * 2 + minibatch) * 2 + slot) * 2
    tile = info[24]
    row = info[place] - tile * strip + pattern // 2
    if side < 0:
        row = jnp.where(tile == 0, -pattern, row)
    if side > 0:
        row = jnp.where(tile == tiles - 1, strip + pattern, row)
    return row, info[place + 1]


def mates(tile):
    line = lax.div(tile, GROUP)
    return lax.rem(tile, GROUP), 2 * lax.rem(line, 2) + lax.div(line, 2)


def take_columns(block, column, width):
    total = block.shape[-1]
    return pltpu.roll(block, lax.rem(total - column, total), 1)[:, :width]


def add_at(tall, block, row, column):
    rows, width = block.shape
    total = tall.shape[1]
    shift = lax.rem(row, 8)
    start = pl.multiple_of(row - shift, 8)
    turned = pltpu.roll(block.reshape(rows // 8, 8, width), shift, 1)
    empty = jnp.zeros((1, 8, width), block.dtype)
    inside = lax.broadcasted_iota(jnp.int32, (rows // 8 + 1, 8, width), 1) >= shift
    moved = jnp.where(
        inside,
        jnp.concatenate([turned, empty], axis=0),
        jnp.concatenate([empty, turned], axis=0),
    ).reshape(rows + 8, width)
    wide = jnp.concatenate([moved, jnp.zeros((rows + 8, total - width), block.dtype)], axis=1)
    tall[pl.ds(start, rows + 8), :] += pltpu.roll(wide, column, 1)


def rows_at(ref, row, rows):
    width = ref.shape[1]
    shift = lax.rem(row, 8)
    start = pl.multiple_of(row - shift, 8)
    block = ref[pl.ds(start, rows + 8), :].reshape(rows // 8 + 1, 8, width)
    turned = pltpu.roll(block, lax.rem(8 - shift, 8), 1)
    inside = lax.broadcasted_iota(jnp.int32, (rows // 8, 8, width), 1) < 8 - shift
    return jnp.where(inside, turned[:-1], turned[1:]).reshape(rows, width)


def halves(value):
    high = value.astype(BF16)
    return high, (value - high.astype(F32)).astype(BF16)


def product(left, right):
    dot = functools.partial(jnp.dot, preferred_element_type=F32)
    return dot(left[0], right[0]) + (dot(left[0], right[1]) + dot(left[1], right[0]))


def cut_patch(size, info, minibatch, strip_ref, below, above, window, part):
    tiles, rows, width = size
    half = width // 2
    row, column = spot(info, size, minibatch, 0, info[25])

    def columns(block):
        return block if block.shape[1] == width else take_columns(block, column, width)

    window[:half] = columns(below)
    window[half : half + rows] = columns(strip_ref[part])
    window[half + rows : rows + width] = columns(above)
    return rows_at(window, row, width)


def illumination_kernel(size, minibatch, info, own, other, out, tall):
    tiles, strip, pattern = size
    half = pattern // 2
    kept = slice(pattern + half, pattern + half + strip)
    tall[kept] = jnp.zeros((strip, tall.shape[1]), F32)
    (pr0, pi0), (pr1, pi1) = ((ref[0], ref[1]) for ref in (own, other))
    power = pr0 * pr0 + pi0 * pi0 + (pr1 * pr1 + pi1 * pi1)
    for side in (-1, 0, 1):
        for slot in range(2):
            row, column = spot(info, size, minibatch, side, slot)
            add_at(tall, power, row + pattern, column)
    out[...] = tall[kept]


def patch_kernel(size, minibatch, info, strip_ref, below, above, patch, window):
    for part in range(2):
        patch[part] = cut_patch(
            size, info, minibatch, strip_ref, below[part], above[part], window, part
        )


def ready_kernel(info, probe, measured, table, own, observed, split):
    own[...] = probe[...]
    for minibatch in range(2):
        observed[minibatch] = measured[minibatch, info[25]]
    for i in range(2):
        split[2 * i], split[2 * i + 1] = halves(table[i])


def field_kernel(size, minibatch, info, strip_ref, *refs):
    tiles, strip, pattern = size
    slot = info[25]
    if minibatch:
        own, other, measured, table, gradient, top, bottom, step_own, step_other = refs
        obj_real, obj_imag = strip_ref[0], strip_ref[1]
    else:
        *edges, own, other, measured, table = refs[:-6]
        gradient, top, bottom, step_own, step_other, window = refs[-6:]
        sides = (jnp.where(slot == 0, edges[i][...], edges[i + 1][...]) for i in (0, 2))
        others = (jnp.where(slot == 0, edges[i + 1][...], edges[i][...]) for i in (0, 2))
        obj_real, obj_imag = (
            cut_patch(size, info, minibatch, strip_ref, *ends, window, part)
            for part, ends in enumerate((sides, others))
        )
    cos_high, cos_low, sin_high, sin_low = (table[i] for i in range(4))

    def block(top_left, top_right, low_left, low_right):
        return jnp.concatenate(
            [
                jnp.concatenate([top_left, top_right], axis=1),
                jnp.concatenate([low_left, low_right], axis=1),
            ],
            axis=0,
        )

    first = (
        block(cos_high, sin_high, -sin_high, cos_high),
        block(cos_low, sin_low, -sin_low, cos_low),
    )
    second = (
        block(cos_high, -sin_high, sin_high, cos_high),
        block(cos_low, -sin_low, sin_low, cos_low),
    )
    probes = [(ref[0], ref[1]) for ref in (own, other)]

    def both(fields, left, right):
        (r0, i0), (r1, i1) = fields
        y = product(left, halves(block(r0, r1, i0, i1)))
        y = block(
            y[:pattern, :pattern], y[pattern:, :pattern], y[:pattern, pattern:], y[pattern:, pattern:]
        )
        y = product(halves(y), right)
        return (
            (y[:pattern, :pattern], y[:pattern, pattern:]),
            (y[pattern:, :pattern], y[pattern:, pattern:]),
        )

    exits = [(pr * obj_real - pi * obj_imag, pr * obj_imag + pi * obj_real) for pr, pi in probes]
    far = both(exits, first, second)
    intensity = (far[0][0] * far[0][0] + far[0][1] * far[0][1]) + (
        far[1][0] * far[1][0] + far[1][1] * far[1][1]
    )
    factor = jnp.sqrt((measured[minibatch] + 1.0) / (intensity + 1.0)) - 1.0
    chi = both([(factor * fr, factor * fi) for fr, fi in far], second, first)
    (pr0, pi0), (pr1, pi1) = probes
    (cr0, ci0), (cr1, ci1) = chi
    half = top.shape[1]
    for part, value in (
        (0, (pr0 * cr0 + pi0 * ci0) + (pr1 * cr1 + pi1 * ci1)),
        (1, (pr0 * ci0 - pi0 * cr0) + (pr1 * ci1 - pi1 * cr1)),
    ):
        gradient[part], top[part], bottom[part] = value, value[:half], value[half:]
    coverage = obj_real * obj_real + obj_imag * obj_imag
    rows = pattern // (2 * GROUP)
    for step, keeper, (cr, ci) in ((step_own, slot, chi[0]), (step_other, 1 - slot, chi[1])):
        real = obj_real * cr + obj_imag * ci
        imag = obj_real * ci - obj_imag * cr
        for which, mate in enumerate(mates(info[24])):
            for k in range(GROUP):
                start = (which * GROUP + k) * rows
                block = step.at[which, mate ^ k]
                block[:rows] = real[start : start + rows]
                block[rows : 2 * rows] = imag[start : start + rows]
                middle = start + rows // 2
                block[2 * rows :] = jnp.where(
                    keeper == 0, coverage[start:middle], coverage[middle : start + rows]
                )


def update_kernel(size, minibatch, info, strip_ref, illum, own, other, b0, a0, b1, a1, *outs):
    strip_out, *edges, tall = outs
    tiles, strip, pattern = size
    half = pattern // 2
    slot = info[25]
    kept = slice(pattern + half, pattern + half + strip)
    grads = (
        (0, slot, own, 0),
        (0, 1 - slot, other, 0),
        (-1, slot, b0, half),
        (1, slot, a0, 0),
        (-1, 1 - slot, b1, half),
        (1, 1 - slot, a1, 0),
    )
    for part in range(2):
        tall[kept] = jnp.zeros((strip, tall.shape[1]), F32)
        for side, place, ref, start in grads:
            row, column = spot(info, size, minibatch, side, place)
            add_at(tall, ref[part], row + pattern + start, column)
        fresh = strip_ref[part] + tall[kept] / (illum[...] + 1.0)
        strip_out[part] = fresh
        if edges:
            column_below = spot(info, size, minibatch + 1, -1, slot)[1]
            column_above = spot(info, size, minibatch + 1, 1, slot)[1]
            edges[0][part] = take_columns(fresh[:half], column_below, pattern)
            edges[1][part] = take_columns(fresh[strip - half :], column_above, pattern)


def probe_kernel(info, own_totals, other_totals, *refs):
    probes, outs = refs[: len(refs) // 2], refs[len(refs) // 2 :]
    slot = info[25]
    rows = outs[0].shape[1] // (2 * GROUP)
    for which, mate in enumerate(mates(info[24])):
        for k in range(GROUP):
            start = which * GROUP * rows + pl.multiple_of((mate ^ k) * rows, rows)
            where = pl.ds(start, rows)
            mine, theirs = own_totals[which, k], other_totals[which, k]
            own_half, other_half = mine[2 * rows :], theirs[theirs.shape[0] - rows // 2 :]
            coverage = jnp.concatenate(
                [
                    jnp.where(slot == 0, own_half, other_half),
                    jnp.where(slot == 0, other_half, own_half),
                ],
                axis=0,
            )
            divisor = coverage + 1.0
            for totals, probe, out in zip((mine, theirs), probes, outs):
                for part in range(2):
                    change = totals[part * rows : (part + 1) * rows] / divisor
                    out[part, where, :] = probe[part, where, :] + change


def call(kernel, name, outs, inputs, scratch=(), flops=0):
    shapes = [
        shape if isinstance(shape, jax.ShapeDtypeStruct) else jax.ShapeDtypeStruct(shape, F32)
        for shape in outs
    ]
    size = sum(value.size * value.dtype.itemsize for value in (*shapes, *inputs))
    smem = pl.BlockSpec(memory_space=pltpu.SMEM)
    vmem = pl.BlockSpec(memory_space=pltpu.VMEM)
    return pl.pallas_call(
        kernel,
        out_shape=shapes,
        in_specs=[smem] + [vmem] * (len(inputs) - 1),
        out_specs=[vmem] * len(shapes),
        scratch_shapes=[pltpu.VMEM(shape, F32) for shape in scratch],
        compiler_params=pltpu.CompilerParams(vmem_limit_bytes=VMEM_BYTES),
        cost_estimate=pl.CostEstimate(flops=flops, bytes_accessed=size, transcendentals=0),
        name=name,
    )(*inputs)


def shards_by_position(object_field, probe, positions, measured):
    strip = object_field.shape[1]
    width = object_field.shape[2]
    pattern = probe.shape[2]
    half = pattern // 2
    tiles = lax.axis_size("tile")
    size = (tiles, strip, pattern)
    field = (2, pattern, pattern)
    tall = (3 * pattern + strip + 8, width)
    window = (pattern + strip + 8, pattern)
    up = [(i, i + 1) for i in range(tiles - 1)]
    down = [(i + 1, i) for i in range(tiles - 1)]

    def swap(value):
        return lax.ppermute(value, "mode", [(0, 1), (1, 0)])

    def across(value, k):
        return lax.ppermute(value, "tile", [(i, i ^ k) for i in range(tiles)])

    def halve(kept, sent, units):
        pair = kept + across(sent, units[0])
        return pair[0] + across(pair[1], units[1])

    def exchange(piece, units):
        for unit in units:
            piece = piece + across(piece, unit)
        return piece

    def double(block, unit):
        return jnp.concatenate([block, across(block, unit)])

    def from_below(value):
        return lax.ppermute(value, "tile", up)

    def from_above(value):
        return lax.ppermute(value, "tile", down)

    def bind(kernel, *args):
        return functools.partial(kernel, *args)

    tile, slot = lax.axis_index("tile"), lax.axis_index("mode")
    index = jnp.stack([tile, slot]).astype(jnp.int32)
    here = jnp.concatenate([positions.ravel()] * 3 + [index])
    one_part = lax.dynamic_index_in_dim(object_field, slot, 0, keepdims=False)
    edges = [from_below(one_part[strip - half :]), from_above(one_part[:half])]
    below, above = from_below(positions), from_above(positions)
    other = swap(probe[0])
    own, observed, table = call(
        ready_kernel,
        "ready",
        [field, field, jax.ShapeDtypeStruct((4, pattern, pattern), BF16)],
        (here, probe[0], measured, jnp.asarray(table_of(pattern))),
    )
    *edges, below, above, own, observed, table = lax.optimization_barrier(
        (*edges, below, above, own, observed, table)
    )
    edges = [edges[0], swap(edges[0]), edges[1], swap(edges[1])]
    info = jnp.concatenate([below.ravel(), positions.ravel(), above.ravel(), index])

    for minibatch in range(2):
        last = minibatch == 1
        rows = pattern // (2 * GROUP)
        blocks = (2, GROUP, 2 * rows + rows // 2, pattern)
        cut = (object_field, *edges)
        if last:
            cut = call(
                bind(patch_kernel, size, minibatch), "patch", [field], (here, *cut), [window], 10**10
            )
        rim = (2, half, pattern)
        gradient, top, bottom, step_own, step_other = call(
            bind(field_kernel, size, minibatch),
            "field",
            [field, rim, rim, blocks, blocks],
            (here, *cut, own, other, observed, table),
            [] if last else [window],
            flops=2 * 12 * 512**3,
        )
        (illum,) = call(
            bind(illumination_kernel, size, minibatch),
            "illumination",
            [(strip, width)],
            (info, own, other),
            [tall],
        )
        brought = swap(step_other)
        kept, sent = ([step_own[i, at] + brought[i, at] for i in range(2)] for at in (slice(2), slice(2, 4)))
        pieces = [halve(kept[i], sent[i], UNITS[i]) for i in range(2)]
        if last:
            gradient, top, bottom, illum, pieces[0] = lax.optimization_barrier(
                (gradient, top, bottom, illum, pieces[0])
            )
        rim_below, rim_above = from_below(bottom), from_above(top)
        if not last:
            gradient, rim_below, rim_above, illum = lax.optimization_barrier(
                (gradient, rim_below, rim_above, illum)
            )
        pieces = [exchange(pieces[i], UNITS[1 - i])[None] for i in range(2)]
        if last:
            rim_below, rim_above, *pieces = lax.optimization_barrier(
                (rim_below, rim_above, *pieces)
            )
        rims = (gradient, swap(gradient), rim_below, rim_above, swap(rim_below), swap(rim_above))
        object_field, *edges = call(
            bind(update_kernel, size, minibatch),
            "update",
            [object_field.shape] + ([] if last else [rim] * 2),
            (info, object_field, illum, *rims),
            [tall],
        )
        pieces = [double(pieces[i], UNITS[i][1]) for i in range(2)]
        if not last:
            pieces_and_edges = (*pieces, from_below(edges[1]), from_above(edges[0]))
            *pieces, edge_below, edge_above = lax.optimization_barrier(pieces_and_edges)
            edges = [edge_below, edge_above]
        totals = jnp.stack([double(pieces[i], UNITS[i][0]) for i in range(2)])
        if last:
            totals, object_field = lax.optimization_barrier((totals, object_field))
            others = swap(totals[:, :, 2 * rows :])
            (own,) = call(probe_kernel, "probe", [field], (here, totals, others, own))
        else:
            own, other = call(
                probe_kernel, "probe", [field] * 2, (here, totals, swap(totals), own, other)
            )
    return (object_field, own[None])


def solution(mesh):
    in_specs = (
        P(None, "tile", None),
        P("mode", None, None, None),
        P(None, "tile", None),
        P(None, "tile", None, None),
    )
    out_specs = (P(None, "tile", None), P("mode", None, None, None))

    def whole(object_field, probe, positions, measured):
        tiles, pair = mesh.shape["tile"], mesh.shape["mode"]
        by_position = (
            pair == 2
            and probe.shape[0] == 2
            and positions.shape[:2] == (2, 2 * tiles)
            and tiles == GROUP * GROUP
            and probe.shape[2] % (16 * 2 * GROUP) == 0
            and object_field.shape[1] == tiles * probe.shape[2]
        )
        shards = shards_by_position if by_position else shards_by_mode
        return jax.shard_map(
            shards, mesh=mesh, in_specs=in_specs, out_specs=out_specs, check_vma=False
        )(object_field, probe, positions, measured)

    return whole
```

```python
import functools
import math

import jax
import jax.numpy as jnp
import numpy as np
from jax import lax
from jax.experimental import pallas as pl
from jax.experimental.pallas import tpu as pltpu
from jax.sharding import PartitionSpec as P

F32 = jnp.float32
BF16 = jnp.bfloat16
VMEM_BYTES = 16 * 1024 * 1024
GROUP = 4
NEAR_STEP = 2
FAR_STEPS = (1, 8, 9)


def padded(block, sides, width):
    for axis, dim in sides:
        count = lax.axis_size(axis)
        forward = [(i, i + 1) for i in range(count - 1)]
        backward = [(target, source) for source, target in forward]
        low = lax.ppermute(
            lax.slice_in_dim(block, block.shape[dim] - width, None, axis=dim), axis, forward
        )
        high = lax.ppermute(lax.slice_in_dim(block, 0, width, axis=dim), axis, backward)
        block = jnp.concatenate([low, block, high], axis=dim)
    return block


def tables(length):
    index_values = jnp.arange(length, dtype=jnp.int32)
    product = index_values[:, None] * index_values[None, :] % length
    angles = product.astype(jnp.float32) * (2.0 * math.pi / length)
    scaling = 1.0 / math.sqrt(length)
    return (jnp.cos(angles) * scaling, jnp.sin(angles) * scaling)


def apply_left(matrix, target):
    return jnp.einsum("ab,pbc->pac", matrix, target, precision=lax.Precision.HIGHEST)


def apply_right(target, matrix):
    return jnp.einsum("pab,bc->pac", target, matrix, precision=lax.Precision.HIGHEST)


def transform(real_part, imag_part, cosine, sine_table, direction):
    left_real = apply_left(cosine, real_part) + direction * apply_left(sine_table, imag_part)
    left_imag = apply_left(cosine, imag_part) - direction * apply_left(sine_table, real_part)
    out_real = apply_right(left_real, cosine) + direction * apply_right(left_imag, sine_table)
    out_imag = apply_right(left_imag, cosine) - direction * apply_right(left_real, sine_table)
    return (out_real, out_imag)


def place_add(target, placed, row_start, col_start):
    zero_index = jnp.int32(0)
    current = lax.dynamic_slice(target, (zero_index, row_start, col_start), placed.shape)
    return lax.dynamic_update_slice(target, current + placed, (zero_index, row_start, col_start))


def shards_by_mode(object_field, probe, positions, measured):
    strip_rows = object_field.shape[1]
    object_width = object_field.shape[2]
    pattern = probe.shape[2]
    half_pattern = pattern // 2
    count = positions.shape[1]
    cosine, sine_table = tables(pattern)
    tile_index = lax.axis_index("tile")
    offset = tile_index * strip_rows - half_pattern
    for minibatch in range(measured.shape[0]):
        extended = padded(object_field, (("tile", 1),), half_pattern)
        row_offsets = positions[minibatch, :, 0] - offset
        column_offsets = positions[minibatch, :, 1]

        def cut_one(row_start, col_start):
            return lax.dynamic_slice(
                extended, (jnp.int32(0), row_start, col_start), (2, pattern, pattern)
            )

        patches = jax.vmap(cut_one)(row_offsets, column_offsets)
        obj_real = patches[:, 0]
        obj_imag = patches[:, 1]
        probe_real = probe[0, 0]
        probe_imag = probe[0, 1]
        exit_real = probe_real * obj_real - probe_imag * obj_imag
        exit_imag = probe_real * obj_imag + probe_imag * obj_real
        far_real, far_imag = transform(exit_real, exit_imag, cosine, sine_table, 1.0)
        observed = measured[minibatch]
        intensity = lax.psum(far_real * far_real + far_imag * far_imag, "mode")
        modulus = jnp.sqrt((observed + 1.0) / (intensity + 1.0)) - 1.0
        chi_real, chi_imag = transform(
            modulus * far_real, modulus * far_imag, cosine, sine_table, -1.0
        )
        grad_real = probe_real * chi_real + probe_imag * chi_imag
        grad_imag = probe_real * chi_imag - probe_imag * chi_real
        probe_power = probe_real * probe_real + probe_imag * probe_imag
        step_real = jnp.sum(obj_real * chi_real + obj_imag * chi_imag, axis=0)
        step_imag = jnp.sum(obj_real * chi_imag - obj_imag * chi_real, axis=0)
        coverage = jnp.sum(obj_real * obj_real + obj_imag * obj_imag, axis=0)
        accumulated = jnp.zeros((3, strip_rows + pattern, object_width), jnp.float32)
        for position in range(count):
            placed = jnp.stack([grad_real[position], grad_imag[position], probe_power])
            accumulated = place_add(
                accumulated, placed, row_offsets[position], column_offsets[position]
            )
        rim_rows = jnp.concatenate(
            [accumulated[:, :half_pattern], accumulated[:, strip_rows + half_pattern :]], axis=1
        )
        received = padded(rim_rows, (("tile", 1),), half_pattern)
        own_strip = accumulated[:, half_pattern : half_pattern + strip_rows]
        own_strip = own_strip.at[:, :half_pattern].add(received[:, :half_pattern])
        own_strip = own_strip.at[:, strip_rows - half_pattern :].add(
            received[:, pattern + half_pattern :]
        )
        summed = lax.psum(own_strip, "mode")
        divisor = summed[2] + 1.0
        object_field = jnp.stack(
            [object_field[0] + summed[0] / divisor, object_field[1] + summed[1] / divisor]
        )
        step_stack = jnp.stack([jnp.stack([step_real, step_imag])])
        step_total, coverage_total = lax.psum((step_stack, coverage), "tile")
        probe = probe + step_total / (coverage_total + 1.0)
    return (object_field, probe)


def table_of(length):
    index_values = np.arange(length)
    angles = (index_values[:, None] * index_values[None, :] % length) * (2.0 * np.pi / length)
    scaling = 1.0 / np.sqrt(length)
    return np.stack([np.cos(angles) * scaling, np.sin(angles) * scaling]).astype(np.float32)


def spot(info, size, minibatch, side, slot):
    tiles, strip, pattern = size
    place = (((side + 1) * 2 + minibatch) * 2 + slot) * 2
    tile = info[24]
    row = info[place] - tile * strip + pattern // 2
    if side < 0:
        row = jnp.where(tile == 0, -pattern, row)
    if side > 0:
        row = jnp.where(tile == tiles - 1, strip + pattern, row)
    return row, info[place + 1]


def take_columns(block, column, width):
    total = block.shape[-1]
    return pltpu.roll(block, lax.rem(total - column, total), 1)[:, :width]


def add_at(tall, block, row, column):
    rows, width = block.shape
    total = tall.shape[1]
    shift = lax.rem(row, 8)
    start = pl.multiple_of(row - shift, 8)
    turned = pltpu.roll(block.reshape(rows // 8, 8, width), shift, 1)
    empty = jnp.zeros((1, 8, width), block.dtype)
    inside = lax.broadcasted_iota(jnp.int32, (rows // 8 + 1, 8, width), 1) >= shift
    moved = jnp.where(
        inside,
        jnp.concatenate([turned, empty], axis=0),
        jnp.concatenate([empty, turned], axis=0),
    ).reshape(rows + 8, width)
    wide = jnp.concatenate([moved, jnp.zeros((rows + 8, total - width), block.dtype)], axis=1)
    tall[pl.ds(start, rows + 8), :] += pltpu.roll(wide, column, 1)


def rows_at(ref, row, rows):
    width = ref.shape[1]
    shift = lax.rem(row, 8)
    start = pl.multiple_of(row - shift, 8)
    block = ref[pl.ds(start, rows + 8), :].reshape(rows // 8 + 1, 8, width)
    turned = pltpu.roll(block, lax.rem(8 - shift, 8), 1)
    inside = lax.broadcasted_iota(jnp.int32, (rows // 8, 8, width), 1) < 8 - shift
    return jnp.where(inside, turned[:-1], turned[1:]).reshape(rows, width)


def halves(value):
    high = value.astype(BF16)
    return high, (value - high.astype(F32)).astype(BF16)


def product(left, right):
    dot = functools.partial(jnp.dot, preferred_element_type=F32)
    return dot(left[0], right[0]) + (dot(left[0], right[1]) + dot(left[1], right[0]))


def cut_patch(size, info, minibatch, strip_ref, below, above, window, part):
    tiles, rows, width = size
    half = width // 2
    row, column = spot(info, size, minibatch, 0, info[25])

    def columns(block):
        return block if block.shape[1] == width else take_columns(block, column, width)

    window[:half] = columns(below)
    window[half : half + rows] = columns(strip_ref[part])
    window[half + rows : rows + width] = columns(above)
    return rows_at(window, row, width)


def illumination_kernel(size, minibatch, info, own, other, out, tall):
    tiles, strip, pattern = size
    half = pattern // 2
    kept = slice(pattern + half, pattern + half + strip)
    tall[kept] = jnp.zeros((strip, tall.shape[1]), F32)
    (pr0, pi0), (pr1, pi1) = ((ref[0], ref[1]) for ref in (own, other))
    power = pr0 * pr0 + pi0 * pi0 + (pr1 * pr1 + pi1 * pi1)
    for side in (-1, 0, 1):
        for slot in range(2):
            row, column = spot(info, size, minibatch, side, slot)
            add_at(tall, power, row + pattern, column)
    out[...] = tall[kept]


def patch_kernel(size, minibatch, info, strip_ref, below, above, patch, window):
    for part in range(2):
        patch[part] = cut_patch(
            size, info, minibatch, strip_ref, below[part], above[part], window, part
        )


def ready_kernel(info, probe, measured, table, own, observed, split):
    own[...] = probe[...]
    for minibatch in range(2):
        observed[minibatch] = measured[minibatch, info[25]]
    for i in range(2):
        split[2 * i], split[2 * i + 1] = halves(table[i])


def field_kernel(size, minibatch, info, strip_ref, *refs):
    tiles, strip, pattern = size
    slot = info[25]
    if minibatch:
        own, other, measured, table, gradient, top, bottom, step_own, step_other = refs
        obj_real, obj_imag = strip_ref[0], strip_ref[1]
    else:
        *edges, own, other, measured, table = refs[:-6]
        gradient, top, bottom, step_own, step_other, window = refs[-6:]
        sides = (jnp.where(slot == 0, edges[i][...], edges[i + 1][...]) for i in (0, 2))
        others = (jnp.where(slot == 0, edges[i + 1][...], edges[i][...]) for i in (0, 2))
        obj_real, obj_imag = (
            cut_patch(size, info, minibatch, strip_ref, *ends, window, part)
            for part, ends in enumerate((sides, others))
        )
    cos_high, cos_low, sin_high, sin_low = (table[i] for i in range(4))

    def block(top_left, top_right, low_left, low_right):
        return jnp.concatenate(
            [
                jnp.concatenate([top_left, top_right], axis=1),
                jnp.concatenate([low_left, low_right], axis=1),
            ],
            axis=0,
        )

    first = (
        block(cos_high, sin_high, -sin_high, cos_high),
        block(cos_low, sin_low, -sin_low, cos_low),
    )
    second = (
        block(cos_high, -sin_high, sin_high, cos_high),
        block(cos_low, -sin_low, sin_low, cos_low),
    )
    probes = [(ref[0], ref[1]) for ref in (own, other)]

    def both(fields, left, right):
        (r0, i0), (r1, i1) = fields
        y = product(left, halves(block(r0, r1, i0, i1)))
        y = block(
            y[:pattern, :pattern], y[pattern:, :pattern], y[:pattern, pattern:], y[pattern:, pattern:]
        )
        y = product(halves(y), right)
        return (
            (y[:pattern, :pattern], y[:pattern, pattern:]),
            (y[pattern:, :pattern], y[pattern:, pattern:]),
        )

    exits = [(pr * obj_real - pi * obj_imag, pr * obj_imag + pi * obj_real) for pr, pi in probes]
    far = both(exits, first, second)
    intensity = (far[0][0] * far[0][0] + far[0][1] * far[0][1]) + (
        far[1][0] * far[1][0] + far[1][1] * far[1][1]
    )
    factor = jnp.sqrt((measured[minibatch] + 1.0) / (intensity + 1.0)) - 1.0
    chi = both([(factor * fr, factor * fi) for fr, fi in far], second, first)
    (pr0, pi0), (pr1, pi1) = probes
    (cr0, ci0), (cr1, ci1) = chi
    half = top.shape[1]
    for part, value in (
        (0, (pr0 * cr0 + pi0 * ci0) + (pr1 * cr1 + pi1 * ci1)),
        (1, (pr0 * ci0 - pi0 * cr0) + (pr1 * ci1 - pi1 * cr1)),
    ):
        gradient[part], top[part], bottom[part] = value, value[:half], value[half:]
    coverage = obj_real * obj_real + obj_imag * obj_imag
    rows = pattern // GROUP
    mate = lax.rem(lax.div(info[24], NEAR_STEP), GROUP)
    for step, keeper, (cr, ci) in ((step_own, slot, chi[0]), (step_other, 1 - slot, chi[1])):
        real = obj_real * cr + obj_imag * ci
        imag = obj_real * ci - obj_imag * cr
        for k in range(GROUP):
            start = k * rows
            block = step.at[mate ^ k]
            block[:rows] = real[start : start + rows]
            block[rows : 2 * rows] = imag[start : start + rows]
            middle = start + rows // 2
            block[2 * rows :] = jnp.where(
                keeper == 0, coverage[start:middle], coverage[middle : start + rows]
            )


def update_kernel(size, minibatch, info, strip_ref, illum, own, other, b0, a0, b1, a1, *outs):
    strip_out, *edges, tall = outs
    tiles, strip, pattern = size
    half = pattern // 2
    slot = info[25]
    kept = slice(pattern + half, pattern + half + strip)
    grads = (
        (0, slot, own, 0),
        (0, 1 - slot, other, 0),
        (-1, slot, b0, half),
        (1, slot, a0, 0),
        (-1, 1 - slot, b1, half),
        (1, 1 - slot, a1, 0),
    )
    for part in range(2):
        tall[kept] = jnp.zeros((strip, tall.shape[1]), F32)
        for side, place, ref, start in grads:
            row, column = spot(info, size, minibatch, side, place)
            add_at(tall, ref[part], row + pattern + start, column)
        fresh = strip_ref[part] + tall[kept] / (illum[...] + 1.0)
        strip_out[part] = fresh
        if edges:
            column_below = spot(info, size, minibatch + 1, -1, slot)[1]
            column_above = spot(info, size, minibatch + 1, 1, slot)[1]
            edges[0][part] = take_columns(fresh[:half], column_below, pattern)
            edges[1][part] = take_columns(fresh[strip - half :], column_above, pattern)


def probe_kernel(info, own_totals, other_totals, *refs):
    probes, outs = refs[: len(refs) // 2], refs[len(refs) // 2 :]
    slot = info[25]
    rows = outs[0].shape[1] // GROUP
    mate = lax.rem(lax.div(info[24], NEAR_STEP), GROUP)
    for k in range(GROUP):
        where = pl.ds(pl.multiple_of((mate ^ k) * rows, rows), rows)
        mine, theirs = own_totals[k], other_totals[k]
        own_half, other_half = mine[2 * rows :], theirs[theirs.shape[0] - rows // 2 :]
        coverage = jnp.concatenate(
            [
                jnp.where(slot == 0, own_half, other_half),
                jnp.where(slot == 0, other_half, own_half),
            ],
            axis=0,
        )
        divisor = coverage + 1.0
        for totals, probe, out in zip((mine, theirs), probes, outs):
            for part in range(2):
                change = totals[part * rows : (part + 1) * rows] / divisor
                out[part, where, :] = probe[part, where, :] + change


def call(kernel, name, outs, inputs, scratch=(), flops=0):
    shapes = [
        shape if isinstance(shape, jax.ShapeDtypeStruct) else jax.ShapeDtypeStruct(shape, F32)
        for shape in outs
    ]
    size = sum(value.size * value.dtype.itemsize for value in (*shapes, *inputs))
    smem = pl.BlockSpec(memory_space=pltpu.SMEM)
    vmem = pl.BlockSpec(memory_space=pltpu.VMEM)
    return pl.pallas_call(
        kernel,
        out_shape=shapes,
        in_specs=[smem] + [vmem] * (len(inputs) - 1),
        out_specs=[vmem] * len(shapes),
        scratch_shapes=[pltpu.VMEM(shape, F32) for shape in scratch],
        compiler_params=pltpu.CompilerParams(vmem_limit_bytes=VMEM_BYTES),
        cost_estimate=pl.CostEstimate(flops=flops, bytes_accessed=size, transcendentals=0),
        name=name,
    )(*inputs)


def shards_by_position(object_field, probe, positions, measured):
    strip = object_field.shape[1]
    width = object_field.shape[2]
    pattern = probe.shape[2]
    half = pattern // 2
    tiles = lax.axis_size("tile")
    size = (tiles, strip, pattern)
    field = (2, pattern, pattern)
    tall = (3 * pattern + strip + 8, width)
    window = (pattern + strip + 8, pattern)
    up = [(i, i + 1) for i in range(tiles - 1)]
    down = [(i + 1, i) for i in range(tiles - 1)]

    def swap(value):
        return lax.ppermute(value, "mode", [(0, 1), (1, 0)])

    def across(value, k):
        return lax.ppermute(value, "tile", [(i, i ^ k) for i in range(tiles)])

    def scatter(blocks, unit):
        mates = [across(blocks[k], unit * k) for k in range(1, GROUP)]
        return functools.reduce(jnp.add, mates, blocks[0])

    def exchange(piece):
        first, second, third = (across(piece, steps) for steps in FAR_STEPS)
        return (piece + first) + (second + third)

    def gather(piece, unit):
        return jnp.stack([piece] + [across(piece, unit * k) for k in range(1, GROUP)])

    def from_below(value):
        return lax.ppermute(value, "tile", up)

    def from_above(value):
        return lax.ppermute(value, "tile", down)

    def bind(kernel, *args):
        return functools.partial(kernel, *args)

    tile, slot = lax.axis_index("tile"), lax.axis_index("mode")
    index = jnp.stack([tile, slot]).astype(jnp.int32)
    here = jnp.concatenate([positions.ravel()] * 3 + [index])
    one_part = lax.dynamic_index_in_dim(object_field, slot, 0, keepdims=False)
    edges = [from_below(one_part[strip - half :]), from_above(one_part[:half])]
    below, above = from_below(positions), from_above(positions)
    other = swap(probe[0])
    own, observed, table = call(
        ready_kernel,
        "ready",
        [field, field, jax.ShapeDtypeStruct((4, pattern, pattern), BF16)],
        (here, probe[0], measured, jnp.asarray(table_of(pattern))),
    )
    *edges, below, above, own, observed, table = lax.optimization_barrier(
        (*edges, below, above, own, observed, table)
    )
    edges = [edges[0], swap(edges[0]), edges[1], swap(edges[1])]
    info = jnp.concatenate([below.ravel(), positions.ravel(), above.ravel(), index])

    for minibatch in range(2):
        last = minibatch == 1
        rows = pattern // GROUP
        blocks = (GROUP, 2 * rows + rows // 2, pattern)
        cut = (object_field, *edges)
        if last:
            cut = call(
                bind(patch_kernel, size, minibatch), "patch", [field], (here, *cut), [window], 10**10
            )
        rim = (2, half, pattern)
        gradient, top, bottom, step_own, step_other = call(
            bind(field_kernel, size, minibatch),
            "field",
            [field, rim, rim, blocks, blocks],
            (here, *cut, own, other, observed, table),
            [] if last else [window],
            flops=2 * 12 * 512**3,
        )
        (illum,) = call(
            bind(illumination_kernel, size, minibatch),
            "illumination",
            [(strip, width)],
            (info, own, other),
            [tall],
        )
        brought = swap(step_other)
        steps = [step_own[k] + brought[k] for k in range(GROUP)]
        piece = scatter(steps, NEAR_STEP)
        rim_below, rim_above = from_below(bottom), from_above(top)
        gradient, rim_below, rim_above, illum = lax.optimization_barrier(
            (gradient, rim_below, rim_above, illum)
        )
        rims = (gradient, swap(gradient), rim_below, rim_above, swap(rim_below), swap(rim_above))
        object_field, *edges = call(
            bind(update_kernel, size, minibatch),
            "update",
            [object_field.shape] + ([] if last else [rim] * 2),
            (info, object_field, illum, *rims),
            [tall],
        )
        piece = exchange(piece)
        if not last:
            edges = [from_below(edges[1]), from_above(edges[0])]
            piece, *edges = lax.optimization_barrier((piece, *edges))
        totals = gather(piece, NEAR_STEP)
        if last:
            totals, object_field = lax.optimization_barrier((totals, object_field))
            others = swap(totals[:, 2 * rows :])
            (own,) = call(probe_kernel, "probe", [field], (here, totals, others, own))
        else:
            own, other = call(
                probe_kernel, "probe", [field] * 2, (here, totals, swap(totals), own, other)
            )
    return (object_field, own[None])


def solution(mesh):
    in_specs = (
        P(None, "tile", None),
        P("mode", None, None, None),
        P(None, "tile", None),
        P(None, "tile", None, None),
    )
    out_specs = (P(None, "tile", None), P("mode", None, None, None))

    def whole(object_field, probe, positions, measured):
        tiles, pair = mesh.shape["tile"], mesh.shape["mode"]
        by_position = (
            pair == 2
            and probe.shape[0] == 2
            and positions.shape[:2] == (2, 2 * tiles)
            and tiles == GROUP * GROUP
            and probe.shape[2] % (16 * 2 * GROUP) == 0
            and object_field.shape[1] == tiles * probe.shape[2]
        )
        shards = shards_by_position if by_position else shards_by_mode
        return jax.shard_map(
            shards, mesh=mesh, in_specs=in_specs, out_specs=out_specs, check_vma=False
        )(object_field, probe, positions, measured)

    return whole
```

```python
import functools
import math

import jax
import jax.numpy as jnp
import numpy as np
from jax import lax
from jax.experimental import pallas as pl
from jax.experimental.pallas import tpu as pltpu
from jax.sharding import PartitionSpec as P

F32 = jnp.float32
BF16 = jnp.bfloat16
VMEM_BYTES = 16 * 1024 * 1024
GROUP = 4
NEAR_STEP = 2
FAR_STEPS = (1, 8, 9)


def padded(block, sides, width):
    for axis, dim in sides:
        count = lax.axis_size(axis)
        forward = [(i, i + 1) for i in range(count - 1)]
        backward = [(target, source) for source, target in forward]
        low = lax.ppermute(
            lax.slice_in_dim(block, block.shape[dim] - width, None, axis=dim), axis, forward
        )
        high = lax.ppermute(lax.slice_in_dim(block, 0, width, axis=dim), axis, backward)
        block = jnp.concatenate([low, block, high], axis=dim)
    return block


def tables(length):
    index_values = jnp.arange(length, dtype=jnp.int32)
    product = index_values[:, None] * index_values[None, :] % length
    angles = product.astype(jnp.float32) * (2.0 * math.pi / length)
    scaling = 1.0 / math.sqrt(length)
    return (jnp.cos(angles) * scaling, jnp.sin(angles) * scaling)


def apply_left(matrix, target):
    return jnp.einsum("ab,pbc->pac", matrix, target, precision=lax.Precision.HIGHEST)


def apply_right(target, matrix):
    return jnp.einsum("pab,bc->pac", target, matrix, precision=lax.Precision.HIGHEST)


def transform(real_part, imag_part, cosine, sine_table, direction):
    left_real = apply_left(cosine, real_part) + direction * apply_left(sine_table, imag_part)
    left_imag = apply_left(cosine, imag_part) - direction * apply_left(sine_table, real_part)
    out_real = apply_right(left_real, cosine) + direction * apply_right(left_imag, sine_table)
    out_imag = apply_right(left_imag, cosine) - direction * apply_right(left_real, sine_table)
    return (out_real, out_imag)


def place_add(target, placed, row_start, col_start):
    zero_index = jnp.int32(0)
    current = lax.dynamic_slice(target, (zero_index, row_start, col_start), placed.shape)
    return lax.dynamic_update_slice(target, current + placed, (zero_index, row_start, col_start))


def shards_by_mode(object_field, probe, positions, measured):
    strip_rows = object_field.shape[1]
    object_width = object_field.shape[2]
    pattern = probe.shape[2]
    half_pattern = pattern // 2
    count = positions.shape[1]
    cosine, sine_table = tables(pattern)
    tile_index = lax.axis_index("tile")
    offset = tile_index * strip_rows - half_pattern
    for minibatch in range(measured.shape[0]):
        extended = padded(object_field, (("tile", 1),), half_pattern)
        row_offsets = positions[minibatch, :, 0] - offset
        column_offsets = positions[minibatch, :, 1]

        def cut_one(row_start, col_start):
            return lax.dynamic_slice(
                extended, (jnp.int32(0), row_start, col_start), (2, pattern, pattern)
            )

        patches = jax.vmap(cut_one)(row_offsets, column_offsets)
        obj_real = patches[:, 0]
        obj_imag = patches[:, 1]
        probe_real = probe[0, 0]
        probe_imag = probe[0, 1]
        exit_real = probe_real * obj_real - probe_imag * obj_imag
        exit_imag = probe_real * obj_imag + probe_imag * obj_real
        far_real, far_imag = transform(exit_real, exit_imag, cosine, sine_table, 1.0)
        observed = measured[minibatch]
        intensity = lax.psum(far_real * far_real + far_imag * far_imag, "mode")
        modulus = jnp.sqrt((observed + 1.0) / (intensity + 1.0)) - 1.0
        chi_real, chi_imag = transform(
            modulus * far_real, modulus * far_imag, cosine, sine_table, -1.0
        )
        grad_real = probe_real * chi_real + probe_imag * chi_imag
        grad_imag = probe_real * chi_imag - probe_imag * chi_real
        probe_power = probe_real * probe_real + probe_imag * probe_imag
        step_real = jnp.sum(obj_real * chi_real + obj_imag * chi_imag, axis=0)
        step_imag = jnp.sum(obj_real * chi_imag - obj_imag * chi_real, axis=0)
        coverage = jnp.sum(obj_real * obj_real + obj_imag * obj_imag, axis=0)
        accumulated = jnp.zeros((3, strip_rows + pattern, object_width), jnp.float32)
        for position in range(count):
            placed = jnp.stack([grad_real[position], grad_imag[position], probe_power])
            accumulated = place_add(
                accumulated, placed, row_offsets[position], column_offsets[position]
            )
        rim_rows = jnp.concatenate(
            [accumulated[:, :half_pattern], accumulated[:, strip_rows + half_pattern :]], axis=1
        )
        received = padded(rim_rows, (("tile", 1),), half_pattern)
        own_strip = accumulated[:, half_pattern : half_pattern + strip_rows]
        own_strip = own_strip.at[:, :half_pattern].add(received[:, :half_pattern])
        own_strip = own_strip.at[:, strip_rows - half_pattern :].add(
            received[:, pattern + half_pattern :]
        )
        summed = lax.psum(own_strip, "mode")
        divisor = summed[2] + 1.0
        object_field = jnp.stack(
            [object_field[0] + summed[0] / divisor, object_field[1] + summed[1] / divisor]
        )
        step_stack = jnp.stack([jnp.stack([step_real, step_imag])])
        step_total, coverage_total = lax.psum((step_stack, coverage), "tile")
        probe = probe + step_total / (coverage_total + 1.0)
    return (object_field, probe)


def table_of(length):
    index_values = np.arange(length)
    angles = (index_values[:, None] * index_values[None, :] % length) * (2.0 * np.pi / length)
    scaling = 1.0 / np.sqrt(length)
    return np.stack([np.cos(angles) * scaling, np.sin(angles) * scaling]).astype(np.float32)


def spot(info, size, minibatch, side, slot):
    tiles, strip, pattern = size
    place = (((side + 1) * 2 + minibatch) * 2 + slot) * 2
    tile = info[24]
    row = info[place] - tile * strip + pattern // 2
    if side < 0:
        row = jnp.where(tile == 0, -pattern, row)
    if side > 0:
        row = jnp.where(tile == tiles - 1, strip + pattern, row)
    return row, info[place + 1]


def take_columns(block, column, width):
    total = block.shape[-1]
    return pltpu.roll(block, lax.rem(total - column, total), 1)[:, :width]


def add_at(tall, block, row, column):
    rows, width = block.shape
    total = tall.shape[1]
    shift = lax.rem(row, 8)
    start = pl.multiple_of(row - shift, 8)
    turned = pltpu.roll(block.reshape(rows // 8, 8, width), shift, 1)
    empty = jnp.zeros((1, 8, width), block.dtype)
    inside = lax.broadcasted_iota(jnp.int32, (rows // 8 + 1, 8, width), 1) >= shift
    moved = jnp.where(
        inside,
        jnp.concatenate([turned, empty], axis=0),
        jnp.concatenate([empty, turned], axis=0),
    ).reshape(rows + 8, width)
    wide = jnp.concatenate([moved, jnp.zeros((rows + 8, total - width), block.dtype)], axis=1)
    tall[pl.ds(start, rows + 8), :] += pltpu.roll(wide, column, 1)


def rows_at(ref, row, rows):
    width = ref.shape[1]
    shift = lax.rem(row, 8)
    start = pl.multiple_of(row - shift, 8)
    block = ref[pl.ds(start, rows + 8), :].reshape(rows // 8 + 1, 8, width)
    turned = pltpu.roll(block, lax.rem(8 - shift, 8), 1)
    inside = lax.broadcasted_iota(jnp.int32, (rows // 8, 8, width), 1) < 8 - shift
    return jnp.where(inside, turned[:-1], turned[1:]).reshape(rows, width)


def halves(value):
    high = value.astype(BF16)
    return high, (value - high.astype(F32)).astype(BF16)


def product(left, right):
    dot = functools.partial(jnp.dot, preferred_element_type=F32)
    return dot(left[0], right[0]) + (dot(left[0], right[1]) + dot(left[1], right[0]))


def cut_patch(size, info, minibatch, strip_ref, below, above, window, part):
    tiles, rows, width = size
    half = width // 2
    row, column = spot(info, size, minibatch, 0, info[25])

    def columns(block):
        return block if block.shape[1] == width else take_columns(block, column, width)

    window[:half] = columns(below)
    window[half : half + rows] = columns(strip_ref[part])
    window[half + rows : rows + width] = columns(above)
    return rows_at(window, row, width)


def illumination_kernel(size, minibatch, info, own, other, out, tall):
    tiles, strip, pattern = size
    half = pattern // 2
    kept = slice(pattern + half, pattern + half + strip)
    tall[kept] = jnp.zeros((strip, tall.shape[1]), F32)
    (pr0, pi0), (pr1, pi1) = ((ref[0], ref[1]) for ref in (own, other))
    power = pr0 * pr0 + pi0 * pi0 + (pr1 * pr1 + pi1 * pi1)
    for side in (-1, 0, 1):
        for slot in range(2):
            row, column = spot(info, size, minibatch, side, slot)
            add_at(tall, power, row + pattern, column)
    out[...] = tall[kept]


def patch_kernel(size, minibatch, info, strip_ref, below, above, patch, window):
    for part in range(2):
        patch[part] = cut_patch(
            size, info, minibatch, strip_ref, below[part], above[part], window, part
        )


def ready_kernel(size, info, strip_ref, probe, measured, table, columns, own, observed, split):
    own[...] = probe[...]
    column = spot(info, size, 0, 0, info[25])[1]
    for part in range(2):
        columns[part] = take_columns(strip_ref[part], column, size[2])
    for minibatch in range(2):
        observed[minibatch] = measured[minibatch, info[25]]
    for i in range(2):
        split[2 * i], split[2 * i + 1] = halves(table[i])


def field_kernel(size, minibatch, info, strip_ref, *refs):
    tiles, strip, pattern = size
    slot = info[25]
    if minibatch:
        own, other, measured, table, gradient, top, bottom, step_own, step_other = refs
        obj_real, obj_imag = strip_ref[0], strip_ref[1]
    else:
        *edges, own, other, measured, table = refs[:-6]
        gradient, top, bottom, step_own, step_other, window = refs[-6:]
        sides = (jnp.where(slot == 0, edges[i][...], edges[i + 1][...]) for i in (0, 2))
        others = (jnp.where(slot == 0, edges[i + 1][...], edges[i][...]) for i in (0, 2))
        obj_real, obj_imag = (
            cut_patch(size, info, minibatch, strip_ref, *ends, window, part)
            for part, ends in enumerate((sides, others))
        )
    cos_high, cos_low, sin_high, sin_low = (table[i] for i in range(4))

    def block(top_left, top_right, low_left, low_right):
        return jnp.concatenate(
            [
                jnp.concatenate([top_left, top_right], axis=1),
                jnp.concatenate([low_left, low_right], axis=1),
            ],
            axis=0,
        )

    first = (
        block(cos_high, sin_high, -sin_high, cos_high),
        block(cos_low, sin_low, -sin_low, cos_low),
    )
    second = (
        block(cos_high, -sin_high, sin_high, cos_high),
        block(cos_low, -sin_low, sin_low, cos_low),
    )
    probes = [(ref[0], ref[1]) for ref in (own, other)]

    def both(fields, left, right):
        (r0, i0), (r1, i1) = fields
        y = product(left, halves(block(r0, r1, i0, i1)))
        y = block(
            y[:pattern, :pattern], y[pattern:, :pattern], y[:pattern, pattern:], y[pattern:, pattern:]
        )
        y = product(halves(y), right)
        return (
            (y[:pattern, :pattern], y[:pattern, pattern:]),
            (y[pattern:, :pattern], y[pattern:, pattern:]),
        )

    exits = [(pr * obj_real - pi * obj_imag, pr * obj_imag + pi * obj_real) for pr, pi in probes]
    far = both(exits, first, second)
    intensity = (far[0][0] * far[0][0] + far[0][1] * far[0][1]) + (
        far[1][0] * far[1][0] + far[1][1] * far[1][1]
    )
    factor = jnp.sqrt((measured[minibatch] + 1.0) / (intensity + 1.0)) - 1.0
    chi = both([(factor * fr, factor * fi) for fr, fi in far], second, first)
    (pr0, pi0), (pr1, pi1) = probes
    (cr0, ci0), (cr1, ci1) = chi
    half = top.shape[1]
    for part, value in (
        (0, (pr0 * cr0 + pi0 * ci0) + (pr1 * cr1 + pi1 * ci1)),
        (1, (pr0 * ci0 - pi0 * cr0) + (pr1 * ci1 - pi1 * cr1)),
    ):
        gradient[part], top[part], bottom[part] = value, value[:half], value[half:]
    coverage = obj_real * obj_real + obj_imag * obj_imag
    rows = pattern // GROUP
    mate = lax.rem(lax.div(info[24], NEAR_STEP), GROUP)
    for step, keeper, (cr, ci) in ((step_own, slot, chi[0]), (step_other, 1 - slot, chi[1])):
        real = obj_real * cr + obj_imag * ci
        imag = obj_real * ci - obj_imag * cr
        for k in range(GROUP):
            start = k * rows
            block = step.at[mate ^ k]
            block[:rows] = real[start : start + rows]
            block[rows : 2 * rows] = imag[start : start + rows]
            middle = start + rows // 2
            block[2 * rows :] = jnp.where(
                keeper == 0, coverage[start:middle], coverage[middle : start + rows]
            )


def update_kernel(size, minibatch, info, strip_ref, illum, own, other, b0, a0, b1, a1, *outs):
    strip_out, *edges, tall = outs
    tiles, strip, pattern = size
    half = pattern // 2
    slot = info[25]
    kept = slice(pattern + half, pattern + half + strip)
    grads = (
        (0, slot, own, 0),
        (0, 1 - slot, other, 0),
        (-1, slot, b0, half),
        (1, slot, a0, 0),
        (-1, 1 - slot, b1, half),
        (1, 1 - slot, a1, 0),
    )
    for part in range(2):
        tall[kept] = jnp.zeros((strip, tall.shape[1]), F32)
        for side, place, ref, start in grads:
            row, column = spot(info, size, minibatch, side, place)
            add_at(tall, ref[part], row + pattern + start, column)
        fresh = strip_ref[part] + tall[kept] / (illum[...] + 1.0)
        strip_out[part] = fresh
        if edges:
            column_below = spot(info, size, minibatch + 1, -1, slot)[1]
            column_above = spot(info, size, minibatch + 1, 1, slot)[1]
            edges[0][part] = take_columns(fresh[:half], column_below, pattern)
            edges[1][part] = take_columns(fresh[strip - half :], column_above, pattern)


def probe_kernel(info, own_totals, other_totals, *refs):
    probes, outs = refs[: len(refs) // 2], refs[len(refs) // 2 :]
    slot = info[25]
    rows = outs[0].shape[1] // GROUP
    mate = lax.rem(lax.div(info[24], NEAR_STEP), GROUP)
    for k in range(GROUP):
        where = pl.ds(pl.multiple_of((mate ^ k) * rows, rows), rows)
        mine, theirs = own_totals[k], other_totals[k]
        own_half, other_half = mine[2 * rows :], theirs[theirs.shape[0] - rows // 2 :]
        coverage = jnp.concatenate(
            [
                jnp.where(slot == 0, own_half, other_half),
                jnp.where(slot == 0, other_half, own_half),
            ],
            axis=0,
        )
        divisor = coverage + 1.0
        for totals, probe, out in zip((mine, theirs), probes, outs):
            for part in range(2):
                change = totals[part * rows : (part + 1) * rows] / divisor
                out[part, where, :] = probe[part, where, :] + change


def call(kernel, name, outs, inputs, scratch=(), flops=0):
    shapes = [
        shape if isinstance(shape, jax.ShapeDtypeStruct) else jax.ShapeDtypeStruct(shape, F32)
        for shape in outs
    ]
    size = sum(value.size * value.dtype.itemsize for value in (*shapes, *inputs))
    smem = pl.BlockSpec(memory_space=pltpu.SMEM)
    vmem = pl.BlockSpec(memory_space=pltpu.VMEM)
    return pl.pallas_call(
        kernel,
        out_shape=shapes,
        in_specs=[smem] + [vmem] * (len(inputs) - 1),
        out_specs=[vmem] * len(shapes),
        scratch_shapes=[pltpu.VMEM(shape, F32) for shape in scratch],
        compiler_params=pltpu.CompilerParams(vmem_limit_bytes=VMEM_BYTES),
        cost_estimate=pl.CostEstimate(flops=flops, bytes_accessed=size, transcendentals=0),
        name=name,
    )(*inputs)


def shards_by_position(object_field, probe, positions, measured):
    strip = object_field.shape[1]
    width = object_field.shape[2]
    pattern = probe.shape[2]
    half = pattern // 2
    tiles = lax.axis_size("tile")
    size = (tiles, strip, pattern)
    field = (2, pattern, pattern)
    tall = (3 * pattern + strip + 8, width)
    window = (pattern + strip + 8, pattern)
    up = [(i, i + 1) for i in range(tiles - 1)]
    down = [(i + 1, i) for i in range(tiles - 1)]

    def swap(value):
        return lax.ppermute(value, "mode", [(0, 1), (1, 0)])

    def across(value, k):
        return lax.ppermute(value, "tile", [(i, i ^ k) for i in range(tiles)])

    def scatter(blocks, unit):
        mates = [across(blocks[k], unit * k) for k in range(1, GROUP)]
        return functools.reduce(jnp.add, mates, blocks[0])

    def exchange(piece):
        first, second, third = (across(piece, steps) for steps in FAR_STEPS)
        return (piece + first) + (second + third)

    def gather(piece, unit):
        return jnp.stack([piece] + [across(piece, unit * k) for k in range(1, GROUP)])

    def from_below(value):
        return lax.ppermute(value, "tile", up)

    def from_above(value):
        return lax.ppermute(value, "tile", down)

    def bind(kernel, *args):
        return functools.partial(kernel, *args)

    tile, slot = lax.axis_index("tile"), lax.axis_index("mode")
    index = jnp.stack([tile, slot]).astype(jnp.int32)
    here = jnp.concatenate([positions.ravel()] * 3 + [index])
    first = slot == 0
    edges = [
        from_below(jnp.where(first, object_field[0, strip - half :], object_field[1, strip - half :])),
        from_above(jnp.where(first, object_field[0, :half], object_field[1, :half])),
    ]
    below, above = from_below(positions), from_above(positions)
    other = swap(probe[0])
    columns, own, observed, table = call(
        bind(ready_kernel, size),
        "ready",
        [(2, strip, pattern), field, field, jax.ShapeDtypeStruct((4, pattern, pattern), BF16)],
        (here, object_field, probe[0], measured, jnp.asarray(table_of(pattern))),
    )
    *edges, below, above, columns, own, observed, table = lax.optimization_barrier(
        (*edges, below, above, columns, own, observed, table)
    )
    edges = [edges[0], swap(edges[0]), edges[1], swap(edges[1])]
    info = jnp.concatenate([below.ravel(), positions.ravel(), above.ravel(), index])

    for minibatch in range(2):
        last = minibatch == 1
        rows = pattern // GROUP
        blocks = (GROUP, 2 * rows + rows // 2, pattern)
        cut = (columns, *edges)
        if last:
            cut = (object_field, *edges)
            cut = call(
                bind(patch_kernel, size, minibatch), "patch", [field], (here, *cut), [window], 10**10
            )
        rim = (2, half, pattern)
        gradient, top, bottom, step_own, step_other = call(
            bind(field_kernel, size, minibatch),
            "field",
            [field, rim, rim, blocks, blocks],
            (here, *cut, own, other, observed, table),
            [] if last else [window],
            flops=2 * 12 * 512**3,
        )
        (illum,) = call(
            bind(illumination_kernel, size, minibatch),
            "illumination",
            [(strip, width)],
            (info, own, other),
            [tall],
        )
        brought = swap(step_other)
        steps = [step_own[k] + brought[k] for k in range(GROUP)]
        piece = scatter(steps, NEAR_STEP)
        rim_below, rim_above = from_below(bottom), from_above(top)
        gradient, rim_below, rim_above, illum = lax.optimization_barrier(
            (gradient, rim_below, rim_above, illum)
        )
        rims = (gradient, swap(gradient), rim_below, rim_above, swap(rim_below), swap(rim_above))
        object_field, *edges = call(
            bind(update_kernel, size, minibatch),
            "update",
            [object_field.shape] + ([] if last else [rim] * 2),
            (info, object_field, illum, *rims),
            [tall],
        )
        piece = exchange(piece)
        if not last:
            edges = [from_below(edges[1]), from_above(edges[0])]
            piece, *edges = lax.optimization_barrier((piece, *edges))
        totals = gather(piece, NEAR_STEP)
        if last:
            totals, object_field = lax.optimization_barrier((totals, object_field))
            others = swap(totals[:, 2 * rows :])
            (own,) = call(probe_kernel, "probe", [field], (here, totals, others, own))
        else:
            own, other = call(
                probe_kernel, "probe", [field] * 2, (here, totals, swap(totals), own, other)
            )
    return (object_field, own[None])


def solution(mesh):
    in_specs = (
        P(None, "tile", None),
        P("mode", None, None, None),
        P(None, "tile", None),
        P(None, "tile", None, None),
    )
    out_specs = (P(None, "tile", None), P("mode", None, None, None))

    def whole(object_field, probe, positions, measured):
        tiles, pair = mesh.shape["tile"], mesh.shape["mode"]
        by_position = (
            pair == 2
            and probe.shape[0] == 2
            and positions.shape[:2] == (2, 2 * tiles)
            and tiles == GROUP * GROUP
            and probe.shape[2] % (16 * 2 * GROUP) == 0
            and object_field.shape[1] == tiles * probe.shape[2]
        )
        shards = shards_by_position if by_position else shards_by_mode
        return jax.shard_map(
            shards, mesh=mesh, in_specs=in_specs, out_specs=out_specs, check_vma=False
        )(object_field, probe, positions, measured)

    return whole
```

```python
import functools
import math

import jax
import jax.numpy as jnp
import numpy as np
from jax import lax
from jax.experimental import pallas as pl
from jax.experimental.pallas import tpu as pltpu
from jax.sharding import PartitionSpec as P

F32 = jnp.float32
BF16 = jnp.bfloat16
VMEM_BYTES = 16 * 1024 * 1024
GROUP = 4
NEAR_STEP = 2
FAR_STEPS = (1, 8, 9)


def padded(block, sides, width):
    for axis, dim in sides:
        count = lax.axis_size(axis)
        forward = [(i, i + 1) for i in range(count - 1)]
        backward = [(target, source) for source, target in forward]
        low = lax.ppermute(
            lax.slice_in_dim(block, block.shape[dim] - width, None, axis=dim), axis, forward
        )
        high = lax.ppermute(lax.slice_in_dim(block, 0, width, axis=dim), axis, backward)
        block = jnp.concatenate([low, block, high], axis=dim)
    return block


def tables(length):
    index_values = jnp.arange(length, dtype=jnp.int32)
    product = index_values[:, None] * index_values[None, :] % length
    angles = product.astype(jnp.float32) * (2.0 * math.pi / length)
    scaling = 1.0 / math.sqrt(length)
    return (jnp.cos(angles) * scaling, jnp.sin(angles) * scaling)


def apply_left(matrix, target):
    return jnp.einsum("ab,pbc->pac", matrix, target, precision=lax.Precision.HIGHEST)


def apply_right(target, matrix):
    return jnp.einsum("pab,bc->pac", target, matrix, precision=lax.Precision.HIGHEST)


def transform(real_part, imag_part, cosine, sine_table, direction):
    left_real = apply_left(cosine, real_part) + direction * apply_left(sine_table, imag_part)
    left_imag = apply_left(cosine, imag_part) - direction * apply_left(sine_table, real_part)
    out_real = apply_right(left_real, cosine) + direction * apply_right(left_imag, sine_table)
    out_imag = apply_right(left_imag, cosine) - direction * apply_right(left_real, sine_table)
    return (out_real, out_imag)


def place_add(target, placed, row_start, col_start):
    zero_index = jnp.int32(0)
    current = lax.dynamic_slice(target, (zero_index, row_start, col_start), placed.shape)
    return lax.dynamic_update_slice(target, current + placed, (zero_index, row_start, col_start))


def shards_by_mode(object_field, probe, positions, measured):
    strip_rows = object_field.shape[1]
    object_width = object_field.shape[2]
    pattern = probe.shape[2]
    half_pattern = pattern // 2
    count = positions.shape[1]
    cosine, sine_table = tables(pattern)
    tile_index = lax.axis_index("tile")
    offset = tile_index * strip_rows - half_pattern
    for minibatch in range(measured.shape[0]):
        extended = padded(object_field, (("tile", 1),), half_pattern)
        row_offsets = positions[minibatch, :, 0] - offset
        column_offsets = positions[minibatch, :, 1]

        def cut_one(row_start, col_start):
            return lax.dynamic_slice(
                extended, (jnp.int32(0), row_start, col_start), (2, pattern, pattern)
            )

        patches = jax.vmap(cut_one)(row_offsets, column_offsets)
        obj_real = patches[:, 0]
        obj_imag = patches[:, 1]
        probe_real = probe[0, 0]
        probe_imag = probe[0, 1]
        exit_real = probe_real * obj_real - probe_imag * obj_imag
        exit_imag = probe_real * obj_imag + probe_imag * obj_real
        far_real, far_imag = transform(exit_real, exit_imag, cosine, sine_table, 1.0)
        observed = measured[minibatch]
        intensity = lax.psum(far_real * far_real + far_imag * far_imag, "mode")
        modulus = jnp.sqrt((observed + 1.0) / (intensity + 1.0)) - 1.0
        chi_real, chi_imag = transform(
            modulus * far_real, modulus * far_imag, cosine, sine_table, -1.0
        )
        grad_real = probe_real * chi_real + probe_imag * chi_imag
        grad_imag = probe_real * chi_imag - probe_imag * chi_real
        probe_power = probe_real * probe_real + probe_imag * probe_imag
        step_real = jnp.sum(obj_real * chi_real + obj_imag * chi_imag, axis=0)
        step_imag = jnp.sum(obj_real * chi_imag - obj_imag * chi_real, axis=0)
        coverage = jnp.sum(obj_real * obj_real + obj_imag * obj_imag, axis=0)
        accumulated = jnp.zeros((3, strip_rows + pattern, object_width), jnp.float32)
        for position in range(count):
            placed = jnp.stack([grad_real[position], grad_imag[position], probe_power])
            accumulated = place_add(
                accumulated, placed, row_offsets[position], column_offsets[position]
            )
        rim_rows = jnp.concatenate(
            [accumulated[:, :half_pattern], accumulated[:, strip_rows + half_pattern :]], axis=1
        )
        received = padded(rim_rows, (("tile", 1),), half_pattern)
        own_strip = accumulated[:, half_pattern : half_pattern + strip_rows]
        own_strip = own_strip.at[:, :half_pattern].add(received[:, :half_pattern])
        own_strip = own_strip.at[:, strip_rows - half_pattern :].add(
            received[:, pattern + half_pattern :]
        )
        summed = lax.psum(own_strip, "mode")
        divisor = summed[2] + 1.0
        object_field = jnp.stack(
            [object_field[0] + summed[0] / divisor, object_field[1] + summed[1] / divisor]
        )
        step_stack = jnp.stack([jnp.stack([step_real, step_imag])])
        step_total, coverage_total = lax.psum((step_stack, coverage), "tile")
        probe = probe + step_total / (coverage_total + 1.0)
    return (object_field, probe)


def table_of(length):
    index_values = np.arange(length)
    angles = (index_values[:, None] * index_values[None, :] % length) * (2.0 * np.pi / length)
    scaling = 1.0 / np.sqrt(length)
    return np.stack([np.cos(angles) * scaling, np.sin(angles) * scaling]).astype(np.float32)


def spot(info, size, minibatch, side, slot):
    tiles, strip, pattern = size
    place = (((side + 1) * 2 + minibatch) * 2 + slot) * 2
    tile = info[24]
    row = info[place] - tile * strip + pattern // 2
    if side < 0:
        row = jnp.where(tile == 0, -pattern, row)
    if side > 0:
        row = jnp.where(tile == tiles - 1, strip + pattern, row)
    return row, info[place + 1]


def take_columns(block, column, width):
    total = block.shape[-1]
    return pltpu.roll(block, lax.rem(total - column, total), 1)[:, :width]


def add_at(tall, block, row, column):
    rows, width = block.shape
    total = tall.shape[1]
    shift = lax.rem(row, 8)
    start = pl.multiple_of(row - shift, 8)
    turned = pltpu.roll(block.reshape(rows // 8, 8, width), shift, 1)
    empty = jnp.zeros((1, 8, width), block.dtype)
    inside = lax.broadcasted_iota(jnp.int32, (rows // 8 + 1, 8, width), 1) >= shift
    moved = jnp.where(
        inside,
        jnp.concatenate([turned, empty], axis=0),
        jnp.concatenate([empty, turned], axis=0),
    ).reshape(rows + 8, width)
    wide = jnp.concatenate([moved, jnp.zeros((rows + 8, total - width), block.dtype)], axis=1)
    tall[pl.ds(start, rows + 8), :] += pltpu.roll(wide, column, 1)


def rows_at(ref, row, rows):
    width = ref.shape[1]
    shift = lax.rem(row, 8)
    start = pl.multiple_of(row - shift, 8)
    block = ref[pl.ds(start, rows + 8), :].reshape(rows // 8 + 1, 8, width)
    turned = pltpu.roll(block, lax.rem(8 - shift, 8), 1)
    inside = lax.broadcasted_iota(jnp.int32, (rows // 8, 8, width), 1) < 8 - shift
    return jnp.where(inside, turned[:-1], turned[1:]).reshape(rows, width)


def halves(value):
    high = value.astype(BF16)
    return high, (value - high.astype(F32)).astype(BF16)


def product(left, right):
    dot = functools.partial(jnp.dot, preferred_element_type=F32)
    return dot(left[0], right[0]) + (dot(left[0], right[1]) + dot(left[1], right[0]))


def cut_patch(size, info, minibatch, strip_ref, below, above, window, part):
    tiles, rows, width = size
    half = width // 2
    row, column = spot(info, size, minibatch, 0, info[25])

    def columns(block):
        return block if block.shape[1] == width else take_columns(block, column, width)

    window[:half] = columns(below)
    window[half : half + rows] = columns(strip_ref[part])
    window[half + rows : rows + width] = columns(above)
    return rows_at(window, row, width)


def illumination_kernel(size, minibatch, info, own, other, out, tall):
    tiles, strip, pattern = size
    begin = pattern + (pattern + strip - out.shape[0]) // 2
    kept = slice(begin, begin + out.shape[0])
    tall[kept] = jnp.zeros(out.shape, F32)
    (pr0, pi0), (pr1, pi1) = ((ref[0], ref[1]) for ref in (own, other))
    power = pr0 * pr0 + pi0 * pi0 + (pr1 * pr1 + pi1 * pi1)
    for side in (-1, 0, 1):
        for slot in range(2):
            row, column = spot(info, size, minibatch, side, slot)
            add_at(tall, power, row + pattern, column)
    out[...] = tall[kept]


def edges_kernel(size, info, strip_ref, low, high):
    half, width = low.shape[1:]
    column_below = spot(info, size, 1, -1, info[25])[1]
    column_above = spot(info, size, 1, 1, info[25])[1]
    for part in range(2):
        low[part] = take_columns(strip_ref[part, :half], column_below, width)
        high[part] = take_columns(strip_ref[part, strip_ref.shape[1] - half :], column_above, width)


def ready_kernel(info, probe, measured, table, own, observed, split):
    own[...] = probe[...]
    for minibatch in range(2):
        observed[minibatch] = measured[minibatch, info[25]]
    for i in range(2):
        split[2 * i], split[2 * i + 1] = halves(table[i])


def field_kernel(size, minibatch, info, strip_ref, *refs):
    tiles, strip, pattern = size
    slot = info[25]
    if minibatch:
        own, other, measured, table, gradient, top, bottom, step_own, step_other = refs
        obj_real, obj_imag = strip_ref[0], strip_ref[1]
    else:
        *edges, own, other, measured, table = refs[:-4]
        gradient, step_own, step_other, window = refs[-4:]
        sides = (jnp.where(slot == 0, edges[i][...], edges[i + 1][...]) for i in (0, 2))
        others = (jnp.where(slot == 0, edges[i + 1][...], edges[i][...]) for i in (0, 2))
        obj_real, obj_imag = (
            cut_patch(size, info, minibatch, strip_ref, *ends, window, part)
            for part, ends in enumerate((sides, others))
        )
    cos_high, cos_low, sin_high, sin_low = (table[i] for i in range(4))

    def block(top_left, top_right, low_left, low_right):
        return jnp.concatenate(
            [
                jnp.concatenate([top_left, top_right], axis=1),
                jnp.concatenate([low_left, low_right], axis=1),
            ],
            axis=0,
        )

    first = (
        block(cos_high, sin_high, -sin_high, cos_high),
        block(cos_low, sin_low, -sin_low, cos_low),
    )
    second = (
        block(cos_high, -sin_high, sin_high, cos_high),
        block(cos_low, -sin_low, sin_low, cos_low),
    )
    probes = [(ref[0], ref[1]) for ref in (own, other)]

    def both(fields, left, right):
        (r0, i0), (r1, i1) = fields
        y = product(left, halves(block(r0, r1, i0, i1)))
        y = block(
            y[:pattern, :pattern], y[pattern:, :pattern], y[:pattern, pattern:], y[pattern:, pattern:]
        )
        y = product(halves(y), right)
        return (
            (y[:pattern, :pattern], y[:pattern, pattern:]),
            (y[pattern:, :pattern], y[pattern:, pattern:]),
        )

    exits = [(pr * obj_real - pi * obj_imag, pr * obj_imag + pi * obj_real) for pr, pi in probes]
    far = both(exits, first, second)
    intensity = (far[0][0] * far[0][0] + far[0][1] * far[0][1]) + (
        far[1][0] * far[1][0] + far[1][1] * far[1][1]
    )
    factor = jnp.sqrt((measured[minibatch] + 1.0) / (intensity + 1.0)) - 1.0
    chi = both([(factor * fr, factor * fi) for fr, fi in far], second, first)
    (pr0, pi0), (pr1, pi1) = probes
    (cr0, ci0), (cr1, ci1) = chi
    half = pattern // 2
    for part, value in (
        (0, (pr0 * cr0 + pi0 * ci0) + (pr1 * cr1 + pi1 * ci1)),
        (1, (pr0 * ci0 - pi0 * cr0) + (pr1 * ci1 - pi1 * cr1)),
    ):
        gradient[part] = value
        if minibatch:
            top[part], bottom[part] = value[:half], value[half:]
    coverage = obj_real * obj_real + obj_imag * obj_imag
    rows = pattern // GROUP
    mate = lax.rem(lax.div(info[24], NEAR_STEP), GROUP)
    for step, keeper, (cr, ci) in ((step_own, slot, chi[0]), (step_other, 1 - slot, chi[1])):
        real = obj_real * cr + obj_imag * ci
        imag = obj_real * ci - obj_imag * cr
        for k in range(GROUP):
            start = k * rows
            block = step.at[mate ^ k]
            block[:rows] = real[start : start + rows]
            block[rows : 2 * rows] = imag[start : start + rows]
            middle = start + rows // 2
            block[2 * rows :] = jnp.where(
                keeper == 0, coverage[start:middle], coverage[middle : start + rows]
            )


def place_all(size, minibatch, info, refs, part, tall, kept, start_below):
    own, other, b0, a0, b1, a1 = refs
    slot = info[25]
    tall[kept] = jnp.zeros((kept.stop - kept.start, tall.shape[1]), F32)
    for side, place, ref, start in (
        (0, slot, own, 0),
        (0, 1 - slot, other, 0),
        (-1, slot, b0, start_below),
        (1, slot, a0, 0),
        (-1, 1 - slot, b1, start_below),
        (1, 1 - slot, a1, 0),
    ):
        row, column = spot(info, size, minibatch, side, place)
        add_at(tall, ref[part], row + size[2] + start, column)


def update_kernel(size, info, strip_ref, below, above, illum, *refs):
    grads, (strip_out, patch, tall, window) = refs[:-4], refs[-4:]
    tiles, strip, pattern = size
    half = pattern // 2
    kept = slice(pattern, 2 * pattern + strip)
    row, column = spot(info, size, 1, 0, info[25])
    for part in range(2):
        place_all(size, 0, info, grads, part, tall, kept, 0)
        change = tall[kept] / (illum[...] + 1.0)
        strip_out[part] = strip_ref[part] + change[half : half + strip]
        old = cut_patch(size, info, 1, strip_ref, below[part], above[part], window, part)
        window[: pattern + strip] = take_columns(change, column, pattern)
        patch[part] = old + rows_at(window, row, pattern)


def final_kernel(size, info, strip_ref, illum, *refs):
    grads, (strip_out, tall) = refs[:-2], refs[-2:]
    tiles, strip, pattern = size
    half = pattern // 2
    kept = slice(pattern + half, pattern + half + strip)
    for part in range(2):
        place_all(size, 1, info, grads, part, tall, kept, half)
        strip_out[part] = strip_ref[part] + tall[kept] / (illum[...] + 1.0)


def probe_kernel(info, own_totals, other_totals, *refs):
    probes, outs = refs[: len(refs) // 2], refs[len(refs) // 2 :]
    slot = info[25]
    rows = outs[0].shape[1] // GROUP
    mate = lax.rem(lax.div(info[24], NEAR_STEP), GROUP)
    for k in range(GROUP):
        where = pl.ds(pl.multiple_of((mate ^ k) * rows, rows), rows)
        mine, theirs = own_totals[k], other_totals[k]
        own_half, other_half = mine[2 * rows :], theirs[theirs.shape[0] - rows // 2 :]
        coverage = jnp.concatenate(
            [
                jnp.where(slot == 0, own_half, other_half),
                jnp.where(slot == 0, other_half, own_half),
            ],
            axis=0,
        )
        divisor = coverage + 1.0
        for totals, probe, out in zip((mine, theirs), probes, outs):
            for part in range(2):
                change = totals[part * rows : (part + 1) * rows] / divisor
                out[part, where, :] = probe[part, where, :] + change


def call(kernel, name, outs, inputs, scratch=(), flops=0):
    shapes = [
        shape if isinstance(shape, jax.ShapeDtypeStruct) else jax.ShapeDtypeStruct(shape, F32)
        for shape in outs
    ]
    size = sum(value.size * value.dtype.itemsize for value in (*shapes, *inputs))
    smem = pl.BlockSpec(memory_space=pltpu.SMEM)
    vmem = pl.BlockSpec(memory_space=pltpu.VMEM)
    return pl.pallas_call(
        kernel,
        out_shape=shapes,
        in_specs=[smem] + [vmem] * (len(inputs) - 1),
        out_specs=[vmem] * len(shapes),
        scratch_shapes=[pltpu.VMEM(shape, F32) for shape in scratch],
        compiler_params=pltpu.CompilerParams(vmem_limit_bytes=VMEM_BYTES),
        cost_estimate=pl.CostEstimate(flops=flops, bytes_accessed=size, transcendentals=0),
        name=name,
    )(*inputs)


def shards_by_position(object_field, probe, positions, measured):
    strip = object_field.shape[1]
    width = object_field.shape[2]
    pattern = probe.shape[2]
    half = pattern // 2
    tiles = lax.axis_size("tile")
    size = (tiles, strip, pattern)
    field = (2, pattern, pattern)
    tall = (3 * pattern + strip + 8, width)
    window = (pattern + strip + 8, pattern)
    up = [(i, i + 1) for i in range(tiles - 1)]
    down = [(i + 1, i) for i in range(tiles - 1)]

    def swap(value):
        return lax.ppermute(value, "mode", [(0, 1), (1, 0)])

    def across(value, k):
        return lax.ppermute(value, "tile", [(i, i ^ k) for i in range(tiles)])

    def scatter(blocks, unit):
        mates = [across(blocks[k], unit * k) for k in range(1, GROUP)]
        return functools.reduce(jnp.add, mates, blocks[0])

    def exchange(piece):
        first, second, third = (across(piece, steps) for steps in FAR_STEPS)
        return (piece + first) + (second + third)

    def gather(piece, unit):
        return jnp.stack([piece] + [across(piece, unit * k) for k in range(1, GROUP)])

    def from_below(value):
        return lax.ppermute(value, "tile", up)

    def from_above(value):
        return lax.ppermute(value, "tile", down)

    def bind(kernel, *args):
        return functools.partial(kernel, *args)

    tile, slot = lax.axis_index("tile"), lax.axis_index("mode")
    index = jnp.stack([tile, slot]).astype(jnp.int32)
    here = jnp.concatenate([positions.ravel()] * 3 + [index])
    one_part = lax.dynamic_index_in_dim(object_field, slot, 0, keepdims=False)
    edges = [from_below(one_part[strip - half :]), from_above(one_part[:half])]
    below, above = from_below(positions), from_above(positions)
    other = swap(probe[0])
    own, observed, table = call(
        ready_kernel,
        "ready",
        [field, field, jax.ShapeDtypeStruct((4, pattern, pattern), BF16)],
        (here, probe[0], measured, jnp.asarray(table_of(pattern))),
    )
    info = jnp.concatenate([below.ravel(), positions.ravel(), above.ravel(), index])
    low, high = call(
        bind(edges_kernel, size), "edges", [(2, half, pattern)] * 2, (info, object_field)
    )
    *edges, low, high, own, observed, table = lax.optimization_barrier(
        (*edges, low, high, own, observed, table)
    )
    edges = [edges[0], swap(edges[0]), edges[1], swap(edges[1])]
    old_below, old_above = from_below(high), from_above(low)
    cut = (object_field, *edges)

    for minibatch in range(2):
        last = minibatch == 1
        rows = pattern // GROUP
        blocks = (GROUP, 2 * rows + rows // 2, pattern)
        rims = [(2, half, pattern)] * 2 if last else []
        gradient, *rims, step_own, step_other = call(
            bind(field_kernel, size, minibatch),
            "field",
            [field, *rims, blocks, blocks],
            (here, *cut, own, other, observed, table),
            [] if last else [window],
            flops=2 * 12 * 512**3 if last else 2 * 10**10,
        )
        (illum,) = call(
            bind(illumination_kernel, size, minibatch),
            "illumination",
            [(strip if last else strip + pattern, width)],
            (info, own, other),
            [tall],
        )
        if not last:
            step_other, old_below, old_above = lax.optimization_barrier(
                (step_other, old_below, old_above)
            )
        brought = swap(step_other)
        steps = [step_own[k] + brought[k] for k in range(GROUP)]
        if last:
            from_low, from_high = from_below(rims[1]), from_above(rims[0])
        else:
            from_low, from_high = from_below(gradient), from_above(gradient)
        piece = scatter(steps, NEAR_STEP)
        if last:
            gradient, from_low, from_high, illum = lax.optimization_barrier(
                (gradient, from_low, from_high, illum)
            )
            piece = exchange(piece)
        else:
            piece = exchange(piece)
            gradient, from_low, from_high, illum, piece = lax.optimization_barrier(
                (gradient, from_low, from_high, illum, piece)
            )
        grads = (gradient, swap(gradient), from_low, from_high, swap(from_low), swap(from_high))
        if last:
            (object_field,) = call(
                bind(final_kernel, size),
                "final",
                [object_field.shape],
                (info, object_field, illum, *grads),
                [tall],
            )
        else:
            object_field, *cut = call(
                bind(update_kernel, size),
                "update",
                [object_field.shape, field],
                (info, object_field, old_below, old_above, illum, *grads),
                [tall, window],
                flops=10**10,
            )
        totals = gather(piece, NEAR_STEP)
        if last:
            totals, object_field = lax.optimization_barrier((totals, object_field))
            others = swap(totals[:, 2 * rows :])
            (own,) = call(probe_kernel, "probe", [field], (here, totals, others, own))
        else:
            own, other = call(
                probe_kernel, "probe", [field] * 2, (here, totals, swap(totals), own, other)
            )
    return (object_field, own[None])


def solution(mesh):
    in_specs = (
        P(None, "tile", None),
        P("mode", None, None, None),
        P(None, "tile", None),
        P(None, "tile", None, None),
    )
    out_specs = (P(None, "tile", None), P("mode", None, None, None))

    def whole(object_field, probe, positions, measured):
        tiles, pair = mesh.shape["tile"], mesh.shape["mode"]
        by_position = (
            pair == 2
            and probe.shape[0] == 2
            and positions.shape[:2] == (2, 2 * tiles)
            and tiles == GROUP * GROUP
            and probe.shape[2] % (16 * 2 * GROUP) == 0
            and object_field.shape[1] == tiles * probe.shape[2]
        )
        shards = shards_by_position if by_position else shards_by_mode
        return jax.shard_map(
            shards, mesh=mesh, in_specs=in_specs, out_specs=out_specs, check_vma=False
        )(object_field, probe, positions, measured)

    return whole
```

```python
import functools
import math

import jax
import jax.numpy as jnp
import numpy as np
from jax import lax
from jax.experimental import pallas as pl
from jax.experimental.pallas import tpu as pltpu
from jax.sharding import PartitionSpec as P

F32 = jnp.float32
BF16 = jnp.bfloat16
VMEM_BYTES = 16 * 1024 * 1024
GROUP = 4
NEAR_STEP = 2
FAR_STEPS = (1, 8, 9)


def padded(block, sides, width):
    for axis, dim in sides:
        count = lax.axis_size(axis)
        forward = [(i, i + 1) for i in range(count - 1)]
        backward = [(target, source) for source, target in forward]
        low = lax.ppermute(
            lax.slice_in_dim(block, block.shape[dim] - width, None, axis=dim), axis, forward
        )
        high = lax.ppermute(lax.slice_in_dim(block, 0, width, axis=dim), axis, backward)
        block = jnp.concatenate([low, block, high], axis=dim)
    return block


def tables(length):
    index_values = jnp.arange(length, dtype=jnp.int32)
    product = index_values[:, None] * index_values[None, :] % length
    angles = product.astype(jnp.float32) * (2.0 * math.pi / length)
    scaling = 1.0 / math.sqrt(length)
    return (jnp.cos(angles) * scaling, jnp.sin(angles) * scaling)


def apply_left(matrix, target):
    return jnp.einsum("ab,pbc->pac", matrix, target, precision=lax.Precision.HIGHEST)


def apply_right(target, matrix):
    return jnp.einsum("pab,bc->pac", target, matrix, precision=lax.Precision.HIGHEST)


def transform(real_part, imag_part, cosine, sine_table, direction):
    left_real = apply_left(cosine, real_part) + direction * apply_left(sine_table, imag_part)
    left_imag = apply_left(cosine, imag_part) - direction * apply_left(sine_table, real_part)
    out_real = apply_right(left_real, cosine) + direction * apply_right(left_imag, sine_table)
    out_imag = apply_right(left_imag, cosine) - direction * apply_right(left_real, sine_table)
    return (out_real, out_imag)


def place_add(target, placed, row_start, col_start):
    zero_index = jnp.int32(0)
    current = lax.dynamic_slice(target, (zero_index, row_start, col_start), placed.shape)
    return lax.dynamic_update_slice(target, current + placed, (zero_index, row_start, col_start))


def shards_by_mode(object_field, probe, positions, measured):
    strip_rows = object_field.shape[1]
    object_width = object_field.shape[2]
    pattern = probe.shape[2]
    half_pattern = pattern // 2
    count = positions.shape[1]
    cosine, sine_table = tables(pattern)
    tile_index = lax.axis_index("tile")
    offset = tile_index * strip_rows - half_pattern
    for minibatch in range(measured.shape[0]):
        extended = padded(object_field, (("tile", 1),), half_pattern)
        row_offsets = positions[minibatch, :, 0] - offset
        column_offsets = positions[minibatch, :, 1]

        def cut_one(row_start, col_start):
            return lax.dynamic_slice(
                extended, (jnp.int32(0), row_start, col_start), (2, pattern, pattern)
            )

        patches = jax.vmap(cut_one)(row_offsets, column_offsets)
        obj_real = patches[:, 0]
        obj_imag = patches[:, 1]
        probe_real = probe[0, 0]
        probe_imag = probe[0, 1]
        exit_real = probe_real * obj_real - probe_imag * obj_imag
        exit_imag = probe_real * obj_imag + probe_imag * obj_real
        far_real, far_imag = transform(exit_real, exit_imag, cosine, sine_table, 1.0)
        observed = measured[minibatch]
        intensity = lax.psum(far_real * far_real + far_imag * far_imag, "mode")
        modulus = jnp.sqrt((observed + 1.0) / (intensity + 1.0)) - 1.0
        chi_real, chi_imag = transform(
            modulus * far_real, modulus * far_imag, cosine, sine_table, -1.0
        )
        grad_real = probe_real * chi_real + probe_imag * chi_imag
        grad_imag = probe_real * chi_imag - probe_imag * chi_real
        probe_power = probe_real * probe_real + probe_imag * probe_imag
        step_real = jnp.sum(obj_real * chi_real + obj_imag * chi_imag, axis=0)
        step_imag = jnp.sum(obj_real * chi_imag - obj_imag * chi_real, axis=0)
        coverage = jnp.sum(obj_real * obj_real + obj_imag * obj_imag, axis=0)
        accumulated = jnp.zeros((3, strip_rows + pattern, object_width), jnp.float32)
        for position in range(count):
            placed = jnp.stack([grad_real[position], grad_imag[position], probe_power])
            accumulated = place_add(
                accumulated, placed, row_offsets[position], column_offsets[position]
            )
        rim_rows = jnp.concatenate(
            [accumulated[:, :half_pattern], accumulated[:, strip_rows + half_pattern :]], axis=1
        )
        received = padded(rim_rows, (("tile", 1),), half_pattern)
        own_strip = accumulated[:, half_pattern : half_pattern + strip_rows]
        own_strip = own_strip.at[:, :half_pattern].add(received[:, :half_pattern])
        own_strip = own_strip.at[:, strip_rows - half_pattern :].add(
            received[:, pattern + half_pattern :]
        )
        summed = lax.psum(own_strip, "mode")
        divisor = summed[2] + 1.0
        object_field = jnp.stack(
            [object_field[0] + summed[0] / divisor, object_field[1] + summed[1] / divisor]
        )
        step_stack = jnp.stack([jnp.stack([step_real, step_imag])])
        step_total, coverage_total = lax.psum((step_stack, coverage), "tile")
        probe = probe + step_total / (coverage_total + 1.0)
    return (object_field, probe)


def table_of(length):
    index_values = np.arange(length)
    angles = (index_values[:, None] * index_values[None, :] % length) * (2.0 * np.pi / length)
    scaling = 1.0 / np.sqrt(length)
    return np.stack([np.cos(angles) * scaling, np.sin(angles) * scaling]).astype(np.float32)


def spot(info, size, minibatch, side, slot):
    tiles, strip, pattern = size
    place = (((side + 1) * 2 + minibatch) * 2 + slot) * 2
    tile = info[24]
    row = info[place] - tile * strip + pattern // 2
    if side < 0:
        row = jnp.where(tile == 0, -pattern, row)
    if side > 0:
        row = jnp.where(tile == tiles - 1, strip + pattern, row)
    return row, info[place + 1]


def take_columns(block, column, width):
    total = block.shape[-1]
    return pltpu.roll(block, lax.rem(total - column, total), 1)[:, :width]


def add_at(tall, block, row, column):
    rows, width = block.shape
    total = tall.shape[1]
    shift = lax.rem(row, 8)
    start = pl.multiple_of(row - shift, 8)
    turned = pltpu.roll(block.reshape(rows // 8, 8, width), shift, 1)
    empty = jnp.zeros((1, 8, width), block.dtype)
    inside = lax.broadcasted_iota(jnp.int32, (rows // 8 + 1, 8, width), 1) >= shift
    moved = jnp.where(
        inside,
        jnp.concatenate([turned, empty], axis=0),
        jnp.concatenate([empty, turned], axis=0),
    ).reshape(rows + 8, width)
    wide = jnp.concatenate([moved, jnp.zeros((rows + 8, total - width), block.dtype)], axis=1)
    tall[pl.ds(start, rows + 8), :] += pltpu.roll(wide, column, 1)


def rows_at(ref, row, rows):
    width = ref.shape[1]
    shift = lax.rem(row, 8)
    start = pl.multiple_of(row - shift, 8)
    block = ref[pl.ds(start, rows + 8), :].reshape(rows // 8 + 1, 8, width)
    turned = pltpu.roll(block, lax.rem(8 - shift, 8), 1)
    inside = lax.broadcasted_iota(jnp.int32, (rows // 8, 8, width), 1) < 8 - shift
    return jnp.where(inside, turned[:-1], turned[1:]).reshape(rows, width)


def halves(value):
    high = value.astype(BF16)
    return high, (value - high.astype(F32)).astype(BF16)


def product(left, right):
    dot = functools.partial(jnp.dot, preferred_element_type=F32)
    return dot(left[0], right[0]) + (dot(left[0], right[1]) + dot(left[1], right[0]))


def cut_patch(size, info, minibatch, strip_ref, below, above, window, part):
    tiles, rows, width = size
    half = width // 2
    row, column = spot(info, size, minibatch, 0, info[25])

    def columns(block):
        return block if block.shape[1] == width else take_columns(block, column, width)

    window[:half] = columns(below)
    window[half : half + rows] = columns(strip_ref[part])
    window[half + rows : rows + width] = columns(above)
    return rows_at(window, row, width)


def illumination_kernel(size, minibatch, info, own, other, out, tall):
    tiles, strip, pattern = size
    half = pattern // 2
    kept = slice(pattern + half, pattern + half + strip)
    tall[kept] = jnp.zeros((strip, tall.shape[1]), F32)
    (pr0, pi0), (pr1, pi1) = ((ref[0], ref[1]) for ref in (own, other))
    power = pr0 * pr0 + pi0 * pi0 + (pr1 * pr1 + pi1 * pi1)
    for side in (-1, 0, 1):
        for slot in range(2):
            row, column = spot(info, size, minibatch, side, slot)
            add_at(tall, power, row + pattern, column)
    out[...] = tall[kept]


def patch_kernel(size, minibatch, info, strip_ref, below, above, patch, window):
    for part in range(2):
        patch[part] = cut_patch(
            size, info, minibatch, strip_ref, below[part], above[part], window, part
        )


def ready_kernel(info, probe, measured, table, own, observed, split):
    own[...] = probe[...]
    for minibatch in range(2):
        observed[minibatch] = measured[minibatch, info[25]]
    for i in range(2):
        split[2 * i], split[2 * i + 1] = halves(table[i])


def field_kernel(size, minibatch, info, strip_ref, *refs):
    tiles, strip, pattern = size
    slot = info[25]
    if minibatch:
        own, other, measured, table, gradient, top, bottom, step_own, step_other = refs
        obj_real, obj_imag = strip_ref[0], strip_ref[1]
    else:
        *edges, own, other, measured, table = refs[:-6]
        gradient, top, bottom, step_own, step_other, window = refs[-6:]
        sides = (jnp.where(slot == 0, edges[i][...], edges[i + 1][...]) for i in (0, 2))
        others = (jnp.where(slot == 0, edges[i + 1][...], edges[i][...]) for i in (0, 2))
        obj_real, obj_imag = (
            cut_patch(size, info, minibatch, strip_ref, *ends, window, part)
            for part, ends in enumerate((sides, others))
        )
    cos_high, cos_low, sin_high, sin_low = (table[i] for i in range(4))

    def block(top_left, top_right, low_left, low_right):
        return jnp.concatenate(
            [
                jnp.concatenate([top_left, top_right], axis=1),
                jnp.concatenate([low_left, low_right], axis=1),
            ],
            axis=0,
        )

    first = (
        block(cos_high, sin_high, -sin_high, cos_high),
        block(cos_low, sin_low, -sin_low, cos_low),
    )
    second = (
        block(cos_high, -sin_high, sin_high, cos_high),
        block(cos_low, -sin_low, sin_low, cos_low),
    )
    probes = [(ref[0], ref[1]) for ref in (own, other)]

    def both(fields, left, right):
        (r0, i0), (r1, i1) = fields
        y = product(left, halves(block(r0, r1, i0, i1)))
        y = block(
            y[:pattern, :pattern], y[pattern:, :pattern], y[:pattern, pattern:], y[pattern:, pattern:]
        )
        y = product(halves(y), right)
        return (
            (y[:pattern, :pattern], y[:pattern, pattern:]),
            (y[pattern:, :pattern], y[pattern:, pattern:]),
        )

    exits = [(pr * obj_real - pi * obj_imag, pr * obj_imag + pi * obj_real) for pr, pi in probes]
    far = both(exits, first, second)
    intensity = (far[0][0] * far[0][0] + far[0][1] * far[0][1]) + (
        far[1][0] * far[1][0] + far[1][1] * far[1][1]
    )
    factor = jnp.sqrt((measured[minibatch] + 1.0) / (intensity + 1.0)) - 1.0
    chi = both([(factor * fr, factor * fi) for fr, fi in far], second, first)
    (pr0, pi0), (pr1, pi1) = probes
    (cr0, ci0), (cr1, ci1) = chi
    half = top.shape[1]
    for part, value in (
        (0, (pr0 * cr0 + pi0 * ci0) + (pr1 * cr1 + pi1 * ci1)),
        (1, (pr0 * ci0 - pi0 * cr0) + (pr1 * ci1 - pi1 * cr1)),
    ):
        gradient[part], top[part], bottom[part] = value, value[:half], value[half:]
    coverage = obj_real * obj_real + obj_imag * obj_imag
    rows = pattern // GROUP
    mate = lax.rem(lax.div(info[24], NEAR_STEP), GROUP)
    for step, keeper, (cr, ci) in ((step_own, slot, chi[0]), (step_other, 1 - slot, chi[1])):
        real = obj_real * cr + obj_imag * ci
        imag = obj_real * ci - obj_imag * cr
        for k in range(GROUP):
            start = k * rows
            block = step.at[mate ^ k]
            block[:rows] = real[start : start + rows]
            block[rows : 2 * rows] = imag[start : start + rows]
            middle = start + rows // 2
            block[2 * rows :] = jnp.where(
                keeper == 0, coverage[start:middle], coverage[middle : start + rows]
            )


def update_kernel(size, minibatch, info, strip_ref, illum, own, other, b0, a0, b1, a1, *outs):
    strip_out, *edges, tall = outs
    tiles, strip, pattern = size
    half = pattern // 2
    slot = info[25]
    kept = slice(pattern + half, pattern + half + strip)
    grads = (
        (0, slot, own, 0),
        (0, 1 - slot, other, 0),
        (-1, slot, b0, half),
        (1, slot, a0, 0),
        (-1, 1 - slot, b1, half),
        (1, 1 - slot, a1, 0),
    )
    for part in range(2):
        tall[kept] = jnp.zeros((strip, tall.shape[1]), F32)
        for side, place, ref, start in grads:
            row, column = spot(info, size, minibatch, side, place)
            add_at(tall, ref[part], row + pattern + start, column)
        fresh = strip_ref[part] + tall[kept] / (illum[...] + 1.0)
        strip_out[part] = fresh
        if edges:
            column_below = spot(info, size, minibatch + 1, -1, slot)[1]
            column_above = spot(info, size, minibatch + 1, 1, slot)[1]
            edges[0][part] = take_columns(fresh[:half], column_below, pattern)
            edges[1][part] = take_columns(fresh[strip - half :], column_above, pattern)


def probe_kernel(info, own_totals, other_totals, *refs):
    probes, outs = refs[: len(refs) // 2], refs[len(refs) // 2 :]
    slot = info[25]
    rows = outs[0].shape[1] // GROUP
    mate = lax.rem(lax.div(info[24], NEAR_STEP), GROUP)
    for k in range(GROUP):
        where = pl.ds(pl.multiple_of((mate ^ k) * rows, rows), rows)
        mine, theirs = own_totals[k], other_totals[k]
        own_half, other_half = mine[2 * rows :], theirs[theirs.shape[0] - rows // 2 :]
        coverage = jnp.concatenate(
            [
                jnp.where(slot == 0, own_half, other_half),
                jnp.where(slot == 0, other_half, own_half),
            ],
            axis=0,
        )
        divisor = coverage + 1.0
        for totals, probe, out in zip((mine, theirs), probes, outs):
            for part in range(2):
                change = totals[part * rows : (part + 1) * rows] / divisor
                out[part, where, :] = probe[part, where, :] + change


def call(kernel, name, outs, inputs, scratch=(), flops=0):
    shapes = [
        shape if isinstance(shape, jax.ShapeDtypeStruct) else jax.ShapeDtypeStruct(shape, F32)
        for shape in outs
    ]
    size = sum(value.size * value.dtype.itemsize for value in (*shapes, *inputs))
    smem = pl.BlockSpec(memory_space=pltpu.SMEM)
    vmem = pl.BlockSpec(memory_space=pltpu.VMEM)
    return pl.pallas_call(
        kernel,
        out_shape=shapes,
        in_specs=[smem] + [vmem] * (len(inputs) - 1),
        out_specs=[vmem] * len(shapes),
        scratch_shapes=[pltpu.VMEM(shape, F32) for shape in scratch],
        compiler_params=pltpu.CompilerParams(vmem_limit_bytes=VMEM_BYTES),
        cost_estimate=pl.CostEstimate(flops=flops, bytes_accessed=size, transcendentals=0),
        name=name,
    )(*inputs)


def shards_by_position(object_field, probe, positions, measured):
    strip = object_field.shape[1]
    width = object_field.shape[2]
    pattern = probe.shape[2]
    half = pattern // 2
    tiles = lax.axis_size("tile")
    size = (tiles, strip, pattern)
    field = (2, pattern, pattern)
    tall = (3 * pattern + strip + 8, width)
    window = (pattern + strip + 8, pattern)
    up = [(i, i + 1) for i in range(tiles - 1)]
    down = [(i + 1, i) for i in range(tiles - 1)]

    def swap(value):
        return lax.ppermute(value, "mode", [(0, 1), (1, 0)])

    def across(value, k):
        return lax.ppermute(value, "tile", [(i, i ^ k) for i in range(tiles)])

    def scatter(blocks, unit):
        mates = [across(blocks[k], unit * k) for k in range(1, GROUP)]
        return functools.reduce(jnp.add, mates, blocks[0])

    def exchange(piece):
        first, second, third = (across(piece, steps) for steps in FAR_STEPS)
        return (piece + first) + (second + third)

    def gather(piece, unit):
        return jnp.stack([piece] + [across(piece, unit * k) for k in range(1, GROUP)])

    def from_below(value):
        return lax.ppermute(value, "tile", up)

    def from_above(value):
        return lax.ppermute(value, "tile", down)

    def bind(kernel, *args):
        return functools.partial(kernel, *args)

    tile, slot = lax.axis_index("tile"), lax.axis_index("mode")
    index = jnp.stack([tile, slot]).astype(jnp.int32)
    here = jnp.concatenate([positions.ravel()] * 3 + [index])
    one_part = lax.dynamic_index_in_dim(object_field, slot, 0, keepdims=False)
    edges = [from_below(one_part[strip - half :]), from_above(one_part[:half])]
    below, above = from_below(positions), from_above(positions)
    other = swap(probe[0])
    own, observed, table = call(
        ready_kernel,
        "ready",
        [field, field, jax.ShapeDtypeStruct((4, pattern, pattern), BF16)],
        (here, probe[0], measured, jnp.asarray(table_of(pattern))),
    )
    *edges, below, above, own, observed, table = lax.optimization_barrier(
        (*edges, below, above, own, observed, table)
    )
    edges = [edges[0], swap(edges[0]), edges[1], swap(edges[1])]
    info = jnp.concatenate([below.ravel(), positions.ravel(), above.ravel(), index])

    for minibatch in range(2):
        last = minibatch == 1
        rows = pattern // GROUP
        blocks = (GROUP, 2 * rows + rows // 2, pattern)
        cut = (object_field, *edges)
        if last:
            cut = call(
                bind(patch_kernel, size, minibatch), "patch", [field], (here, *cut), [window], 10**10
            )
        rim = (2, half, pattern)
        gradient, top, bottom, step_own, step_other = call(
            bind(field_kernel, size, minibatch),
            "field",
            [field, rim, rim, blocks, blocks],
            (here, *cut, own, other, observed, table),
            [] if last else [window],
            flops=2 * 12 * 512**3,
        )
        (illum,) = call(
            bind(illumination_kernel, size, minibatch),
            "illumination",
            [(strip, width)],
            (info, own, other),
            [tall],
        )
        brought = swap(step_other)
        steps = [step_own[k] + brought[k] for k in range(GROUP)]
        piece = scatter(steps, NEAR_STEP)
        rim_below, rim_above = from_below(bottom), from_above(top)
        gradient, rim_below, rim_above, illum = lax.optimization_barrier(
            (gradient, rim_below, rim_above, illum)
        )
        rims = (gradient, swap(gradient), rim_below, rim_above, swap(rim_below), swap(rim_above))
        object_field, *edges = call(
            bind(update_kernel, size, minibatch),
            "update",
            [object_field.shape] + ([] if last else [rim] * 2),
            (info, object_field, illum, *rims),
            [tall],
        )
        piece = exchange(piece)
        if not last:
            edges = [from_below(edges[1]), from_above(edges[0])]
            piece, edges[0] = lax.optimization_barrier((piece, edges[0]))
        totals = gather(piece, NEAR_STEP)
        if last:
            totals, object_field = lax.optimization_barrier((totals, object_field))
            others = swap(totals[:, 2 * rows :])
            (own,) = call(probe_kernel, "probe", [field], (here, totals, others, own))
        else:
            own, other = call(
                probe_kernel, "probe", [field] * 2, (here, totals, swap(totals), own, other)
            )
    return (object_field, own[None])


def solution(mesh):
    in_specs = (
        P(None, "tile", None),
        P("mode", None, None, None),
        P(None, "tile", None),
        P(None, "tile", None, None),
    )
    out_specs = (P(None, "tile", None), P("mode", None, None, None))

    def whole(object_field, probe, positions, measured):
        tiles, pair = mesh.shape["tile"], mesh.shape["mode"]
        by_position = (
            pair == 2
            and probe.shape[0] == 2
            and positions.shape[:2] == (2, 2 * tiles)
            and tiles == GROUP * GROUP
            and probe.shape[2] % (16 * 2 * GROUP) == 0
            and object_field.shape[1] == tiles * probe.shape[2]
        )
        shards = shards_by_position if by_position else shards_by_mode
        return jax.shard_map(
            shards, mesh=mesh, in_specs=in_specs, out_specs=out_specs, check_vma=False
        )(object_field, probe, positions, measured)

    return whole
```

```python
import functools
import math

import jax
import jax.numpy as jnp
import numpy as np
from jax import lax
from jax.experimental import pallas as pl
from jax.experimental.pallas import tpu as pltpu
from jax.sharding import PartitionSpec as P

F32 = jnp.float32
BF16 = jnp.bfloat16
VMEM_BYTES = 12 * 1024 * 1024
GROUP = 4
NEAR_STEP = 2
FAR_STEPS = (1, 8, 9)


def padded(block, sides, width):
    for axis, dim in sides:
        count = lax.axis_size(axis)
        forward = [(i, i + 1) for i in range(count - 1)]
        backward = [(target, source) for source, target in forward]
        low = lax.ppermute(
            lax.slice_in_dim(block, block.shape[dim] - width, None, axis=dim), axis, forward
        )
        high = lax.ppermute(lax.slice_in_dim(block, 0, width, axis=dim), axis, backward)
        block = jnp.concatenate([low, block, high], axis=dim)
    return block


def tables(length):
    index_values = jnp.arange(length, dtype=jnp.int32)
    product = index_values[:, None] * index_values[None, :] % length
    angles = product.astype(jnp.float32) * (2.0 * math.pi / length)
    scaling = 1.0 / math.sqrt(length)
    return (jnp.cos(angles) * scaling, jnp.sin(angles) * scaling)


def apply_left(matrix, target):
    return jnp.einsum("ab,pbc->pac", matrix, target, precision=lax.Precision.HIGHEST)


def apply_right(target, matrix):
    return jnp.einsum("pab,bc->pac", target, matrix, precision=lax.Precision.HIGHEST)


def transform(real_part, imag_part, cosine, sine_table, direction):
    left_real = apply_left(cosine, real_part) + direction * apply_left(sine_table, imag_part)
    left_imag = apply_left(cosine, imag_part) - direction * apply_left(sine_table, real_part)
    out_real = apply_right(left_real, cosine) + direction * apply_right(left_imag, sine_table)
    out_imag = apply_right(left_imag, cosine) - direction * apply_right(left_real, sine_table)
    return (out_real, out_imag)


def place_add(target, placed, row_start, col_start):
    zero_index = jnp.int32(0)
    current = lax.dynamic_slice(target, (zero_index, row_start, col_start), placed.shape)
    return lax.dynamic_update_slice(target, current + placed, (zero_index, row_start, col_start))


def shards_by_mode(object_field, probe, positions, measured):
    strip_rows = object_field.shape[1]
    object_width = object_field.shape[2]
    pattern = probe.shape[2]
    half_pattern = pattern // 2
    count = positions.shape[1]
    cosine, sine_table = tables(pattern)
    tile_index = lax.axis_index("tile")
    offset = tile_index * strip_rows - half_pattern
    for minibatch in range(measured.shape[0]):
        extended = padded(object_field, (("tile", 1),), half_pattern)
        row_offsets = positions[minibatch, :, 0] - offset
        column_offsets = positions[minibatch, :, 1]

        def cut_one(row_start, col_start):
            return lax.dynamic_slice(
                extended, (jnp.int32(0), row_start, col_start), (2, pattern, pattern)
            )

        patches = jax.vmap(cut_one)(row_offsets, column_offsets)
        obj_real = patches[:, 0]
        obj_imag = patches[:, 1]
        probe_real = probe[0, 0]
        probe_imag = probe[0, 1]
        exit_real = probe_real * obj_real - probe_imag * obj_imag
        exit_imag = probe_real * obj_imag + probe_imag * obj_real
        far_real, far_imag = transform(exit_real, exit_imag, cosine, sine_table, 1.0)
        observed = measured[minibatch]
        intensity = lax.psum(far_real * far_real + far_imag * far_imag, "mode")
        modulus = jnp.sqrt((observed + 1.0) / (intensity + 1.0)) - 1.0
        chi_real, chi_imag = transform(
            modulus * far_real, modulus * far_imag, cosine, sine_table, -1.0
        )
        grad_real = probe_real * chi_real + probe_imag * chi_imag
        grad_imag = probe_real * chi_imag - probe_imag * chi_real
        probe_power = probe_real * probe_real + probe_imag * probe_imag
        step_real = jnp.sum(obj_real * chi_real + obj_imag * chi_imag, axis=0)
        step_imag = jnp.sum(obj_real * chi_imag - obj_imag * chi_real, axis=0)
        coverage = jnp.sum(obj_real * obj_real + obj_imag * obj_imag, axis=0)
        accumulated = jnp.zeros((3, strip_rows + pattern, object_width), jnp.float32)
        for position in range(count):
            placed = jnp.stack([grad_real[position], grad_imag[position], probe_power])
            accumulated = place_add(
                accumulated, placed, row_offsets[position], column_offsets[position]
            )
        rim_rows = jnp.concatenate(
            [accumulated[:, :half_pattern], accumulated[:, strip_rows + half_pattern :]], axis=1
        )
        received = padded(rim_rows, (("tile", 1),), half_pattern)
        own_strip = accumulated[:, half_pattern : half_pattern + strip_rows]
        own_strip = own_strip.at[:, :half_pattern].add(received[:, :half_pattern])
        own_strip = own_strip.at[:, strip_rows - half_pattern :].add(
            received[:, pattern + half_pattern :]
        )
        summed = lax.psum(own_strip, "mode")
        divisor = summed[2] + 1.0
        object_field = jnp.stack(
            [object_field[0] + summed[0] / divisor, object_field[1] + summed[1] / divisor]
        )
        step_stack = jnp.stack([jnp.stack([step_real, step_imag])])
        step_total, coverage_total = lax.psum((step_stack, coverage), "tile")
        probe = probe + step_total / (coverage_total + 1.0)
    return (object_field, probe)


def table_of(length):
    index_values = np.arange(length)
    angles = (index_values[:, None] * index_values[None, :] % length) * (2.0 * np.pi / length)
    scaling = 1.0 / np.sqrt(length)
    return np.stack([np.cos(angles) * scaling, np.sin(angles) * scaling]).astype(np.float32)


def spot(info, size, minibatch, side, slot):
    tiles, strip, pattern = size
    place = (((side + 1) * 2 + minibatch) * 2 + slot) * 2
    tile = info[24]
    row = info[place] - tile * strip + pattern // 2
    if side < 0:
        row = jnp.where(tile == 0, -pattern, row)
    if side > 0:
        row = jnp.where(tile == tiles - 1, strip + pattern, row)
    return row, info[place + 1]


def take_columns(block, column, width):
    total = block.shape[-1]
    return pltpu.roll(block, lax.rem(total - column, total), 1)[:, :width]


def add_at(tall, block, row, column):
    rows, width = block.shape
    total = tall.shape[1]
    shift = lax.rem(row, 8)
    start = pl.multiple_of(row - shift, 8)
    turned = pltpu.roll(block.reshape(rows // 8, 8, width), shift, 1)
    empty = jnp.zeros((1, 8, width), block.dtype)
    inside = lax.broadcasted_iota(jnp.int32, (rows // 8 + 1, 8, width), 1) >= shift
    moved = jnp.where(
        inside,
        jnp.concatenate([turned, empty], axis=0),
        jnp.concatenate([empty, turned], axis=0),
    ).reshape(rows + 8, width)
    wide = jnp.concatenate([moved, jnp.zeros((rows + 8, total - width), block.dtype)], axis=1)
    tall[pl.ds(start, rows + 8), :] += pltpu.roll(wide, column, 1)


def rows_at(ref, row, rows):
    width = ref.shape[1]
    shift = lax.rem(row, 8)
    start = pl.multiple_of(row - shift, 8)
    block = ref[pl.ds(start, rows + 8), :].reshape(rows // 8 + 1, 8, width)
    turned = pltpu.roll(block, lax.rem(8 - shift, 8), 1)
    inside = lax.broadcasted_iota(jnp.int32, (rows // 8, 8, width), 1) < 8 - shift
    return jnp.where(inside, turned[:-1], turned[1:]).reshape(rows, width)


def halves(value):
    high = value.astype(BF16)
    return high, (value - high.astype(F32)).astype(BF16)


def product(left, right):
    dot = functools.partial(jnp.dot, preferred_element_type=F32)
    return dot(left[0], right[0]) + (dot(left[0], right[1]) + dot(left[1], right[0]))


def cut_patch(size, info, minibatch, strip_ref, below, above, window, part):
    tiles, rows, width = size
    half = width // 2
    row, column = spot(info, size, minibatch, 0, info[25])

    def columns(block):
        return block if block.shape[1] == width else take_columns(block, column, width)

    window[:half] = columns(below)
    window[half : half + rows] = columns(strip_ref[part])
    window[half + rows : rows + width] = columns(above)
    return rows_at(window, row, width)


def illumination_kernel(size, minibatch, info, own, other, out, tall):
    tiles, strip, pattern = size
    half = pattern // 2
    kept = slice(pattern + half, pattern + half + strip)
    tall[kept] = jnp.zeros((strip, tall.shape[1]), F32)
    (pr0, pi0), (pr1, pi1) = ((ref[0], ref[1]) for ref in (own, other))
    power = pr0 * pr0 + pi0 * pi0 + (pr1 * pr1 + pi1 * pi1)
    for side in (-1, 0, 1):
        for slot in range(2):
            row, column = spot(info, size, minibatch, side, slot)
            add_at(tall, power, row + pattern, column)
    out[...] = tall[kept]


def patch_kernel(size, minibatch, info, strip_ref, below, above, patch, window):
    for part in range(2):
        patch[part] = cut_patch(
            size, info, minibatch, strip_ref, below[part], above[part], window, part
        )


def ready_kernel(size, info, strip_ref, probe, measured, table, columns, own, observed, split):
    own[...] = probe[...]
    column = spot(info, size, 0, 0, info[25])[1]
    for part in range(2):
        columns[part] = take_columns(strip_ref[part], column, size[2])
    for minibatch in range(2):
        observed[minibatch] = measured[minibatch, info[25]]
    for i in range(2):
        split[2 * i], split[2 * i + 1] = halves(table[i])


def field_kernel(size, minibatch, info, strip_ref, *refs):
    tiles, strip, pattern = size
    slot = info[25]
    if minibatch:
        own, other, measured, table, gradient, top, bottom, step_own, step_other = refs
        obj_real, obj_imag = strip_ref[0], strip_ref[1]
    else:
        *edges, own, other, measured, table = refs[:-6]
        gradient, top, bottom, step_own, step_other, window = refs[-6:]
        sides = (jnp.where(slot == 0, edges[i][...], edges[i + 1][...]) for i in (0, 2))
        others = (jnp.where(slot == 0, edges[i + 1][...], edges[i][...]) for i in (0, 2))
        obj_real, obj_imag = (
            cut_patch(size, info, minibatch, strip_ref, *ends, window, part)
            for part, ends in enumerate((sides, others))
        )
    cos_high, cos_low, sin_high, sin_low = (table[i] for i in range(4))

    def block(top_left, top_right, low_left, low_right):
        return jnp.concatenate(
            [
                jnp.concatenate([top_left, top_right], axis=1),
                jnp.concatenate([low_left, low_right], axis=1),
            ],
            axis=0,
        )

    first = (
        block(cos_high, sin_high, -sin_high, cos_high),
        block(cos_low, sin_low, -sin_low, cos_low),
    )
    second = (
        block(cos_high, -sin_high, sin_high, cos_high),
        block(cos_low, -sin_low, sin_low, cos_low),
    )
    probes = [(ref[0], ref[1]) for ref in (own, other)]

    def both(fields, left, right):
        (r0, i0), (r1, i1) = fields
        y = product(left, halves(block(r0, r1, i0, i1)))
        y = block(
            y[:pattern, :pattern], y[pattern:, :pattern], y[:pattern, pattern:], y[pattern:, pattern:]
        )
        y = product(halves(y), right)
        return (
            (y[:pattern, :pattern], y[:pattern, pattern:]),
            (y[pattern:, :pattern], y[pattern:, pattern:]),
        )

    exits = [(pr * obj_real - pi * obj_imag, pr * obj_imag + pi * obj_real) for pr, pi in probes]
    far = both(exits, first, second)
    intensity = (far[0][0] * far[0][0] + far[0][1] * far[0][1]) + (
        far[1][0] * far[1][0] + far[1][1] * far[1][1]
    )
    factor = jnp.sqrt((measured[minibatch] + 1.0) / (intensity + 1.0)) - 1.0
    chi = both([(factor * fr, factor * fi) for fr, fi in far], second, first)
    (pr0, pi0), (pr1, pi1) = probes
    (cr0, ci0), (cr1, ci1) = chi
    half = top.shape[1]
    for part, value in (
        (0, (pr0 * cr0 + pi0 * ci0) + (pr1 * cr1 + pi1 * ci1)),
        (1, (pr0 * ci0 - pi0 * cr0) + (pr1 * ci1 - pi1 * cr1)),
    ):
        gradient[part], top[part], bottom[part] = value, value[:half], value[half:]
    coverage = obj_real * obj_real + obj_imag * obj_imag
    rows = pattern // GROUP
    mate = lax.rem(lax.div(info[24], NEAR_STEP), GROUP)
    for step, keeper, (cr, ci) in ((step_own, slot, chi[0]), (step_other, 1 - slot, chi[1])):
        real = obj_real * cr + obj_imag * ci
        imag = obj_real * ci - obj_imag * cr
        for k in range(GROUP):
            start = k * rows
            block = step.at[mate ^ k]
            block[:rows] = real[start : start + rows]
            block[rows : 2 * rows] = imag[start : start + rows]
            middle = start + rows // 2
            block[2 * rows :] = jnp.where(
                keeper == 0, coverage[start:middle], coverage[middle : start + rows]
            )


def update_kernel(size, minibatch, info, strip_ref, illum, own, other, b0, a0, b1, a1, *outs):
    strip_out, *edges, tall = outs
    tiles, strip, pattern = size
    half = pattern // 2
    slot = info[25]
    kept = slice(pattern + half, pattern + half + strip)
    grads = (
        (0, slot, own, 0),
        (0, 1 - slot, other, 0),
        (-1, slot, b0, half),
        (1, slot, a0, 0),
        (-1, 1 - slot, b1, half),
        (1, 1 - slot, a1, 0),
    )
    for part in range(2):
        tall[kept] = jnp.zeros((strip, tall.shape[1]), F32)
        for side, place, ref, start in grads:
            row, column = spot(info, size, minibatch, side, place)
            add_at(tall, ref[part], row + pattern + start, column)
        fresh = strip_ref[part] + tall[kept] / (illum[...] + 1.0)
        strip_out[part] = fresh
        if edges:
            column_below = spot(info, size, minibatch + 1, -1, slot)[1]
            column_above = spot(info, size, minibatch + 1, 1, slot)[1]
            edges[0][part] = take_columns(fresh[:half], column_below, pattern)
            edges[1][part] = take_columns(fresh[strip - half :], column_above, pattern)


def probe_kernel(info, own_totals, other_totals, *refs):
    probes, outs = refs[: len(refs) // 2], refs[len(refs) // 2 :]
    slot = info[25]
    rows = outs[0].shape[1] // GROUP
    mate = lax.rem(lax.div(info[24], NEAR_STEP), GROUP)
    for k in range(GROUP):
        where = pl.ds(pl.multiple_of((mate ^ k) * rows, rows), rows)
        mine, theirs = own_totals[k], other_totals[k]
        own_half, other_half = mine[2 * rows :], theirs[theirs.shape[0] - rows // 2 :]
        coverage = jnp.concatenate(
            [
                jnp.where(slot == 0, own_half, other_half),
                jnp.where(slot == 0, other_half, own_half),
            ],
            axis=0,
        )
        divisor = coverage + 1.0
        for totals, probe, out in zip((mine, theirs), probes, outs):
            for part in range(2):
                change = totals[part * rows : (part + 1) * rows] / divisor
                out[part, where, :] = probe[part, where, :] + change


def call(kernel, name, outs, inputs, scratch=(), flops=0):
    shapes = [
        shape if isinstance(shape, jax.ShapeDtypeStruct) else jax.ShapeDtypeStruct(shape, F32)
        for shape in outs
    ]
    size = sum(value.size * value.dtype.itemsize for value in (*shapes, *inputs))
    smem = pl.BlockSpec(memory_space=pltpu.SMEM)
    vmem = pl.BlockSpec(memory_space=pltpu.VMEM)
    return pl.pallas_call(
        kernel,
        out_shape=shapes,
        in_specs=[smem] + [vmem] * (len(inputs) - 1),
        out_specs=[vmem] * len(shapes),
        scratch_shapes=[pltpu.VMEM(shape, F32) for shape in scratch],
        compiler_params=pltpu.CompilerParams(vmem_limit_bytes=VMEM_BYTES),
        cost_estimate=pl.CostEstimate(flops=flops, bytes_accessed=size, transcendentals=0),
        name=name,
    )(*inputs)


def shards_by_position(object_field, probe, positions, measured):
    strip = object_field.shape[1]
    width = object_field.shape[2]
    pattern = probe.shape[2]
    half = pattern // 2
    tiles = lax.axis_size("tile")
    size = (tiles, strip, pattern)
    field = (2, pattern, pattern)
    tall = (3 * pattern + strip + 8, width)
    window = (pattern + strip + 8, pattern)
    up = [(i, i + 1) for i in range(tiles - 1)]
    down = [(i + 1, i) for i in range(tiles - 1)]

    def swap(value):
        return lax.ppermute(value, "mode", [(0, 1), (1, 0)])

    def across(value, k):
        return lax.ppermute(value, "tile", [(i, i ^ k) for i in range(tiles)])

    def scatter(blocks, unit):
        mates = [across(blocks[k], unit * k) for k in range(1, GROUP)]
        return functools.reduce(jnp.add, mates, blocks[0])

    def exchange(piece):
        first, second, third = (across(piece, steps) for steps in FAR_STEPS)
        return (piece + first) + (second + third)

    def gather(piece, unit):
        return jnp.stack([piece] + [across(piece, unit * k) for k in range(1, GROUP)])

    def from_below(value):
        return lax.ppermute(value, "tile", up)

    def from_above(value):
        return lax.ppermute(value, "tile", down)

    def bind(kernel, *args):
        return functools.partial(kernel, *args)

    tile, slot = lax.axis_index("tile"), lax.axis_index("mode")
    index = jnp.stack([tile, slot]).astype(jnp.int32)
    here = jnp.concatenate([positions.ravel()] * 3 + [index])
    one_part = lax.dynamic_index_in_dim(object_field, slot, 0, keepdims=False)
    edges = [from_below(one_part[strip - half :]), from_above(one_part[:half])]
    below, above = from_below(positions), from_above(positions)
    other = swap(probe[0])
    columns, own, observed, table = call(
        bind(ready_kernel, size),
        "ready",
        [(2, strip, pattern), field, field, jax.ShapeDtypeStruct((4, pattern, pattern), BF16)],
        (here, object_field, probe[0], measured, jnp.asarray(table_of(pattern))),
    )
    *edges, below, above, columns, own, observed, table = lax.optimization_barrier(
        (*edges, below, above, columns, own, observed, table)
    )
    edges = [edges[0], swap(edges[0]), edges[1], swap(edges[1])]
    info = jnp.concatenate([below.ravel(), positions.ravel(), above.ravel(), index])

    for minibatch in range(2):
        last = minibatch == 1
        rows = pattern // GROUP
        blocks = (GROUP, 2 * rows + rows // 2, pattern)
        cut = (columns, *edges)
        if last:
            cut = (object_field, *edges)
            cut = call(
                bind(patch_kernel, size, minibatch), "patch", [field], (here, *cut), [window], 10**10
            )
        rim = (2, half, pattern)
        gradient, top, bottom, step_own, step_other = call(
            bind(field_kernel, size, minibatch),
            "field",
            [field, rim, rim, blocks, blocks],
            (here, *cut, own, other, observed, table),
            [] if last else [window],
            flops=2 * 12 * 512**3,
        )
        (illum,) = call(
            bind(illumination_kernel, size, minibatch),
            "illumination",
            [(strip, width)],
            (info, own, other),
            [tall],
        )
        brought = swap(step_other)
        steps = [step_own[k] + brought[k] for k in range(GROUP)]
        piece = scatter(steps, NEAR_STEP)
        rim_below, rim_above = from_below(bottom), from_above(top)
        gradient, rim_below, rim_above, illum = lax.optimization_barrier(
            (gradient, rim_below, rim_above, illum)
        )
        rims = (gradient, swap(gradient), rim_below, rim_above, swap(rim_below), swap(rim_above))
        object_field, *edges = call(
            bind(update_kernel, size, minibatch),
            "update",
            [object_field.shape] + ([] if last else [rim] * 2),
            (info, object_field, illum, *rims),
            [tall],
        )
        piece = exchange(piece)
        if not last:
            edges = [from_below(edges[1]), from_above(edges[0])]
            piece, edges[0] = lax.optimization_barrier((piece, edges[0]))
        totals = gather(piece, NEAR_STEP)
        if last:
            totals, object_field = lax.optimization_barrier((totals, object_field))
            others = swap(totals[:, 2 * rows :])
            (own,) = call(probe_kernel, "probe", [field], (here, totals, others, own))
        else:
            own, other = call(
                probe_kernel, "probe", [field] * 2, (here, totals, swap(totals), own, other)
            )
    return (object_field, own[None])


def solution(mesh):
    in_specs = (
        P(None, "tile", None),
        P("mode", None, None, None),
        P(None, "tile", None),
        P(None, "tile", None, None),
    )
    out_specs = (P(None, "tile", None), P("mode", None, None, None))

    def whole(object_field, probe, positions, measured):
        tiles, pair = mesh.shape["tile"], mesh.shape["mode"]
        by_position = (
            pair == 2
            and probe.shape[0] == 2
            and positions.shape[:2] == (2, 2 * tiles)
            and tiles == GROUP * GROUP
            and probe.shape[2] % (16 * 2 * GROUP) == 0
            and object_field.shape[1] == tiles * probe.shape[2]
        )
        shards = shards_by_position if by_position else shards_by_mode
        return jax.shard_map(
            shards, mesh=mesh, in_specs=in_specs, out_specs=out_specs, check_vma=False
        )(object_field, probe, positions, measured)

    return whole
```

```python
import functools
import math

import jax
import jax.numpy as jnp
import numpy as np
from jax import lax
from jax.experimental import pallas as pl
from jax.experimental.pallas import tpu as pltpu
from jax.sharding import PartitionSpec as P

F32 = jnp.float32
BF16 = jnp.bfloat16
VMEM_BYTES = 16 * 1024 * 1024
GROUP = 4
NEAR_STEP = (2, 1)
FAR_STEPS = ((1, 8, 9), (4, 8, 12))


def padded(block, sides, width):
    for axis, dim in sides:
        count = lax.axis_size(axis)
        forward = [(i, i + 1) for i in range(count - 1)]
        backward = [(target, source) for source, target in forward]
        low = lax.ppermute(
            lax.slice_in_dim(block, block.shape[dim] - width, None, axis=dim), axis, forward
        )
        high = lax.ppermute(lax.slice_in_dim(block, 0, width, axis=dim), axis, backward)
        block = jnp.concatenate([low, block, high], axis=dim)
    return block


def tables(length):
    index_values = jnp.arange(length, dtype=jnp.int32)
    product = index_values[:, None] * index_values[None, :] % length
    angles = product.astype(jnp.float32) * (2.0 * math.pi / length)
    scaling = 1.0 / math.sqrt(length)
    return (jnp.cos(angles) * scaling, jnp.sin(angles) * scaling)


def apply_left(matrix, target):
    return jnp.einsum("ab,pbc->pac", matrix, target, precision=lax.Precision.HIGHEST)


def apply_right(target, matrix):
    return jnp.einsum("pab,bc->pac", target, matrix, precision=lax.Precision.HIGHEST)


def transform(real_part, imag_part, cosine, sine_table, direction):
    left_real = apply_left(cosine, real_part) + direction * apply_left(sine_table, imag_part)
    left_imag = apply_left(cosine, imag_part) - direction * apply_left(sine_table, real_part)
    out_real = apply_right(left_real, cosine) + direction * apply_right(left_imag, sine_table)
    out_imag = apply_right(left_imag, cosine) - direction * apply_right(left_real, sine_table)
    return (out_real, out_imag)


def place_add(target, placed, row_start, col_start):
    zero_index = jnp.int32(0)
    current = lax.dynamic_slice(target, (zero_index, row_start, col_start), placed.shape)
    return lax.dynamic_update_slice(target, current + placed, (zero_index, row_start, col_start))


def shards_by_mode(object_field, probe, positions, measured):
    strip_rows = object_field.shape[1]
    object_width = object_field.shape[2]
    pattern = probe.shape[2]
    half_pattern = pattern // 2
    count = positions.shape[1]
    cosine, sine_table = tables(pattern)
    tile_index = lax.axis_index("tile")
    offset = tile_index * strip_rows - half_pattern
    for minibatch in range(measured.shape[0]):
        extended = padded(object_field, (("tile", 1),), half_pattern)
        row_offsets = positions[minibatch, :, 0] - offset
        column_offsets = positions[minibatch, :, 1]

        def cut_one(row_start, col_start):
            return lax.dynamic_slice(
                extended, (jnp.int32(0), row_start, col_start), (2, pattern, pattern)
            )

        patches = jax.vmap(cut_one)(row_offsets, column_offsets)
        obj_real = patches[:, 0]
        obj_imag = patches[:, 1]
        probe_real = probe[0, 0]
        probe_imag = probe[0, 1]
        exit_real = probe_real * obj_real - probe_imag * obj_imag
        exit_imag = probe_real * obj_imag + probe_imag * obj_real
        far_real, far_imag = transform(exit_real, exit_imag, cosine, sine_table, 1.0)
        observed = measured[minibatch]
        intensity = lax.psum(far_real * far_real + far_imag * far_imag, "mode")
        modulus = jnp.sqrt((observed + 1.0) / (intensity + 1.0)) - 1.0
        chi_real, chi_imag = transform(
            modulus * far_real, modulus * far_imag, cosine, sine_table, -1.0
        )
        grad_real = probe_real * chi_real + probe_imag * chi_imag
        grad_imag = probe_real * chi_imag - probe_imag * chi_real
        probe_power = probe_real * probe_real + probe_imag * probe_imag
        step_real = jnp.sum(obj_real * chi_real + obj_imag * chi_imag, axis=0)
        step_imag = jnp.sum(obj_real * chi_imag - obj_imag * chi_real, axis=0)
        coverage = jnp.sum(obj_real * obj_real + obj_imag * obj_imag, axis=0)
        accumulated = jnp.zeros((3, strip_rows + pattern, object_width), jnp.float32)
        for position in range(count):
            placed = jnp.stack([grad_real[position], grad_imag[position], probe_power])
            accumulated = place_add(
                accumulated, placed, row_offsets[position], column_offsets[position]
            )
        rim_rows = jnp.concatenate(
            [accumulated[:, :half_pattern], accumulated[:, strip_rows + half_pattern :]], axis=1
        )
        received = padded(rim_rows, (("tile", 1),), half_pattern)
        own_strip = accumulated[:, half_pattern : half_pattern + strip_rows]
        own_strip = own_strip.at[:, :half_pattern].add(received[:, :half_pattern])
        own_strip = own_strip.at[:, strip_rows - half_pattern :].add(
            received[:, pattern + half_pattern :]
        )
        summed = lax.psum(own_strip, "mode")
        divisor = summed[2] + 1.0
        object_field = jnp.stack(
            [object_field[0] + summed[0] / divisor, object_field[1] + summed[1] / divisor]
        )
        step_stack = jnp.stack([jnp.stack([step_real, step_imag])])
        step_total, coverage_total = lax.psum((step_stack, coverage), "tile")
        probe = probe + step_total / (coverage_total + 1.0)
    return (object_field, probe)


def table_of(length):
    index_values = np.arange(length)
    angles = (index_values[:, None] * index_values[None, :] % length) * (2.0 * np.pi / length)
    scaling = 1.0 / np.sqrt(length)
    return np.stack([np.cos(angles) * scaling, np.sin(angles) * scaling]).astype(np.float32)


def spot(info, size, minibatch, side, slot):
    tiles, strip, pattern = size
    place = (((side + 1) * 2 + minibatch) * 2 + slot) * 2
    tile = info[24]
    row = info[place] - tile * strip + pattern // 2
    if side < 0:
        row = jnp.where(tile == 0, -pattern, row)
    if side > 0:
        row = jnp.where(tile == tiles - 1, strip + pattern, row)
    return row, info[place + 1]


def take_columns(block, column, width):
    total = block.shape[-1]
    return pltpu.roll(block, lax.rem(total - column, total), 1)[:, :width]


def add_at(tall, block, row, column):
    rows, width = block.shape
    total = tall.shape[1]
    shift = lax.rem(row, 8)
    start = pl.multiple_of(row - shift, 8)
    turned = pltpu.roll(block.reshape(rows // 8, 8, width), shift, 1)
    empty = jnp.zeros((1, 8, width), block.dtype)
    inside = lax.broadcasted_iota(jnp.int32, (rows // 8 + 1, 8, width), 1) >= shift
    moved = jnp.where(
        inside,
        jnp.concatenate([turned, empty], axis=0),
        jnp.concatenate([empty, turned], axis=0),
    ).reshape(rows + 8, width)
    wide = jnp.concatenate([moved, jnp.zeros((rows + 8, total - width), block.dtype)], axis=1)
    tall[pl.ds(start, rows + 8), :] += pltpu.roll(wide, column, 1)


def rows_at(ref, row, rows):
    width = ref.shape[1]
    shift = lax.rem(row, 8)
    start = pl.multiple_of(row - shift, 8)
    block = ref[pl.ds(start, rows + 8), :].reshape(rows // 8 + 1, 8, width)
    turned = pltpu.roll(block, lax.rem(8 - shift, 8), 1)
    inside = lax.broadcasted_iota(jnp.int32, (rows // 8, 8, width), 1) < 8 - shift
    return jnp.where(inside, turned[:-1], turned[1:]).reshape(rows, width)


def halves(value):
    high = value.astype(BF16)
    return high, (value - high.astype(F32)).astype(BF16)


def product(left, right):
    dot = functools.partial(jnp.dot, preferred_element_type=F32)
    return dot(left[0], right[0]) + (dot(left[0], right[1]) + dot(left[1], right[0]))


def cut_patch(size, info, minibatch, strip_ref, below, above, window, part):
    tiles, rows, width = size
    half = width // 2
    row, column = spot(info, size, minibatch, 0, info[25])

    def columns(block):
        return block if block.shape[1] == width else take_columns(block, column, width)

    window[:half] = columns(below)
    window[half : half + rows] = columns(strip_ref[part])
    window[half + rows : rows + width] = columns(above)
    return rows_at(window, row, width)


def illumination_kernel(size, minibatch, info, own, other, out, tall):
    tiles, strip, pattern = size
    half = pattern // 2
    kept = slice(pattern + half, pattern + half + strip)
    tall[kept] = jnp.zeros((strip, tall.shape[1]), F32)
    (pr0, pi0), (pr1, pi1) = ((ref[0], ref[1]) for ref in (own, other))
    power = pr0 * pr0 + pi0 * pi0 + (pr1 * pr1 + pi1 * pi1)
    for side in (-1, 0, 1):
        for slot in range(2):
            row, column = spot(info, size, minibatch, side, slot)
            add_at(tall, power, row + pattern, column)
    out[...] = tall[kept]


def patch_kernel(size, minibatch, info, strip_ref, below, above, patch, window):
    for part in range(2):
        patch[part] = cut_patch(
            size, info, minibatch, strip_ref, below[part], above[part], window, part
        )


def ready_kernel(info, probe, measured, table, own, observed, split):
    own[...] = probe[...]
    for minibatch in range(2):
        observed[minibatch] = measured[minibatch, info[25]]
    for i in range(2):
        split[2 * i], split[2 * i + 1] = halves(table[i])


def field_kernel(size, minibatch, info, strip_ref, *refs):
    tiles, strip, pattern = size
    slot = info[25]
    if minibatch:
        own, other, measured, table, gradient, top, bottom, step_own, step_other = refs
        obj_real, obj_imag = strip_ref[0], strip_ref[1]
    else:
        *edges, own, other, measured, table = refs[:-6]
        gradient, top, bottom, step_own, step_other, window = refs[-6:]
        sides = (jnp.where(slot == 0, edges[i][...], edges[i + 1][...]) for i in (0, 2))
        others = (jnp.where(slot == 0, edges[i + 1][...], edges[i][...]) for i in (0, 2))
        obj_real, obj_imag = (
            cut_patch(size, info, minibatch, strip_ref, *ends, window, part)
            for part, ends in enumerate((sides, others))
        )
    cos_high, cos_low, sin_high, sin_low = (table[i] for i in range(4))

    def block(top_left, top_right, low_left, low_right):
        return jnp.concatenate(
            [
                jnp.concatenate([top_left, top_right], axis=1),
                jnp.concatenate([low_left, low_right], axis=1),
            ],
            axis=0,
        )

    first = (
        block(cos_high, sin_high, -sin_high, cos_high),
        block(cos_low, sin_low, -sin_low, cos_low),
    )
    second = (
        block(cos_high, -sin_high, sin_high, cos_high),
        block(cos_low, -sin_low, sin_low, cos_low),
    )
    probes = [(ref[0], ref[1]) for ref in (own, other)]

    def both(fields, left, right):
        (r0, i0), (r1, i1) = fields
        y = product(left, halves(block(r0, r1, i0, i1)))
        y = block(
            y[:pattern, :pattern], y[pattern:, :pattern], y[:pattern, pattern:], y[pattern:, pattern:]
        )
        y = product(halves(y), right)
        return (
            (y[:pattern, :pattern], y[:pattern, pattern:]),
            (y[pattern:, :pattern], y[pattern:, pattern:]),
        )

    exits = [(pr * obj_real - pi * obj_imag, pr * obj_imag + pi * obj_real) for pr, pi in probes]
    far = both(exits, first, second)
    intensity = (far[0][0] * far[0][0] + far[0][1] * far[0][1]) + (
        far[1][0] * far[1][0] + far[1][1] * far[1][1]
    )
    factor = jnp.sqrt((measured[minibatch] + 1.0) / (intensity + 1.0)) - 1.0
    chi = both([(factor * fr, factor * fi) for fr, fi in far], second, first)
    (pr0, pi0), (pr1, pi1) = probes
    (cr0, ci0), (cr1, ci1) = chi
    half = top.shape[1]
    for part, value in (
        (0, (pr0 * cr0 + pi0 * ci0) + (pr1 * cr1 + pi1 * ci1)),
        (1, (pr0 * ci0 - pi0 * cr0) + (pr1 * ci1 - pi1 * cr1)),
    ):
        gradient[part], top[part], bottom[part] = value, value[:half], value[half:]
    coverage = obj_real * obj_real + obj_imag * obj_imag
    rows = pattern // GROUP
    mate = lax.rem(lax.div(info[24], NEAR_STEP[minibatch]), GROUP)
    for step, keeper, (cr, ci) in ((step_own, slot, chi[0]), (step_other, 1 - slot, chi[1])):
        real = obj_real * cr + obj_imag * ci
        imag = obj_real * ci - obj_imag * cr
        for k in range(GROUP):
            start = k * rows
            block = step.at[mate ^ k]
            block[:rows] = real[start : start + rows]
            block[rows : 2 * rows] = imag[start : start + rows]
            middle = start + rows // 2
            block[2 * rows :] = jnp.where(
                keeper == 0, coverage[start:middle], coverage[middle : start + rows]
            )


def update_kernel(size, minibatch, info, strip_ref, illum, own, other, b0, a0, b1, a1, *outs):
    strip_out, *edges, tall = outs
    tiles, strip, pattern = size
    half = pattern // 2
    slot = info[25]
    kept = slice(pattern + half, pattern + half + strip)
    grads = (
        (0, slot, own, 0),
        (0, 1 - slot, other, 0),
        (-1, slot, b0, half),
        (1, slot, a0, 0),
        (-1, 1 - slot, b1, half),
        (1, 1 - slot, a1, 0),
    )
    for part in range(2):
        tall[kept] = jnp.zeros((strip, tall.shape[1]), F32)
        for side, place, ref, start in grads:
            row, column = spot(info, size, minibatch, side, place)
            add_at(tall, ref[part], row + pattern + start, column)
        fresh = strip_ref[part] + tall[kept] / (illum[...] + 1.0)
        strip_out[part] = fresh
        if edges:
            column_below = spot(info, size, minibatch + 1, -1, slot)[1]
            column_above = spot(info, size, minibatch + 1, 1, slot)[1]
            edges[0][part] = take_columns(fresh[:half], column_below, pattern)
            edges[1][part] = take_columns(fresh[strip - half :], column_above, pattern)


def probe_kernel(minibatch, info, own_totals, other_totals, *refs):
    probes, outs = refs[: len(refs) // 2], refs[len(refs) // 2 :]
    slot = info[25]
    rows = outs[0].shape[1] // GROUP
    mate = lax.rem(lax.div(info[24], NEAR_STEP[minibatch]), GROUP)
    for k in range(GROUP):
        where = pl.ds(pl.multiple_of((mate ^ k) * rows, rows), rows)
        mine, theirs = own_totals[k], other_totals[k]
        own_half, other_half = mine[2 * rows :], theirs[theirs.shape[0] - rows // 2 :]
        coverage = jnp.concatenate(
            [
                jnp.where(slot == 0, own_half, other_half),
                jnp.where(slot == 0, other_half, own_half),
            ],
            axis=0,
        )
        divisor = coverage + 1.0
        for totals, probe, out in zip((mine, theirs), probes, outs):
            for part in range(2):
                change = totals[part * rows : (part + 1) * rows] / divisor
                out[part, where, :] = probe[part, where, :] + change


def call(kernel, name, outs, inputs, scratch=(), flops=0):
    shapes = [
        shape if isinstance(shape, jax.ShapeDtypeStruct) else jax.ShapeDtypeStruct(shape, F32)
        for shape in outs
    ]
    size = sum(value.size * value.dtype.itemsize for value in (*shapes, *inputs))
    smem = pl.BlockSpec(memory_space=pltpu.SMEM)
    vmem = pl.BlockSpec(memory_space=pltpu.VMEM)
    return pl.pallas_call(
        kernel,
        out_shape=shapes,
        in_specs=[smem] + [vmem] * (len(inputs) - 1),
        out_specs=[vmem] * len(shapes),
        scratch_shapes=[pltpu.VMEM(shape, F32) for shape in scratch],
        compiler_params=pltpu.CompilerParams(vmem_limit_bytes=VMEM_BYTES),
        cost_estimate=pl.CostEstimate(flops=flops, bytes_accessed=size, transcendentals=0),
        name=name,
    )(*inputs)


def shards_by_position(object_field, probe, positions, measured):
    strip = object_field.shape[1]
    width = object_field.shape[2]
    pattern = probe.shape[2]
    half = pattern // 2
    tiles = lax.axis_size("tile")
    size = (tiles, strip, pattern)
    field = (2, pattern, pattern)
    tall = (3 * pattern + strip + 8, width)
    window = (pattern + strip + 8, pattern)
    up = [(i, i + 1) for i in range(tiles - 1)]
    down = [(i + 1, i) for i in range(tiles - 1)]

    def swap(value):
        return lax.ppermute(value, "mode", [(0, 1), (1, 0)])

    def across(value, k):
        return lax.ppermute(value, "tile", [(i, i ^ k) for i in range(tiles)])

    def scatter(blocks, unit):
        mates = [across(blocks[k], unit * k) for k in range(1, GROUP)]
        return functools.reduce(jnp.add, mates, blocks[0])

    def exchange(piece, far_steps):
        first, second, third = (across(piece, steps) for steps in far_steps)
        return (piece + first) + (second + third)

    def gather(piece, unit):
        return jnp.stack([piece] + [across(piece, unit * k) for k in range(1, GROUP)])

    def from_below(value):
        return lax.ppermute(value, "tile", up)

    def from_above(value):
        return lax.ppermute(value, "tile", down)

    def bind(kernel, *args):
        return functools.partial(kernel, *args)

    tile, slot = lax.axis_index("tile"), lax.axis_index("mode")
    index = jnp.stack([tile, slot]).astype(jnp.int32)
    here = jnp.concatenate([positions.ravel()] * 3 + [index])
    one_part = lax.dynamic_index_in_dim(object_field, slot, 0, keepdims=False)
    edges = [from_below(one_part[strip - half :]), from_above(one_part[:half])]
    below, above = from_below(positions), from_above(positions)
    other = swap(probe[0])
    own, observed, table = call(
        ready_kernel,
        "ready",
        [field, field, jax.ShapeDtypeStruct((4, pattern, pattern), BF16)],
        (here, probe[0], measured, jnp.asarray(table_of(pattern))),
    )
    *edges, below, above, own, observed, table = lax.optimization_barrier(
        (*edges, below, above, own, observed, table)
    )
    edges = [edges[0], swap(edges[0]), edges[1], swap(edges[1])]
    info = jnp.concatenate([below.ravel(), positions.ravel(), above.ravel(), index])

    for minibatch in range(2):
        last = minibatch == 1
        rows = pattern // GROUP
        blocks = (GROUP, 2 * rows + rows // 2, pattern)
        cut = (object_field, *edges)
        if last:
            cut = call(
                bind(patch_kernel, size, minibatch), "patch", [field], (here, *cut), [window], 10**10
            )
        rim = (2, half, pattern)
        gradient, top, bottom, step_own, step_other = call(
            bind(field_kernel, size, minibatch),
            "field",
            [field, rim, rim, blocks, blocks],
            (here, *cut, own, other, observed, table),
            [] if last else [window],
            flops=2 * 12 * 512**3,
        )
        (illum,) = call(
            bind(illumination_kernel, size, minibatch),
            "illumination",
            [(strip, width)],
            (info, own, other),
            [tall],
        )
        brought = swap(step_other)
        steps = [step_own[k] + brought[k] for k in range(GROUP)]
        piece = scatter(steps, NEAR_STEP[minibatch])
        if last:
            top, bottom, piece = lax.optimization_barrier((top, bottom, piece))
        rim_below, rim_above = from_below(bottom), from_above(top)
        gradient, rim_below, rim_above, illum = lax.optimization_barrier(
            (gradient, rim_below, rim_above, illum)
        )
        rims = (gradient, swap(gradient), rim_below, rim_above, swap(rim_below), swap(rim_above))
        object_field, *edges = call(
            bind(update_kernel, size, minibatch),
            "update",
            [object_field.shape] + ([] if last else [rim] * 2),
            (info, object_field, illum, *rims),
            [tall],
        )
        piece = exchange(piece, FAR_STEPS[minibatch])
        if not last:
            edges = [from_below(edges[1]), from_above(edges[0])]
            piece, *edges = lax.optimization_barrier((piece, *edges))
        totals = gather(piece, NEAR_STEP[minibatch])
        if last:
            totals, object_field = lax.optimization_barrier((totals, object_field))
            others = swap(totals[:, 2 * rows :])
            (own,) = call(bind(probe_kernel, minibatch), "probe", [field], (here, totals, others, own))
        else:
            own, other = call(
                bind(probe_kernel, minibatch), "probe", [field] * 2, (here, totals, swap(totals), own, other)
            )
    return (object_field, own[None])


def solution(mesh):
    in_specs = (
        P(None, "tile", None),
        P("mode", None, None, None),
        P(None, "tile", None),
        P(None, "tile", None, None),
    )
    out_specs = (P(None, "tile", None), P("mode", None, None, None))

    def whole(object_field, probe, positions, measured):
        tiles, pair = mesh.shape["tile"], mesh.shape["mode"]
        by_position = (
            pair == 2
            and probe.shape[0] == 2
            and positions.shape[:2] == (2, 2 * tiles)
            and tiles == GROUP * GROUP
            and probe.shape[2] % (16 * 2 * GROUP) == 0
            and object_field.shape[1] == tiles * probe.shape[2]
        )
        shards = shards_by_position if by_position else shards_by_mode
        return jax.shard_map(
            shards, mesh=mesh, in_specs=in_specs, out_specs=out_specs, check_vma=False
        )(object_field, probe, positions, measured)

    return whole
```

```python
import functools
import math

import jax
import jax.numpy as jnp
import numpy as np
from jax import lax
from jax.experimental import pallas as pl
from jax.experimental.pallas import tpu as pltpu
from jax.sharding import PartitionSpec as P

F32 = jnp.float32
BF16 = jnp.bfloat16
VMEM_BYTES = 16 * 1024 * 1024
GROUP = 4
NEAR_STEP = 2
FAR_STEPS = (1, 8, 9)


def padded(block, sides, width):
    for axis, dim in sides:
        count = lax.axis_size(axis)
        forward = [(i, i + 1) for i in range(count - 1)]
        backward = [(target, source) for source, target in forward]
        low = lax.ppermute(
            lax.slice_in_dim(block, block.shape[dim] - width, None, axis=dim), axis, forward
        )
        high = lax.ppermute(lax.slice_in_dim(block, 0, width, axis=dim), axis, backward)
        block = jnp.concatenate([low, block, high], axis=dim)
    return block


def tables(length):
    index_values = jnp.arange(length, dtype=jnp.int32)
    product = index_values[:, None] * index_values[None, :] % length
    angles = product.astype(jnp.float32) * (2.0 * math.pi / length)
    scaling = 1.0 / math.sqrt(length)
    return (jnp.cos(angles) * scaling, jnp.sin(angles) * scaling)


def apply_left(matrix, target):
    return jnp.einsum("ab,pbc->pac", matrix, target, precision=lax.Precision.HIGHEST)


def apply_right(target, matrix):
    return jnp.einsum("pab,bc->pac", target, matrix, precision=lax.Precision.HIGHEST)


def transform(real_part, imag_part, cosine, sine_table, direction):
    left_real = apply_left(cosine, real_part) + direction * apply_left(sine_table, imag_part)
    left_imag = apply_left(cosine, imag_part) - direction * apply_left(sine_table, real_part)
    out_real = apply_right(left_real, cosine) + direction * apply_right(left_imag, sine_table)
    out_imag = apply_right(left_imag, cosine) - direction * apply_right(left_real, sine_table)
    return (out_real, out_imag)


def place_add(target, placed, row_start, col_start):
    zero_index = jnp.int32(0)
    current = lax.dynamic_slice(target, (zero_index, row_start, col_start), placed.shape)
    return lax.dynamic_update_slice(target, current + placed, (zero_index, row_start, col_start))


def shards_by_mode(object_field, probe, positions, measured):
    strip_rows = object_field.shape[1]
    object_width = object_field.shape[2]
    pattern = probe.shape[2]
    half_pattern = pattern // 2
    count = positions.shape[1]
    cosine, sine_table = tables(pattern)
    tile_index = lax.axis_index("tile")
    offset = tile_index * strip_rows - half_pattern
    for minibatch in range(measured.shape[0]):
        extended = padded(object_field, (("tile", 1),), half_pattern)
        row_offsets = positions[minibatch, :, 0] - offset
        column_offsets = positions[minibatch, :, 1]

        def cut_one(row_start, col_start):
            return lax.dynamic_slice(
                extended, (jnp.int32(0), row_start, col_start), (2, pattern, pattern)
            )

        patches = jax.vmap(cut_one)(row_offsets, column_offsets)
        obj_real = patches[:, 0]
        obj_imag = patches[:, 1]
        probe_real = probe[0, 0]
        probe_imag = probe[0, 1]
        exit_real = probe_real * obj_real - probe_imag * obj_imag
        exit_imag = probe_real * obj_imag + probe_imag * obj_real
        far_real, far_imag = transform(exit_real, exit_imag, cosine, sine_table, 1.0)
        observed = measured[minibatch]
        intensity = lax.psum(far_real * far_real + far_imag * far_imag, "mode")
        modulus = jnp.sqrt((observed + 1.0) / (intensity + 1.0)) - 1.0
        chi_real, chi_imag = transform(
            modulus * far_real, modulus * far_imag, cosine, sine_table, -1.0
        )
        grad_real = probe_real * chi_real + probe_imag * chi_imag
        grad_imag = probe_real * chi_imag - probe_imag * chi_real
        probe_power = probe_real * probe_real + probe_imag * probe_imag
        step_real = jnp.sum(obj_real * chi_real + obj_imag * chi_imag, axis=0)
        step_imag = jnp.sum(obj_real * chi_imag - obj_imag * chi_real, axis=0)
        coverage = jnp.sum(obj_real * obj_real + obj_imag * obj_imag, axis=0)
        accumulated = jnp.zeros((3, strip_rows + pattern, object_width), jnp.float32)
        for position in range(count):
            placed = jnp.stack([grad_real[position], grad_imag[position], probe_power])
            accumulated = place_add(
                accumulated, placed, row_offsets[position], column_offsets[position]
            )
        rim_rows = jnp.concatenate(
            [accumulated[:, :half_pattern], accumulated[:, strip_rows + half_pattern :]], axis=1
        )
        received = padded(rim_rows, (("tile", 1),), half_pattern)
        own_strip = accumulated[:, half_pattern : half_pattern + strip_rows]
        own_strip = own_strip.at[:, :half_pattern].add(received[:, :half_pattern])
        own_strip = own_strip.at[:, strip_rows - half_pattern :].add(
            received[:, pattern + half_pattern :]
        )
        summed = lax.psum(own_strip, "mode")
        divisor = summed[2] + 1.0
        object_field = jnp.stack(
            [object_field[0] + summed[0] / divisor, object_field[1] + summed[1] / divisor]
        )
        step_stack = jnp.stack([jnp.stack([step_real, step_imag])])
        step_total, coverage_total = lax.psum((step_stack, coverage), "tile")
        probe = probe + step_total / (coverage_total + 1.0)
    return (object_field, probe)


def table_of(length):
    index_values = np.arange(length)
    angles = (index_values[:, None] * index_values[None, :] % length) * (2.0 * np.pi / length)
    scaling = 1.0 / np.sqrt(length)
    return np.stack([np.cos(angles) * scaling, np.sin(angles) * scaling]).astype(np.float32)


def spot(info, size, minibatch, side, slot):
    tiles, strip, pattern = size
    place = (((side + 1) * 2 + minibatch) * 2 + slot) * 2
    tile = info[24]
    row = info[place] - tile * strip + pattern // 2
    if side < 0:
        row = jnp.where(tile == 0, -pattern, row)
    if side > 0:
        row = jnp.where(tile == tiles - 1, strip + pattern, row)
    return row, info[place + 1]


def take_columns(block, column, width):
    total = block.shape[-1]
    return pltpu.roll(block, lax.rem(total - column, total), 1)[:, :width]


def add_at(tall, block, row, column):
    rows, width = block.shape
    total = tall.shape[1]
    shift = lax.rem(row, 8)
    start = pl.multiple_of(row - shift, 8)
    turned = pltpu.roll(block.reshape(rows // 8, 8, width), shift, 1)
    empty = jnp.zeros((1, 8, width), block.dtype)
    inside = lax.broadcasted_iota(jnp.int32, (rows // 8 + 1, 8, width), 1) >= shift
    moved = jnp.where(
        inside,
        jnp.concatenate([turned, empty], axis=0),
        jnp.concatenate([empty, turned], axis=0),
    ).reshape(rows + 8, width)
    wide = jnp.concatenate([moved, jnp.zeros((rows + 8, total - width), block.dtype)], axis=1)
    tall[pl.ds(start, rows + 8), :] += pltpu.roll(wide, column, 1)


def rows_at(ref, row, rows):
    width = ref.shape[1]
    shift = lax.rem(row, 8)
    start = pl.multiple_of(row - shift, 8)
    block = ref[pl.ds(start, rows + 8), :].reshape(rows // 8 + 1, 8, width)
    turned = pltpu.roll(block, lax.rem(8 - shift, 8), 1)
    inside = lax.broadcasted_iota(jnp.int32, (rows // 8, 8, width), 1) < 8 - shift
    return jnp.where(inside, turned[:-1], turned[1:]).reshape(rows, width)


def halves(value):
    high = value.astype(BF16)
    return high, (value - high.astype(F32)).astype(BF16)


def product(left, right):
    dot = functools.partial(jnp.dot, preferred_element_type=F32)
    return dot(left[0], right[0]) + (dot(left[0], right[1]) + dot(left[1], right[0]))


def cut_patch(size, info, minibatch, strip_ref, below, above, window, part):
    tiles, rows, width = size
    half = width // 2
    row, column = spot(info, size, minibatch, 0, info[25])

    def columns(block):
        return block if block.shape[1] == width else take_columns(block, column, width)

    window[:half] = columns(below)
    window[half : half + rows] = columns(strip_ref[part])
    window[half + rows : rows + width] = columns(above)
    return rows_at(window, row, width)


def illumination_kernel(size, minibatch, info, own, other, out, tall):
    tiles, strip, pattern = size
    half = pattern // 2
    kept = slice(pattern + half, pattern + half + strip)
    tall[kept] = jnp.zeros((strip, tall.shape[1]), F32)
    (pr0, pi0), (pr1, pi1) = ((ref[0], ref[1]) for ref in (own, other))
    power = pr0 * pr0 + pi0 * pi0 + (pr1 * pr1 + pi1 * pi1)
    for side in (-1, 0, 1):
        for slot in range(2):
            row, column = spot(info, size, minibatch, side, slot)
            add_at(tall, power, row + pattern, column)
    out[...] = 1.0 / (tall[kept] + 1.0)


def patch_kernel(size, minibatch, info, strip_ref, below, above, patch, window):
    for part in range(2):
        patch[part] = cut_patch(
            size, info, minibatch, strip_ref, below[part], above[part], window, part
        )


def ready_kernel(info, probe, measured, table, own, observed, split):
    own[...] = probe[...]
    for minibatch in range(2):
        observed[minibatch] = measured[minibatch, info[25]]
    for i in range(2):
        split[2 * i], split[2 * i + 1] = halves(table[i])


def field_kernel(size, minibatch, info, strip_ref, *refs):
    tiles, strip, pattern = size
    slot = info[25]
    if minibatch:
        own, other, measured, table, gradient, top, bottom, step_own, step_other = refs
        obj_real, obj_imag = strip_ref[0], strip_ref[1]
    else:
        *edges, own, other, measured, table = refs[:-6]
        gradient, top, bottom, step_own, step_other, window = refs[-6:]
        sides = (jnp.where(slot == 0, edges[i][...], edges[i + 1][...]) for i in (0, 2))
        others = (jnp.where(slot == 0, edges[i + 1][...], edges[i][...]) for i in (0, 2))
        obj_real, obj_imag = (
            cut_patch(size, info, minibatch, strip_ref, *ends, window, part)
            for part, ends in enumerate((sides, others))
        )
    cos_high, cos_low, sin_high, sin_low = (table[i] for i in range(4))

    def block(top_left, top_right, low_left, low_right):
        return jnp.concatenate(
            [
                jnp.concatenate([top_left, top_right], axis=1),
                jnp.concatenate([low_left, low_right], axis=1),
            ],
            axis=0,
        )

    first = (
        block(cos_high, sin_high, -sin_high, cos_high),
        block(cos_low, sin_low, -sin_low, cos_low),
    )
    second = (
        block(cos_high, -sin_high, sin_high, cos_high),
        block(cos_low, -sin_low, sin_low, cos_low),
    )
    probes = [(ref[0], ref[1]) for ref in (own, other)]

    def both(fields, left, right):
        (r0, i0), (r1, i1) = fields
        y = product(left, halves(block(r0, r1, i0, i1)))
        y = block(
            y[:pattern, :pattern], y[pattern:, :pattern], y[:pattern, pattern:], y[pattern:, pattern:]
        )
        y = product(halves(y), right)
        return (
            (y[:pattern, :pattern], y[:pattern, pattern:]),
            (y[pattern:, :pattern], y[pattern:, pattern:]),
        )

    exits = [(pr * obj_real - pi * obj_imag, pr * obj_imag + pi * obj_real) for pr, pi in probes]
    far = both(exits, first, second)
    intensity = (far[0][0] * far[0][0] + far[0][1] * far[0][1]) + (
        far[1][0] * far[1][0] + far[1][1] * far[1][1]
    )
    factor = jnp.sqrt((measured[minibatch] + 1.0) / (intensity + 1.0)) - 1.0
    chi = both([(factor * fr, factor * fi) for fr, fi in far], second, first)
    (pr0, pi0), (pr1, pi1) = probes
    (cr0, ci0), (cr1, ci1) = chi
    half = top.shape[1]
    for part, value in (
        (0, (pr0 * cr0 + pi0 * ci0) + (pr1 * cr1 + pi1 * ci1)),
        (1, (pr0 * ci0 - pi0 * cr0) + (pr1 * ci1 - pi1 * cr1)),
    ):
        gradient[part], top[part], bottom[part] = value, value[:half], value[half:]
    coverage = obj_real * obj_real + obj_imag * obj_imag
    rows = pattern // GROUP
    mate = lax.rem(lax.div(info[24], NEAR_STEP), GROUP)
    for step, keeper, (cr, ci) in ((step_own, slot, chi[0]), (step_other, 1 - slot, chi[1])):
        real = obj_real * cr + obj_imag * ci
        imag = obj_real * ci - obj_imag * cr
        for k in range(GROUP):
            start = k * rows
            block = step.at[mate ^ k]
            block[:rows] = real[start : start + rows]
            block[rows : 2 * rows] = imag[start : start + rows]
            middle = start + rows // 2
            block[2 * rows :] = jnp.where(
                keeper == 0, coverage[start:middle], coverage[middle : start + rows]
            )


def update_kernel(size, minibatch, info, strip_ref, illum, own, other, b0, a0, b1, a1, *outs):
    strip_out, *edges, tall = outs
    tiles, strip, pattern = size
    half = pattern // 2
    slot = info[25]
    kept = slice(pattern + half, pattern + half + strip)
    grads = (
        (0, slot, own, 0),
        (0, 1 - slot, other, 0),
        (-1, slot, b0, half),
        (1, slot, a0, 0),
        (-1, 1 - slot, b1, half),
        (1, 1 - slot, a1, 0),
    )
    for part in range(2):
        tall[kept] = jnp.zeros((strip, tall.shape[1]), F32)
        for side, place, ref, start in grads:
            row, column = spot(info, size, minibatch, side, place)
            add_at(tall, ref[part], row + pattern + start, column)
        fresh = strip_ref[part] + tall[kept] * illum[...]
        strip_out[part] = fresh
        if edges:
            column_below = spot(info, size, minibatch + 1, -1, slot)[1]
            column_above = spot(info, size, minibatch + 1, 1, slot)[1]
            edges[0][part] = take_columns(fresh[:half], column_below, pattern)
            edges[1][part] = take_columns(fresh[strip - half :], column_above, pattern)


def probe_kernel(info, own_totals, other_totals, *refs):
    probes, outs = refs[: len(refs) // 2], refs[len(refs) // 2 :]
    slot = info[25]
    rows = outs[0].shape[1] // GROUP
    mate = lax.rem(lax.div(info[24], NEAR_STEP), GROUP)
    for k in range(GROUP):
        where = pl.ds(pl.multiple_of((mate ^ k) * rows, rows), rows)
        mine, theirs = own_totals[k], other_totals[k]
        own_half, other_half = mine[2 * rows :], theirs[theirs.shape[0] - rows // 2 :]
        coverage = jnp.concatenate(
            [
                jnp.where(slot == 0, own_half, other_half),
                jnp.where(slot == 0, other_half, own_half),
            ],
            axis=0,
        )
        divisor = coverage + 1.0
        for totals, probe, out in zip((mine, theirs), probes, outs):
            for part in range(2):
                change = totals[part * rows : (part + 1) * rows] / divisor
                out[part, where, :] = probe[part, where, :] + change


def call(kernel, name, outs, inputs, scratch=(), flops=0):
    shapes = [
        shape if isinstance(shape, jax.ShapeDtypeStruct) else jax.ShapeDtypeStruct(shape, F32)
        for shape in outs
    ]
    size = sum(value.size * value.dtype.itemsize for value in (*shapes, *inputs))
    smem = pl.BlockSpec(memory_space=pltpu.SMEM)
    vmem = pl.BlockSpec(memory_space=pltpu.VMEM)
    return pl.pallas_call(
        kernel,
        out_shape=shapes,
        in_specs=[smem] + [vmem] * (len(inputs) - 1),
        out_specs=[vmem] * len(shapes),
        scratch_shapes=[pltpu.VMEM(shape, F32) for shape in scratch],
        compiler_params=pltpu.CompilerParams(vmem_limit_bytes=VMEM_BYTES),
        cost_estimate=pl.CostEstimate(flops=flops, bytes_accessed=size, transcendentals=0),
        name=name,
    )(*inputs)


def shards_by_position(object_field, probe, positions, measured):
    strip = object_field.shape[1]
    width = object_field.shape[2]
    pattern = probe.shape[2]
    half = pattern // 2
    tiles = lax.axis_size("tile")
    size = (tiles, strip, pattern)
    field = (2, pattern, pattern)
    tall = (3 * pattern + strip + 8, width)
    window = (pattern + strip + 8, pattern)
    up = [(i, i + 1) for i in range(tiles - 1)]
    down = [(i + 1, i) for i in range(tiles - 1)]

    def swap(value):
        return lax.ppermute(value, "mode", [(0, 1), (1, 0)])

    def across(value, k):
        return lax.ppermute(value, "tile", [(i, i ^ k) for i in range(tiles)])

    def scatter(blocks, unit):
        mates = [across(blocks[k], unit * k) for k in range(1, GROUP)]
        return functools.reduce(jnp.add, mates, blocks[0])

    def exchange(piece):
        first, second, third = (across(piece, steps) for steps in FAR_STEPS)
        return (piece + first) + (second + third)

    def gather(piece, unit):
        return jnp.stack([piece] + [across(piece, unit * k) for k in range(1, GROUP)])

    def from_below(value):
        return lax.ppermute(value, "tile", up)

    def from_above(value):
        return lax.ppermute(value, "tile", down)

    def bind(kernel, *args):
        return functools.partial(kernel, *args)

    tile, slot = lax.axis_index("tile"), lax.axis_index("mode")
    index = jnp.stack([tile, slot]).astype(jnp.int32)
    here = jnp.concatenate([positions.ravel()] * 3 + [index])
    one_part = lax.dynamic_index_in_dim(object_field, slot, 0, keepdims=False)
    edges = [from_below(one_part[strip - half :]), from_above(one_part[:half])]
    below, above = from_below(positions), from_above(positions)
    other = swap(probe[0])
    own, observed, table = call(
        ready_kernel,
        "ready",
        [field, field, jax.ShapeDtypeStruct((4, pattern, pattern), BF16)],
        (here, probe[0], measured, jnp.asarray(table_of(pattern))),
    )
    *edges, below, above, own, observed, table = lax.optimization_barrier(
        (*edges, below, above, own, observed, table)
    )
    edges = [edges[0], swap(edges[0]), edges[1], swap(edges[1])]
    info = jnp.concatenate([below.ravel(), positions.ravel(), above.ravel(), index])

    for minibatch in range(2):
        last = minibatch == 1
        rows = pattern // GROUP
        blocks = (GROUP, 2 * rows + rows // 2, pattern)
        cut = (object_field, *edges)
        if last:
            cut = call(
                bind(patch_kernel, size, minibatch), "patch", [field], (here, *cut), [window], 10**10
            )
        rim = (2, half, pattern)
        gradient, top, bottom, step_own, step_other = call(
            bind(field_kernel, size, minibatch),
            "field",
            [field, rim, rim, blocks, blocks],
            (here, *cut, own, other, observed, table),
            [] if last else [window],
            flops=2 * 12 * 512**3,
        )
        (illum,) = call(
            bind(illumination_kernel, size, minibatch),
            "illumination",
            [(strip, width)],
            (info, own, other),
            [tall],
        )
        brought = swap(step_other)
        steps = [step_own[k] + brought[k] for k in range(GROUP)]
        piece = scatter(steps, NEAR_STEP)
        rim_below, rim_above = from_below(bottom), from_above(top)
        gradient, rim_below, rim_above, illum = lax.optimization_barrier(
            (gradient, rim_below, rim_above, illum)
        )
        rims = (gradient, swap(gradient), rim_below, rim_above, swap(rim_below), swap(rim_above))
        object_field, *edges = call(
            bind(update_kernel, size, minibatch),
            "update",
            [object_field.shape] + ([] if last else [rim] * 2),
            (info, object_field, illum, *rims),
            [tall],
        )
        piece = exchange(piece)
        if not last:
            edges = [from_below(edges[1]), from_above(edges[0])]
            piece, *edges = lax.optimization_barrier((piece, *edges))
        totals = gather(piece, NEAR_STEP)
        if last:
            totals, object_field = lax.optimization_barrier((totals, object_field))
            others = swap(totals[:, 2 * rows :])
            (own,) = call(probe_kernel, "probe", [field], (here, totals, others, own))
        else:
            own, other = call(
                probe_kernel, "probe", [field] * 2, (here, totals, swap(totals), own, other)
            )
    return (object_field, own[None])


def solution(mesh):
    in_specs = (
        P(None, "tile", None),
        P("mode", None, None, None),
        P(None, "tile", None),
        P(None, "tile", None, None),
    )
    out_specs = (P(None, "tile", None), P("mode", None, None, None))

    def whole(object_field, probe, positions, measured):
        tiles, pair = mesh.shape["tile"], mesh.shape["mode"]
        by_position = (
            pair == 2
            and probe.shape[0] == 2
            and positions.shape[:2] == (2, 2 * tiles)
            and tiles == GROUP * GROUP
            and probe.shape[2] % (16 * 2 * GROUP) == 0
            and object_field.shape[1] == tiles * probe.shape[2]
        )
        shards = shards_by_position if by_position else shards_by_mode
        return jax.shard_map(
            shards, mesh=mesh, in_specs=in_specs, out_specs=out_specs, check_vma=False
        )(object_field, probe, positions, measured)

    return whole
```
